256 devices in a mesh: blk: 128 (over z, y, x_hi, core), map: 2 (over x_lo).
Axes of the slice: x: 4 (x_hi: 2, x_lo: 2; x = x_hi * 2 + x_lo), y: 4, z: 8, core: 2. Of those that a mesh axis runs over, the one named last changes fastest.
Arguments:
- phase_history: bfloat16 [128, 2, 128, 1024], P('blk', 'map'), may hold values from -6 to 6
- tile_curvature: float32 [128], P('blk'), may hold values from 20 to 80
- interp_weights: bfloat16 [128, 512, 512], P('blk'), may hold values from -0.25 to 0.25
- strip_tiles: int32 [128, 2, 256, 1], P('blk', 'map'), may hold values from 0 to 127; in each aligned block of 256 rows (0 to 255, 256 to 511, ..., all dimensions but the last counted through in order) at most 4 rows name the same one
- row_offsets: int32 [128, 2, 256], P('blk', 'map'), may hold values from 0 to 255
- tile_owner: int32 [128], replicated, may hold values from 0 to 127, each once
Outputs:
- map_power: float32 [128, 2, 256, 512], P('blk', 'map')
The draws below stay inside these ranges and needn't reach their ends.
Inputs may be any that keep to these rules, and one draw needn't show every extreme that they name: `strip_tiles`: among the rows of one device no map tile is named more than 4 times, and in every draw some device names some tile exactly 4 times. `tile_owner`: every blk index holds exactly one map tile.
All inputs are finite; a program needn't handle non-finite values.
Results may differ from the reference program's by a relative error of at most 0.0055.
Values may be sent and summed in bfloat16 or wider, within the bound.
No kernel may reach another device: no remote copies, remote signals or barrier semaphores. Data moves between devices by JAX's collectives and lax.ppermute only.
A program may use at most 64 MiB of HBM per device.

```python
import math
import jax
import jax.numpy as jnp
import numpy as np
from jax import lax

NB = 128
NF = 512
TR = 512
TC = 512
STOPS = 8
MAPH = 256
ROWS_DEV = 256
CAP = 4
N_BLK = 128
N_MAP = 2


def place_ends(result, own_key, low, largest):
    longest = result.shape.index(max(result.shape))
    spots = []
    for shift in (0, 1):
        where = [jax.random.randint(jax.random.fold_in(own_key, axis), (), 0, length) for axis, length in enumerate(result.shape)]
        where[longest] = (where[longest] + shift) % result.shape[longest]
        spots.append(tuple(where))
    return result.at[spots[0]].set(low).at[spots[1]].set(largest)


def levels(stream_key, shape, split, least, high):
    level = 1.0
    for dim, shards_of in split:
        draws = jax.random.uniform(jax.random.fold_in(jax.random.fold_in(stream_key, 6), dim), (shards_of,), jnp.float32, least / len(split), high / len(split))
        level = level * jnp.repeat(jnp.exp(draws), shape[dim] // shards_of).reshape((-1,) + (1,) * (len(shape) - 1 - dim))
    return level


def assign_block(key, own, number, rows, count, top, limit, slope):
    ranking = jax.random.permutation(key, count)
    crowded, common = load_shares(count, rows * top, limit, slope, True), load_shares(count, rows * top, limit, slope, False)
    places = jnp.arange(count)

    def named(sizes, rotation):
        used = int((sizes > 0).sum())
        fixed = max(1, used // 4)
        passed = fixed + (places - fixed + rotation * (used - fixed)) % max(1, count - fixed)
        return jnp.zeros((count,), jnp.int32).at[ranking[jnp.where(places < fixed, places, passed)]].set(jnp.asarray(sizes, jnp.int32))

    sizes = jnp.where(number % 4 == 0, named(crowded, number // 4), named(common, number - number // 4 - 1))
    mixed = jax.random.permutation(jax.random.fold_in(own, 3), count)
    donor, taker = mixed[0:count // 2 * 2:2], mixed[1:count // 2 * 2:2]
    room = jnp.minimum(sizes[donor] - 1, limit - sizes[taker]) // 2
    room = jnp.where((donor == ranking[0]) | (taker == ranking[0]) | (sizes[taker] == 0), 0, jnp.maximum(room, 0))
    passed = jax.random.randint(jax.random.fold_in(own, 4), (count // 2,), 0, 1 << 20) % (room + 1)
    sizes = sizes.at[donor].add(-passed).at[taker].add(passed)
    members = jnp.searchsorted(jnp.cumsum(sizes), jnp.arange(rows * top), side="right").astype(jnp.int32)
    grid = members.reshape(top, rows).T
    grid = grid[jax.random.permutation(jax.random.fold_in(own, 1), rows)]
    rotation = jax.random.randint(jax.random.fold_in(own, 2), (rows, 1), 0, top)
    return jnp.take_along_axis(grid, (jnp.arange(top)[None, :] + rotation) % top, axis=1)


def load_shares(count, total, most, skew, full):
    weights = [(1 << 20) // math.isqrt(rank ** skew) + 1 for rank in range(1, count + 1)]
    largest = most if full else min(most, max(-(-total // count), total * weights[0] // sum(weights)))
    least = 1 if total - largest >= count - 1 else 0
    given, surplus = [largest] + [least] * (count - 1), total - largest - least * (count - 1)
    while surplus > 0:
        free = [i for i in range(1, count) if given[i] < largest] or [i for i in range(1, count) if given[i] < most]
        mass, left = sum([weights[i] for i in free]), surplus
        for i in free:
            addition = min(most - given[i], max(1, left * weights[i] // mass), surplus)
            given[i] = given[i] + addition
            surplus = surplus - addition
    return np.array(given)


def normal_values(own_key, shape, width, most, cuts=(), kind=jnp.bfloat16):
    drawn = width * jax.random.normal(own_key, shape, jnp.float32)
    if cuts:
        drawn = drawn * levels(own_key, shape, cuts, -0.22, 0.18)
    return jnp.clip(drawn, -most, most).astype(kind)


def setup_inputs(seed: int = 0) -> dict:
    key_of = jax.random.split(jax.random.key(seed), 7)
    phase_history = normal_values(key_of[0], (N_BLK, N_MAP, NB, 2 * NF), 1.0, 6.0, ((0, 128), (1, 2)))
    tile_curvature = jnp.clip(20.0 + 60.0 * jax.random.uniform(key_of[1], (N_BLK,), jnp.float32) ** levels(key_of[1], (N_BLK,), ((0, 128),), -0.2, 0.2), 20.0, 80.0)
    interp_weights = normal_values(key_of[2], (N_BLK, TC, TC), TC ** -0.5, 0.25, ((0, 128),))
    strip_tiles_keys = jax.random.split(jax.random.fold_in(key_of[3], 1), N_BLK * N_MAP * ROWS_DEV // ROWS_DEV)
    strip_tiles_turns = jax.random.permutation(jax.random.fold_in(key_of[3], 3), N_BLK * N_MAP * ROWS_DEV // ROWS_DEV)
    strip_tiles = jax.vmap(lambda own, number: assign_block(jax.random.fold_in(key_of[3], 2), own, number, ROWS_DEV, N_BLK, 1, CAP, 2))(strip_tiles_keys, strip_tiles_turns).reshape((N_BLK, N_MAP, ROWS_DEV, 1))
    row_offsets = place_ends(jax.random.randint(key_of[4], (N_BLK, N_MAP, ROWS_DEV), 0, MAPH), jax.random.fold_in(key_of[4], 1), 0, MAPH - 1).astype(jnp.int32)
    tile_owner = jax.random.permutation(key_of[5], N_BLK).astype(jnp.int32)
    return {"phase_history": phase_history, "tile_curvature": tile_curvature, "interp_weights": interp_weights, "strip_tiles": strip_tiles, "row_offsets": row_offsets, "tile_owner": tile_owner}


def range_matrix(freq_count, column_count):
    freq_index = jnp.arange(freq_count, dtype=jnp.int32)[:, None]
    column_index = jnp.arange(column_count, dtype=jnp.int32)[None, :]
    angle = (freq_index * column_index % freq_count).astype(jnp.float32) * (2.0 * math.pi / freq_count)
    factor = 1.0 / math.sqrt(freq_count)
    real_part = jnp.cos(angle) * factor
    imag_part = -jnp.sin(angle) * factor
    upper = jnp.concatenate([real_part, imag_part], axis=1)
    lower = jnp.concatenate([-imag_part, real_part], axis=1)
    return jnp.concatenate([upper, lower], axis=0).astype(jnp.bfloat16)

def cross_rows(stop_index, map_index, row_index, map_count, pulse_count, span):
    pulse_index = jnp.arange(pulse_count, dtype=jnp.int32)[None, :]
    along = (stop_index * map_count + map_index) * pulse_count + pulse_index
    angle = (row_index[:, None] * along % span).astype(jnp.float32) * (2.0 * math.pi / span)
    factor = 1.0 / math.sqrt(span)
    return jnp.concatenate([jnp.cos(angle) * factor, -jnp.sin(angle) * factor], axis=1).astype(jnp.bfloat16)

def apply_phase(source_block, curvature, stop_index, map_index, map_count, pulse_count, freq_count, span):
    pulse_index = jnp.arange(pulse_count, dtype=jnp.int32)
    along = ((stop_index * map_count + map_index) * pulse_count + pulse_index).astype(jnp.float32) / span - 0.5
    relative = jnp.arange(freq_count, dtype=jnp.int32).astype(jnp.float32) / freq_count - 0.5
    phase_angle = curvature * (along * along)[:, None] * (1.0 + relative[None, :])
    cosine = jnp.cos(phase_angle)
    sine = jnp.sin(phase_angle)
    values = source_block.astype(jnp.float32)
    real_part = values[:, :freq_count]
    imag_part = values[:, freq_count:]
    return jnp.concatenate([real_part * cosine - imag_part * sine, real_part * sine + imag_part * cosine], axis=1).astype(jnp.bfloat16)

def stack_spectrum(spectrum_now):
    half_width = spectrum_now.shape[1] // 2
    real_part = spectrum_now[:, :half_width]
    imag_part = spectrum_now[:, half_width:]
    upper = jnp.concatenate([real_part, imag_part], axis=1)
    lower = jnp.concatenate([-imag_part, real_part], axis=1)
    return jnp.concatenate([upper, lower], axis=0)

def tile_image(tile_index, phase_history, curvature):
    lead_count = STOPS // 2 - 1
    span = STOPS * N_MAP * NB
    ranges = range_matrix(NF, TC).astype(jnp.float32)
    row_index = jnp.arange(TR, dtype=jnp.int32)
    running = jnp.zeros((TR, 2 * TC), jnp.float32)
    for stop_index in range(STOPS):
        source = ((tile_index + stop_index - lead_count) % N_BLK).astype(jnp.int32)
        column_blocks = lax.dynamic_index_in_dim(phase_history, source, 0, keepdims=False)
        for map_index in range(N_MAP):
            phased = apply_phase(column_blocks[map_index], curvature, stop_index, map_index, N_MAP, NB, NF, span)
            spectrum_now = jnp.dot(phased.astype(jnp.float32), ranges, precision=lax.Precision.HIGHEST).astype(jnp.bfloat16)
            crossing = cross_rows(stop_index, map_index, row_index, N_MAP, NB, span).astype(jnp.float32)
            running = running + jnp.dot(crossing, stack_spectrum(spectrum_now).astype(jnp.float32), precision=lax.Precision.HIGHEST)
    return running.astype(jnp.bfloat16)

def reference(phase_history, tile_curvature, interp_weights, strip_tiles, row_offsets, tile_owner):

    def one_tile(tile_index):
        return tile_image(tile_index, phase_history, tile_curvature[tile_index])
    images = lax.map(one_tile, jnp.arange(N_BLK, dtype=jnp.int32))
    strip_rows = images.reshape(N_BLK, N_MAP, ROWS_DEV, 2 * TC)
    destination = tile_owner[strip_tiles[..., 0]].astype(jnp.int32)
    slot_count = N_BLK * CAP
    results = []
    for map_index in range(N_MAP):
        flat_rows = strip_rows[:, map_index].reshape(N_BLK * ROWS_DEV, 2 * TC)
        flat_dest = destination[:, map_index].reshape(N_BLK * ROWS_DEV)
        flat_offsets = row_offsets[:, map_index].reshape(N_BLK * ROWS_DEV).astype(jnp.int32)
        sorted_rows = jnp.argsort(flat_dest, stable=True).astype(jnp.int32)
        holder_counts = lax.optimization_barrier(jnp.sum((flat_dest[:, None] == jnp.arange(N_BLK, dtype=jnp.int32)[None, :]).astype(jnp.int32), axis=0)).astype(jnp.int32)
        holder_starts = (jnp.cumsum(holder_counts) - holder_counts).astype(jnp.int32)
        padded_rows = jnp.concatenate([sorted_rows, jnp.zeros((slot_count,), jnp.int32)])

        def one_holder(holder):
            picked = lax.dynamic_slice_in_dim(padded_rows, holder_starts[holder], slot_count)
            usable = jnp.arange(slot_count, dtype=jnp.int32) < holder_counts[holder]
            chosen = flat_rows[picked].astype(jnp.float32)
            weights = interp_weights[holder].astype(jnp.float32)
            real_out = jnp.dot(chosen[:, :TC], weights, precision=lax.Precision.HIGHEST)
            imag_out = jnp.dot(chosen[:, TC:], weights, precision=lax.Precision.HIGHEST)
            power_rows = real_out * real_out + imag_out * imag_out
            target = jnp.where(usable, flat_offsets[picked], MAPH).astype(jnp.int32)
            return jnp.zeros((MAPH, TC), jnp.float32).at[target].add(power_rows, mode='drop')
        results.append(lax.map(one_holder, jnp.arange(N_BLK, dtype=jnp.int32)))
    return jnp.stack(results, axis=1)
```

```python
import math

import jax
import jax.numpy as jnp
import ml_dtypes
import numpy as np
from jax import lax
from jax.sharding import PartitionSpec as P

STOPS = 8
MAPH = 256
SIDE = 128


def matching(count, distance, parity):
    seen, pairs = set(), []
    for start in range(count):
        cycle, at = [], start
        while at not in seen:
            seen.add(at)
            cycle.append(at)
            at = (at + distance) % count
        for place in range(parity, len(cycle) + parity, 2) if cycle else ():
            a, b = cycle[place % len(cycle)], cycle[(place + 1) % len(cycle)]
            pairs += [(a, b), (b, a)]
    return pairs


def range_table(freq_count):
    index = np.arange(freq_count, dtype=np.int64)
    angle = (index[:, None] * index[None, :] % freq_count).astype(np.float32) * np.float32(
        2.0 * math.pi / freq_count
    )
    factor = np.float32(1.0 / math.sqrt(freq_count))
    real_part, imag_part = np.cos(angle) * factor, -np.sin(angle) * factor
    table = np.block([[real_part, imag_part], [-imag_part, real_part]])
    return table.astype(ml_dtypes.bfloat16)


def cross_table(map_count, row_count, pulse_count):
    span = STOPS * map_count * pulse_count
    rows = np.arange(row_count, dtype=np.int64)[:, None]
    factor = np.float32(1.0 / math.sqrt(span))
    tables = []
    for m in range(map_count):
        along = np.concatenate(
            [(k * map_count + m) * pulse_count + np.arange(pulse_count) for k in range(STOPS)]
        )
        angle = (rows * along[None, :] % span).astype(np.float32) * np.float32(
            2.0 * math.pi / span
        )
        real_part, imag_part = np.cos(angle) * factor, -np.sin(angle) * factor
        tables.append(np.stack([real_part, imag_part]))
    return np.stack(tables).astype(ml_dtypes.bfloat16)


def apply_phase(block, curvature, stop_index, map_index, map_count, pulse_count, freq_count):
    span = STOPS * map_count * pulse_count
    pulse_index = jnp.arange(pulse_count, dtype=jnp.int32)
    along = ((stop_index * map_count + map_index) * pulse_count + pulse_index).astype(
        jnp.float32
    ) / span - 0.5
    relative = jnp.arange(freq_count, dtype=jnp.int32).astype(jnp.float32) / freq_count - 0.5
    phase_angle = curvature * (along * along)[:, None] * (1.0 + relative[None, :])
    cosine = jnp.cos(phase_angle)
    sine = jnp.sin(phase_angle)
    values = block.astype(jnp.float32)
    real_part = values[:, :freq_count]
    imag_part = values[:, freq_count:]
    return jnp.concatenate(
        [real_part * cosine - imag_part * sine, real_part * sine + imag_part * cosine], axis=1
    ).astype(jnp.bfloat16)


def gather_aperture(own_block, blk_count, here):
    core, chip_odd, group_odd = here % 2, (here // 2) % 2, (here // 4) % 2
    sibling = [(i, i ^ 1) for i in range(blk_count)]

    def swap(block):
        return lax.ppermute(block, "blk", sibling)

    near = [lax.ppermute(own_block, "blk", matching(blk_count, 2, p)) for p in (0, 1)]
    far = [lax.ppermute(own_block, "blk", matching(blk_count, 4, p)) for p in (0, 1)]
    twin = swap(own_block)
    twin_near = [swap(block) for block in near]
    far_up = jnp.where(group_odd == 0, far[0], far[1])
    twin_far = swap(jnp.where(core == group_odd, far[0], far[1]))
    up, down = (jnp.where(chip_odd == p, near[0], near[1]) for p in (0, 1))
    twin_up, twin_down = (jnp.where(chip_odd == p, twin_near[0], twin_near[1]) for p in (0, 1))
    return [
        jnp.where(core == 0, twin_far, twin_down),
        down,
        jnp.where(core == 0, twin_down, twin),
        own_block,
        jnp.where(core == 0, twin, twin_up),
        up,
        jnp.where(core == 0, twin_up, twin_far),
        far_up,
    ]


def body(ranges, crosses, phase_history, tile_curvature, interp_weights, strip_tiles, row_offsets, tile_owner):
    blk_count = lax.axis_size("blk")
    map_count = lax.axis_size("map")
    here_blk = lax.axis_index("blk")
    here_map = lax.axis_index("map")
    own_block = phase_history[0, 0]
    pulse_count = own_block.shape[0]
    freq_count = own_block.shape[1] // 2
    columns = interp_weights.shape[2]
    rows_here = strip_tiles.shape[2]

    blocks = gather_aperture(own_block, blk_count, here_blk)
    phased = [
        apply_phase(b, tile_curvature[0], k, here_map, map_count, pulse_count, freq_count)
        for k, b in enumerate(blocks)
    ]
    spectrum = jnp.concatenate(
        [
            jnp.dot(p, ranges, preferred_element_type=jnp.float32).astype(jnp.bfloat16)
            for p in phased
        ],
        axis=0,
    )
    rotated = jnp.concatenate([-spectrum[:, columns:], spectrum[:, :columns]], axis=1)
    cross = lax.dynamic_index_in_dim(crosses, here_map, 0, keepdims=False)

    def contribution(map_index):
        part = lax.dynamic_slice_in_dim(cross, map_index * rows_here, rows_here, 1)
        return jnp.dot(part[0], spectrum, preferred_element_type=jnp.float32) + jnp.dot(
            part[1], rotated, preferred_element_type=jnp.float32
        )

    sent = contribution(1 - here_map).astype(jnp.bfloat16)
    arrived = lax.ppermute(sent, "map", [(0, 1), (1, 0)])
    image_rows = (contribution(here_map) + arrived.astype(jnp.float32)).astype(jnp.bfloat16)

    capacity = max(2, 2 * rows_here // blk_count)
    holder_index = jnp.arange(blk_count, dtype=jnp.int32)
    row_tiles = strip_tiles[0, 0, :, 0]
    own_offsets = row_offsets[0, 0]
    tile_match = row_tiles[:, None] == holder_index[None, :]
    destination = jnp.sum(jnp.where(tile_match, tile_owner[None, :], 0), axis=1)
    row_number = jnp.arange(rows_here, dtype=jnp.int32)
    same_before = (row_tiles[:, None] == row_tiles[None, :]) & (
        row_number[None, :] < row_number[:, None]
    )
    rank_within = jnp.sum(same_before.astype(jnp.int32), axis=1)
    slot_index = destination * capacity + rank_within
    slot_hot = (
        jnp.arange(blk_count * capacity, dtype=jnp.int32)[:, None] == slot_index[None, :]
    ).astype(jnp.bfloat16)
    side = jnp.broadcast_to(own_offsets.astype(jnp.bfloat16)[:, None], (rows_here, SIDE))
    packed = jnp.dot(
        slot_hot, jnp.concatenate([image_rows, side], axis=1), preferred_element_type=jnp.float32
    ).astype(jnp.bfloat16)
    packed = packed.reshape(blk_count, capacity, 2 * columns + SIDE)
    got = lax.all_to_all(packed, "blk", split_axis=0, concat_axis=0, tiled=True)
    got = got.reshape(blk_count * capacity, 2 * columns + SIDE)

    weights = interp_weights[0]
    real_out = jnp.dot(got[:, :columns], weights, preferred_element_type=jnp.float32)
    imag_out = jnp.dot(got[:, columns : 2 * columns], weights, preferred_element_type=jnp.float32)
    power = real_out * real_out + imag_out * imag_out
    offsets = got[:, 2 * columns].astype(jnp.int32)
    place_hot = (jnp.arange(MAPH, dtype=jnp.int32)[:, None] == offsets[None, :]).astype(
        jnp.bfloat16
    )
    high = power.astype(jnp.bfloat16)
    rest = power - high.astype(jnp.float32)
    middle = rest.astype(jnp.bfloat16)
    low = (rest - middle.astype(jnp.float32)).astype(jnp.bfloat16)
    tile_map = sum(
        jnp.dot(place_hot, piece, preferred_element_type=jnp.float32)
        for piece in (low, middle, high)
    )
    return tile_map.reshape(1, 1, MAPH, columns)


def solution(mesh):
    in_specs = (
        P("blk", "map", None, None),
        P("blk"),
        P("blk", None, None),
        P("blk", "map", None, None),
        P("blk", "map", None),
        P(),
    )
    out_specs = P("blk", "map", None, None)

    def run(*args):
        map_count, pulse_count, width = args[0].shape[1:]
        ranges = jnp.asarray(range_table(width // 2))
        crosses = jnp.asarray(
            cross_table(map_count, map_count * args[3].shape[2], pulse_count)
        )
        held = lambda *here: body(ranges, crosses, *here)
        return jax.shard_map(
            held, mesh=mesh, in_specs=in_specs, out_specs=out_specs, check_vma=False
        )(*args)

    return run
```

```python
import functools
import math

import jax
import jax.numpy as jnp
import ml_dtypes
import numpy as np
from jax import lax
from jax.experimental import pallas as pl
from jax.experimental.pallas import tpu as pltpu
from jax.sharding import PartitionSpec as P

STOPS = 8
MAPH = 256
SIDE = 128


def matching(count, distance, parity):
    seen, pairs = set(), []
    for start in range(count):
        cycle, at = [], start
        while at not in seen:
            seen.add(at)
            cycle.append(at)
            at = (at + distance) % count
        for place in range(parity, len(cycle) + parity, 2) if cycle else ():
            a, b = cycle[place % len(cycle)], cycle[(place + 1) % len(cycle)]
            pairs += [(a, b), (b, a)]
    return pairs


def range_table(freq_count):
    index = np.arange(freq_count, dtype=np.int64)
    angle = (index[:, None] * index[None, :] % freq_count).astype(np.float32) * np.float32(
        2.0 * math.pi / freq_count
    )
    factor = np.float32(1.0 / math.sqrt(freq_count))
    real_part, imag_part = np.cos(angle) * factor, -np.sin(angle) * factor
    table = np.block([[real_part, imag_part], [-imag_part, real_part]])
    return table.astype(ml_dtypes.bfloat16)


def stop_order(core):
    return [1, 2, 3, 4, 5, 6 - 6 * core, 6 * core, 7]


def cross_table(map_count, row_count, pulse_count):
    span = STOPS * map_count * pulse_count
    rows = np.arange(row_count, dtype=np.int64)[:, None]
    factor = np.float32(1.0 / math.sqrt(span))
    tables = []
    for m in range(map_count):
        for core in range(2):
            parts = []
            for k in stop_order(core):
                along = (k * map_count + m) * pulse_count + np.arange(pulse_count)
                angle = (rows * along[None, :] % span).astype(np.float32) * np.float32(
                    2.0 * math.pi / span
                )
                parts += [np.cos(angle) * factor, -np.sin(angle) * factor]
            tables.append(np.concatenate(parts, axis=1))
    return np.stack(tables).astype(ml_dtypes.bfloat16)


def call(kernel, outs, operands, scratch=(), flops=0, limit=24):
    specs = [pl.BlockSpec(memory_space=pltpu.SMEM)] + [
        pl.BlockSpec(memory_space=pltpu.VMEM) for _ in operands[1:]
    ]
    size = sum(math.prod(a.shape) * a.dtype.itemsize for a in [*operands, *outs])
    return pl.pallas_call(
        kernel,
        out_shape=outs,
        in_specs=specs,
        out_specs=[pl.BlockSpec(memory_space=pltpu.VMEM) for _ in outs],
        scratch_shapes=list(scratch),
        compiler_params=pltpu.CompilerParams(vmem_limit_bytes=limit * 2**20),
        cost_estimate=pl.CostEstimate(flops=flops, bytes_accessed=size, transcendentals=0),
    )(*operands)


def phase_kernel(map_count, span, facts, curvature, cos_early, sin_early, cos_late, sin_late):
    early, pulses, freqs = cos_early.shape
    width = freqs // 4
    pulse = lax.broadcasted_iota(jnp.int32, (pulses, width), 0)
    fine = lax.broadcasted_iota(jnp.int32, (pulses, width), 1).astype(jnp.float32) / freqs
    core, here_map = facts[0], facts[3]
    for place in range(STOPS):
        stop = {5: 6 - 6 * core, 6: 6 * core}.get(place, place if place == 7 else place + 1)
        along = ((stop * map_count + here_map) * pulses + pulse).astype(jnp.float32) / span - 0.5
        angle = curvature[0] * (along * along)
        low_c, low_s = jnp.cos(angle * fine), jnp.sin(angle * fine)
        step_c, step_s = jnp.cos(angle * 0.25), jnp.sin(angle * 0.25)
        now_c = step_c * low_c - step_s * low_s
        now_s = step_s * low_c + step_c * low_s
        for h in range(4):
            now_c, now_s = step_c * now_c - step_s * now_s, step_s * now_c + step_c * now_s
            columns = slice(h * width, (h + 1) * width)
            if place < early:
                cos_early[place, :, columns] = now_c
                sin_early[place, :, columns] = now_s
            else:
                cos_late[place - early, :, columns] = now_c
                sin_late[place - early, :, columns] = now_s


def transform(blocks, cosines, sines, ranges, phased, right_side):
    freqs = cosines.shape[2]
    pulses = cosines.shape[1]
    for place, block in enumerate(blocks):
        values = block().astype(jnp.float32)
        real_part, imag_part = values[:, :freqs], values[:, freqs:]
        cosine, sine = cosines[place], sines[place]
        rows = slice(place * pulses, (place + 1) * pulses)
        phased[rows, :freqs] = (real_part * cosine - imag_part * sine).astype(jnp.bfloat16)
        phased[rows, freqs:] = (real_part * sine + imag_part * cosine).astype(jnp.bfloat16)
    for half in range(2):
        columns = slice(half * freqs, (half + 1) * freqs)
        spectrum = jnp.dot(
            phased[...], ranges[:, columns], preferred_element_type=jnp.float32
        ).astype(jnp.bfloat16)
        for place in range(len(blocks)):
            piece = spectrum[place * pulses : (place + 1) * pulses]
            top = 2 * place * pulses
            right_side[top : top + pulses, columns] = piece
            other = slice((1 - half) * freqs, (2 - half) * freqs)
            right_side[top + pulses : top + 2 * pulses, other] = piece if half == 0 else -piece


def early_kernel(
    facts, own, near_a, near_b, twin, twin_a, twin_b, cosines, sines, ranges, cross, total,
    phased, right_side,
):
    core, chip_odd = facts[0] == 1, facts[1] == 1
    up = lambda: jnp.where(chip_odd, near_b[...], near_a[...])
    down = lambda: jnp.where(chip_odd, near_a[...], near_b[...])
    twin_up = lambda: jnp.where(chip_odd, twin_b[...], twin_a[...])
    twin_down = lambda: jnp.where(chip_odd, twin_a[...], twin_b[...])
    blocks = [
        down,
        lambda: jnp.where(core, twin[...], twin_down()),
        lambda: own[...],
        lambda: jnp.where(core, twin_up(), twin[...]),
        up,
        lambda: jnp.where(core, twin_down(), twin_up()),
    ]
    transform(blocks, cosines, sines, ranges, phased, right_side)
    total[...] = jnp.dot(cross[...], right_side[...], preferred_element_type=jnp.float32)


def late_kernel(
    facts, far_a, far_b, twin_far, cosines, sines, ranges, cross, total, sent, kept,
    phased, right_side,
):
    group_odd, here_map = facts[2] == 1, facts[3]
    blocks = [lambda: twin_far[...], lambda: jnp.where(group_odd, far_b[...], far_a[...])]
    transform(blocks, cosines, sines, ranges, phased, right_side)
    rows = sent.shape[0]
    for out, part in ((sent, 1 - here_map), (kept, here_map)):
        place = pl.ds(pl.multiple_of(part * rows, rows), rows)
        out[...] = (
            total[place, :]
            + jnp.dot(cross[place, :], right_side[...], preferred_element_type=jnp.float32)
        ).astype(out.dtype)


def pack_kernel(facts, kept, arrived, slot_hot, side, packed):
    width = kept.shape[1]
    image = (kept[...] + arrived[...].astype(jnp.float32)).astype(jnp.bfloat16)
    packed[:, :width] = jnp.dot(
        slot_hot[...], image, preferred_element_type=jnp.float32
    ).astype(packed.dtype)
    packed[:, width:] = jnp.dot(
        slot_hot[...], side[...], preferred_element_type=jnp.float32
    ).astype(packed.dtype)


def swap(block, count):
    return lax.ppermute(block, "blk", [(i, i ^ 1) for i in range(count)])


def body(ranges, crosses, phase_history, tile_curvature, interp_weights, strip_tiles, row_offsets, tile_owner):
    blk_count = lax.axis_size("blk")
    map_count = lax.axis_size("map")
    here_blk = lax.axis_index("blk")
    here_map = lax.axis_index("map")
    own_block = phase_history[0, 0]
    pulse_count = own_block.shape[0]
    freq_count = own_block.shape[1] // 2
    columns = interp_weights.shape[2]
    rows_here = strip_tiles.shape[2]

    core, chip_odd, group_odd = here_blk % 2, (here_blk // 2) % 2, (here_blk // 4) % 2
    facts = jnp.stack([core, chip_odd, group_odd, here_map]).astype(jnp.int32)

    near = [lax.ppermute(own_block, "blk", matching(blk_count, 2, p)) for p in (0, 1)]
    far = [lax.ppermute(own_block, "blk", matching(blk_count, 4, p)) for p in (0, 1)]
    twin = swap(own_block, blk_count)
    twin_near = [swap(block, blk_count) for block in near]
    twin_far = swap(jnp.where(core == group_odd, far[0], far[1]), blk_count)

    cross = lax.dynamic_index_in_dim(crosses, here_map * 2 + core, 0, keepdims=False)
    early, late = STOPS - 2, 2
    deep = 2 * pulse_count
    f32 = lambda *shape: jax.ShapeDtypeStruct(shape, jnp.float32)
    b16 = lambda *shape: jax.ShapeDtypeStruct(shape, jnp.bfloat16)
    curves = pl.pallas_call(
        functools.partial(phase_kernel, map_count, STOPS * map_count * pulse_count),
        out_shape=[f32(n, pulse_count, freq_count) for n in (early, early, late, late)],
        in_specs=[pl.BlockSpec(memory_space=pltpu.SMEM)] * 2,
        out_specs=[pl.BlockSpec(memory_space=pltpu.VMEM)] * 4,
        compiler_params=pltpu.CompilerParams(vmem_limit_bytes=16 * 2**20),
        cost_estimate=pl.CostEstimate(flops=2**22, bytes_accessed=2**22, transcendentals=2**19),
    )(facts, tile_curvature)
    work = lambda n: [
        pltpu.VMEM((n * pulse_count, 2 * freq_count), jnp.bfloat16),
        pltpu.VMEM((n * deep, 2 * columns), jnp.bfloat16),
    ]
    macs = lambda n: n * pulse_count * 4 * columns * (freq_count + map_count * rows_here)
    [total] = call(
        early_kernel,
        [f32(map_count * rows_here, 2 * columns)],
        [facts, own_block, *near, twin, *twin_near, *curves[:2], ranges, cross[:, : early * deep]],
        work(early),
        2 * macs(early),
    )
    sent, kept = call(
        late_kernel,
        [b16(rows_here, 2 * columns), f32(rows_here, 2 * columns)],
        [facts, *far, twin_far, *curves[2:], ranges, cross[:, early * deep :], total],
        work(late),
        2 * macs(late),
    )
    arrived = lax.ppermute(sent, "map", [(0, 1), (1, 0)])

    capacity = max(2, 2 * rows_here // blk_count)
    holder_index = jnp.arange(blk_count, dtype=jnp.int32)
    row_tiles = strip_tiles[0, 0, :, 0]
    own_offsets = row_offsets[0, 0]
    tile_match = row_tiles[:, None] == holder_index[None, :]
    destination = jnp.sum(jnp.where(tile_match, tile_owner[None, :], 0), axis=1)
    row_number = jnp.arange(rows_here, dtype=jnp.int32)
    same_before = (row_tiles[:, None] == row_tiles[None, :]) & (
        row_number[None, :] < row_number[:, None]
    )
    rank_within = jnp.sum(same_before.astype(jnp.int32), axis=1)
    slot_index = destination * capacity + rank_within
    slot_hot = (
        jnp.arange(blk_count * capacity, dtype=jnp.int32)[:, None] == slot_index[None, :]
    ).astype(jnp.bfloat16)
    side = jnp.broadcast_to(own_offsets.astype(jnp.bfloat16)[:, None], (rows_here, SIDE))
    [packed] = call(
        pack_kernel,
        [b16(blk_count * capacity, 2 * columns + SIDE)],
        [facts, kept, arrived, slot_hot, side],
        (),
        2 * blk_count * capacity * rows_here * (2 * columns + SIDE),
    )
    packed = packed.reshape(blk_count, capacity, 2 * columns + SIDE)
    got = lax.all_to_all(packed, "blk", split_axis=0, concat_axis=0, tiled=True)
    got = got.reshape(blk_count * capacity, 2 * columns + SIDE)

    weights = interp_weights[0]
    real_out = jnp.dot(got[:, :columns], weights, preferred_element_type=jnp.float32)
    imag_out = jnp.dot(got[:, columns : 2 * columns], weights, preferred_element_type=jnp.float32)
    power = real_out * real_out + imag_out * imag_out
    offsets = got[:, 2 * columns].astype(jnp.int32)
    place_hot = (jnp.arange(MAPH, dtype=jnp.int32)[:, None] == offsets[None, :]).astype(
        jnp.bfloat16
    )
    high = power.astype(jnp.bfloat16)
    rest = power - high.astype(jnp.float32)
    middle = rest.astype(jnp.bfloat16)
    low = (rest - middle.astype(jnp.float32)).astype(jnp.bfloat16)
    tile_map = sum(
        jnp.dot(place_hot, piece, preferred_element_type=jnp.float32)
        for piece in (low, middle, high)
    )
    return tile_map.reshape(1, 1, MAPH, columns)


def solution(mesh):
    in_specs = (
        P("blk", "map", None, None),
        P("blk"),
        P("blk", None, None),
        P("blk", "map", None, None),
        P("blk", "map", None),
        P(),
    )
    out_specs = P("blk", "map", None, None)

    def run(*args):
        map_count, pulse_count, width = args[0].shape[1:]
        ranges = jnp.asarray(range_table(width // 2))
        crosses = jnp.asarray(
            cross_table(map_count, map_count * args[3].shape[2], pulse_count)
        )
        held = lambda *here: body(ranges, crosses, *here)
        return jax.shard_map(
            held, mesh=mesh, in_specs=in_specs, out_specs=out_specs, check_vma=False
        )(*args)

    return run
```

```python
import functools
import math

import jax
import jax.numpy as jnp
import ml_dtypes
import numpy as np
from jax import lax
from jax.experimental import pallas as pl
from jax.experimental.pallas import tpu as pltpu
from jax.sharding import PartitionSpec as P

STOPS = 8
MAPH = 256
SIDE = 128
GROUPS = (4, 2, 2)


def matching(count, distance, parity):
    seen, pairs = set(), []
    for start in range(count):
        cycle, at = [], start
        while at not in seen:
            seen.add(at)
            cycle.append(at)
            at = (at + distance) % count
        for place in range(parity, len(cycle) + parity, 2) if cycle else ():
            a, b = cycle[place % len(cycle)], cycle[(place + 1) % len(cycle)]
            pairs += [(a, b), (b, a)]
    return pairs


def range_table(freq_count):
    index = np.arange(freq_count, dtype=np.int64)
    angle = (index[:, None] * index[None, :] % freq_count).astype(np.float32) * np.float32(
        2.0 * math.pi / freq_count
    )
    factor = np.float32(1.0 / math.sqrt(freq_count))
    real_part, imag_part = np.cos(angle) * factor, -np.sin(angle) * factor
    table = np.block([[real_part, imag_part], [-imag_part, real_part]])
    return table.astype(ml_dtypes.bfloat16)


def stop_order(core):
    return [1, 4 - 2 * core, 3, 5, 2 - 2 * core, 6 - 2 * core, 6 * core, 7]


def cross_tables(map_count, row_count, pulse_count):
    span = STOPS * map_count * pulse_count
    rows = np.arange(row_count, dtype=np.int64)[:, None]
    factor = np.float32(1.0 / math.sqrt(span))
    tables, first = [], 0
    for size in GROUPS:
        table = []
        for m in range(map_count):
            for core in range(2):
                parts = []
                for k in stop_order(core)[first : first + size]:
                    along = (k * map_count + m) * pulse_count + np.arange(pulse_count)
                    angle = (rows * along[None, :] % span).astype(np.float32) * np.float32(
                        2.0 * math.pi / span
                    )
                    parts += [np.cos(angle) * factor, -np.sin(angle) * factor]
                table.append(np.concatenate(parts, axis=1))
        tables.append(np.stack(table).astype(ml_dtypes.bfloat16))
        first += size
    return tables


def call(kernel, outs, operands, scratch=(), flops=0, limit=24):
    specs = [pl.BlockSpec(memory_space=pltpu.SMEM)] + [
        pl.BlockSpec(memory_space=pltpu.VMEM) for _ in operands[1:]
    ]
    size = sum(math.prod(a.shape) * a.dtype.itemsize for a in [*operands, *outs])
    return pl.pallas_call(
        kernel,
        out_shape=outs,
        in_specs=specs,
        out_specs=[pl.BlockSpec(memory_space=pltpu.VMEM) for _ in outs],
        scratch_shapes=list(scratch),
        compiler_params=pltpu.CompilerParams(vmem_limit_bytes=limit * 2**20),
        cost_estimate=pl.CostEstimate(flops=flops, bytes_accessed=size, transcendentals=0),
    )(*operands)


def phase_kernel(map_count, span, facts, curvature, *curves):
    _, pulses, freqs = curves[0].shape
    width = freqs // 4
    core, here_map = facts[0], facts[3]
    outs = [
        (curves[2 * g], curves[2 * g + 1], p) for g, size in enumerate(GROUPS) for p in range(size)
    ]
    pulse = lax.broadcasted_iota(jnp.int32, (pulses, width), 0)
    fine = lax.broadcasted_iota(jnp.int32, (pulses, width), 1).astype(jnp.float32) / freqs
    pulse_on_lanes = lax.broadcasted_iota(jnp.int32, (STOPS, pulses), 1)
    stop_on_rows = lax.broadcasted_iota(jnp.int32, (STOPS, pulses), 0)

    def bend(stop, index):
        along = ((stop * map_count + here_map) * pulses + index).astype(jnp.float32) / span - 0.5
        return curvature[0] * (along * along)

    quarter = bend(stop_on_rows, pulse_on_lanes) * 0.25
    step = jnp.concatenate([jnp.cos(quarter), jnp.sin(quarter)] * (pulses // STOPS // 2), axis=0)
    turned = step.T
    stops = stop_order(core)
    for place in range(STOPS):
        cosines, sines, row = outs[place]
        options = sorted({stop_order(0)[place], stop_order(1)[place]})
        step_c, step_s = (
            turned[:, options[-1] + part : options[-1] + part + 1] for part in (0, STOPS)
        )
        if len(options) == 2:
            is_last = stops[place] == options[-1]
            step_c = jnp.where(is_last, step_c, turned[:, options[0] : options[0] + 1])
            step_s = jnp.where(
                is_last, step_s, turned[:, options[0] + STOPS : options[0] + STOPS + 1]
            )
        step_c = jnp.broadcast_to(step_c, (pulses, width))
        step_s = jnp.broadcast_to(step_s, (pulses, width))
        angle = bend(stops[place], pulse) * fine
        low_c, low_s = jnp.cos(angle), jnp.sin(angle)
        now_c = step_c * low_c - step_s * low_s
        now_s = step_s * low_c + step_c * low_s
        for h in range(4):
            now_c, now_s = step_c * now_c - step_s * now_s, step_s * now_c + step_c * now_s
            cosines[row, :, h * width : (h + 1) * width] = now_c
            sines[row, :, h * width : (h + 1) * width] = now_s


def transform(blocks, cosines, sines, ranges, phased, right_side):
    freqs = cosines.shape[2]
    pulses = cosines.shape[1]
    for place, block in enumerate(blocks):
        values = block().astype(jnp.float32)
        real_part, imag_part = values[:, :freqs], values[:, freqs:]
        cosine, sine = cosines[place], sines[place]
        rows = slice(place * pulses, (place + 1) * pulses)
        phased[rows, :freqs] = (real_part * cosine - imag_part * sine).astype(jnp.bfloat16)
        phased[rows, freqs:] = (real_part * sine + imag_part * cosine).astype(jnp.bfloat16)
    for half in range(2):
        columns = slice(half * freqs, (half + 1) * freqs)
        spectrum = jnp.dot(
            phased[...], ranges[:, columns], preferred_element_type=jnp.float32
        ).astype(jnp.bfloat16)
        for place in range(len(blocks)):
            piece = spectrum[place * pulses : (place + 1) * pulses]
            top = 2 * place * pulses
            right_side[top : top + pulses, columns] = piece
            other = slice((1 - half) * freqs, (2 - half) * freqs)
            right_side[top + pulses : top + 2 * pulses, other] = piece if half == 0 else -piece


def first_kernel(
    facts, own, near_a, near_b, twin, cosines, sines, ranges, cross, total, phased, right_side
):
    chip_odd = facts[1] == 1
    blocks = [
        lambda: jnp.where(chip_odd, near_a[...], near_b[...]),
        lambda: twin[...],
        lambda: own[...],
        lambda: jnp.where(chip_odd, near_b[...], near_a[...]),
    ]
    transform(blocks, cosines, sines, ranges, phased, right_side)
    total[...] = jnp.dot(cross[...], right_side[...], preferred_element_type=jnp.float32)


def second_kernel(
    facts, twin_a, twin_b, cosines, sines, ranges, cross, before, total, phased, right_side
):
    chip_odd = facts[1] == 1
    blocks = [
        lambda: jnp.where(chip_odd, twin_a[...], twin_b[...]),
        lambda: jnp.where(chip_odd, twin_b[...], twin_a[...]),
    ]
    transform(blocks, cosines, sines, ranges, phased, right_side)
    total[...] = before[...] + jnp.dot(
        cross[...], right_side[...], preferred_element_type=jnp.float32
    )


def last_kernel(
    facts, far_a, far_b, twin_far, cosines, sines, ranges, cross, total, sent, kept,
    phased, right_side,
):
    group_odd, here_map = facts[2] == 1, facts[3]
    blocks = [lambda: twin_far[...], lambda: jnp.where(group_odd, far_b[...], far_a[...])]
    transform(blocks, cosines, sines, ranges, phased, right_side)
    rows = sent.shape[0]
    for out, part in ((sent, 1 - here_map), (kept, here_map)):
        place = pl.ds(pl.multiple_of(part * rows, rows), rows)
        out[...] = (
            total[place, :]
            + jnp.dot(cross[place, :], right_side[...], preferred_element_type=jnp.float32)
        ).astype(out.dtype)


def pack_kernel(facts, kept, arrived, slot_hot, side, packed):
    width = kept.shape[1]
    image = (kept[...] + arrived[...].astype(jnp.float32)).astype(jnp.bfloat16)
    marks = 0.0
    for part in range(2):
        packed[:, part * width : (part + 1) * width] = jnp.dot(
            slot_hot[part], image, preferred_element_type=jnp.float32
        ).astype(packed.dtype)
        marks += jnp.dot(slot_hot[part], side[part], preferred_element_type=jnp.float32)
    packed[:, 2 * width :] = marks.astype(packed.dtype)


def map_kernel(facts, got, weights, out):
    columns = weights.shape[0]
    marks = got[:, 4 * columns :].astype(jnp.float32)
    total = 0.0
    for part in range(2):
        first = 2 * part * columns
        real_out = jnp.dot(
            got[:, first : first + columns], weights[...], preferred_element_type=jnp.float32
        )
        imag_out = jnp.dot(
            got[:, first + columns : first + 2 * columns],
            weights[...],
            preferred_element_type=jnp.float32,
        )
        power = real_out * real_out + imag_out * imag_out
        mark = marks[:, part * (SIDE // 2) : part * (SIDE // 2) + 1].astype(jnp.int32)
        spots = lax.broadcasted_iota(jnp.int32, (power.shape[0], MAPH), 1)
        hot = (mark == spots).astype(jnp.bfloat16)
        high = power.astype(jnp.bfloat16)
        low = (power - high.astype(jnp.float32)).astype(jnp.bfloat16)
        for piece in (low, high):
            total += lax.dot_general(
                hot, piece, (((0,), (0,)), ((), ())), preferred_element_type=jnp.float32
            )
    out[...] = total


def swap(block, count):
    return lax.ppermute(block, "blk", [(i, i ^ 1) for i in range(count)])


def slots(strip_tiles, row_offsets, tile_owner, blk_count):
    rows_here = strip_tiles.shape[2]
    capacity = max(2, 2 * rows_here // blk_count)
    row_tiles = strip_tiles[0, 0, :, 0]
    own_offsets = row_offsets[0, 0]
    tile_match = row_tiles[:, None] == jnp.arange(blk_count, dtype=jnp.int32)[None, :]
    destination = jnp.sum(jnp.where(tile_match, tile_owner[None, :], 0), axis=1)
    row_number = jnp.arange(rows_here, dtype=jnp.int32)
    same_before = (row_tiles[:, None] == row_tiles[None, :]) & (
        row_number[None, :] < row_number[:, None]
    )
    rank_within = jnp.sum(same_before.astype(jnp.int32), axis=1)
    slot_index = destination * capacity + rank_within
    numbers = jnp.arange(blk_count * capacity // 2, dtype=jnp.int32)[:, None] * 2
    slot_hot = jnp.stack([numbers + p == slot_index[None, :] for p in (0, 1)])
    lane_half = jnp.arange(SIDE, dtype=jnp.int32)[None, :] // (SIDE // 2)
    side = jnp.stack(
        [jnp.where(lane_half == p, own_offsets[:, None], 0).astype(jnp.bfloat16) for p in (0, 1)]
    )
    return slot_hot.astype(jnp.bfloat16), side


def body(ranges, crosses, phase_history, tile_curvature, interp_weights, strip_tiles, row_offsets, tile_owner):
    blk_count = lax.axis_size("blk")
    map_count = lax.axis_size("map")
    here_blk = lax.axis_index("blk")
    here_map = lax.axis_index("map")
    own_block = phase_history[0, 0]
    pulse_count = own_block.shape[0]
    freq_count = own_block.shape[1] // 2
    columns = interp_weights.shape[2]
    rows_here = strip_tiles.shape[2]

    core, chip_odd, group_odd = here_blk % 2, (here_blk // 2) % 2, (here_blk // 4) % 2
    facts = jnp.stack([core, chip_odd, group_odd, here_map]).astype(jnp.int32)
    slot_hot, side = slots(strip_tiles, row_offsets, tile_owner, blk_count)

    near = [lax.ppermute(own_block, "blk", matching(blk_count, 2, p)) for p in (0, 1)]
    far = [lax.ppermute(own_block, "blk", matching(blk_count, 4, p)) for p in (0, 1)]
    twin = swap(own_block, blk_count)

    f32 = lambda *shape: jax.ShapeDtypeStruct(shape, jnp.float32)
    b16 = lambda *shape: jax.ShapeDtypeStruct(shape, jnp.bfloat16)
    curves = pl.pallas_call(
        functools.partial(phase_kernel, map_count, STOPS * map_count * pulse_count),
        out_shape=[f32(n, pulse_count, freq_count) for n in GROUPS for _ in range(2)],
        in_specs=[pl.BlockSpec(memory_space=pltpu.SMEM)] * 2,
        out_specs=[pl.BlockSpec(memory_space=pltpu.VMEM)] * (2 * len(GROUPS)),
        compiler_params=pltpu.CompilerParams(vmem_limit_bytes=16 * 2**20),
        cost_estimate=pl.CostEstimate(flops=2**22, bytes_accessed=2**22, transcendentals=2**18),
    )(facts, tile_curvature)
    cross = [
        lax.dynamic_index_in_dim(table, here_map * 2 + core, 0, keepdims=False)
        for table in crosses
    ]
    near, twin, curves, cross, slot_hot, side = lax.optimization_barrier(
        (near, twin, curves, cross, slot_hot, side)
    )
    twin_near = [swap(block, blk_count) for block in near]

    deep = 2 * pulse_count
    work = lambda n: [
        pltpu.VMEM((n * pulse_count, 2 * freq_count), jnp.bfloat16),
        pltpu.VMEM((n * deep, 2 * columns), jnp.bfloat16),
    ]
    flops = lambda n: 2 * n * pulse_count * 4 * columns * (freq_count + map_count * rows_here)
    whole = f32(map_count * rows_here, 2 * columns)
    [total] = call(
        first_kernel,
        [whole],
        [facts, own_block, *near, twin, *curves[:2], ranges, cross[0]],
        work(GROUPS[0]),
        flops(GROUPS[0]),
    )
    far, total = lax.optimization_barrier((far, total))
    twin_far = swap(jnp.where(core == group_odd, far[0], far[1]), blk_count)
    [total] = call(
        second_kernel,
        [whole],
        [facts, *twin_near, *curves[2:4], ranges, cross[1], total],
        work(GROUPS[1]),
        flops(GROUPS[1]),
    )
    sent, kept = call(
        last_kernel,
        [b16(rows_here, 2 * columns), f32(rows_here, 2 * columns)],
        [facts, *far, twin_far, *curves[4:], ranges, cross[2], total],
        work(GROUPS[2]),
        flops(GROUPS[2]),
    )
    arrived = lax.ppermute(sent, "map", [(0, 1), (1, 0)])

    pairs = slot_hot.shape[1]
    wide = 4 * columns + SIDE
    [packed] = call(
        pack_kernel,
        [b16(pairs, wide)],
        [facts, kept, arrived, slot_hot, side],
        (),
        2 * pairs * rows_here * (wide + SIDE),
    )
    packed = packed.reshape(blk_count, pairs // blk_count, wide)
    got = lax.all_to_all(packed, "blk", split_axis=0, concat_axis=0, tiled=True)
    [tile_map] = call(
        map_kernel,
        [f32(MAPH, columns)],
        [facts, got.reshape(pairs, wide), interp_weights[0]],
        (),
        2 * pairs * 4 * columns * (columns + MAPH),
    )
    return tile_map.reshape(1, 1, MAPH, columns)


def solution(mesh):
    in_specs = (
        P("blk", "map", None, None),
        P("blk"),
        P("blk", None, None),
        P("blk", "map", None, None),
        P("blk", "map", None),
        P(),
    )
    out_specs = P("blk", "map", None, None)

    def run(*args):
        map_count, pulse_count, width = args[0].shape[1:]
        ranges = jnp.asarray(range_table(width // 2))
        crosses = [
            jnp.asarray(table)
            for table in cross_tables(map_count, map_count * args[3].shape[2], pulse_count)
        ]
        held = lambda *here: body(ranges, crosses, *here)
        return jax.shard_map(
            held, mesh=mesh, in_specs=in_specs, out_specs=out_specs, check_vma=False
        )(*args)

    return run
```

```python
import functools
import math

import jax
import jax.numpy as jnp
import ml_dtypes
import numpy as np
from jax import lax
from jax.experimental import pallas as pl
from jax.experimental.pallas import tpu as pltpu
from jax.sharding import PartitionSpec as P

STOPS = 8
MAPH = 256
SIDE = 128
GROUPS = (2, 2, 4)


def matching(count, distance, parity):
    seen, pairs = set(), []
    for start in range(count):
        cycle, at = [], start
        while at not in seen:
            seen.add(at)
            cycle.append(at)
            at = (at + distance) % count
        for place in range(parity, len(cycle) + parity, 2) if cycle else ():
            a, b = cycle[place % len(cycle)], cycle[(place + 1) % len(cycle)]
            pairs += [(a, b), (b, a)]
    return pairs


def range_table(freq_count):
    index = np.arange(freq_count, dtype=np.int64)
    angle = (index[:, None] * index[None, :] % freq_count).astype(np.float32) * np.float32(
        2.0 * math.pi / freq_count
    )
    factor = np.float32(1.0 / math.sqrt(freq_count))
    real_part, imag_part = np.cos(angle) * factor, -np.sin(angle) * factor
    table = np.block([[real_part, imag_part], [-imag_part, real_part]])
    return table.astype(ml_dtypes.bfloat16)


def stop_order(core):
    return [3, 4 - 2 * core, 1, 5, 2 - 2 * core, 6 - 2 * core, 6 * core, 7]


def cross_tables(map_count, row_count, pulse_count):
    span = STOPS * map_count * pulse_count
    rows = np.arange(row_count, dtype=np.int64)[:, None]
    factor = np.float32(1.0 / math.sqrt(span))
    tables, first = [], 0
    for size in GROUPS:
        table = []
        for m in range(map_count):
            for core in range(2):
                parts = []
                for k in stop_order(core)[first : first + size]:
                    along = (k * map_count + m) * pulse_count + np.arange(pulse_count)
                    angle = (rows * along[None, :] % span).astype(np.float32) * np.float32(
                        2.0 * math.pi / span
                    )
                    parts += [np.cos(angle) * factor, -np.sin(angle) * factor]
                table.append(np.concatenate(parts, axis=1))
        tables.append(np.stack(table).astype(ml_dtypes.bfloat16))
        first += size
    return tables


def call(kernel, outs, operands, scratch=(), flops=0, limit=24, far=()):
    specs = [pl.BlockSpec(memory_space=pltpu.SMEM)] + [
        pl.BlockSpec(memory_space=pltpu.HBM if n in far else pltpu.VMEM)
        for n in range(1, len(operands))
    ]
    size = sum(math.prod(a.shape) * a.dtype.itemsize for a in [*operands, *outs]) if flops else 0
    return pl.pallas_call(
        kernel,
        out_shape=outs,
        in_specs=specs,
        out_specs=[pl.BlockSpec(memory_space=pltpu.VMEM) for _ in outs],
        scratch_shapes=list(scratch),
        compiler_params=pltpu.CompilerParams(vmem_limit_bytes=limit * 2**20),
        cost_estimate=pl.CostEstimate(flops=flops, bytes_accessed=size, transcendentals=0),
    )(*operands)


def phase_kernel(map_count, span, facts, curvature, *curves):
    _, pulses, freqs = curves[0].shape
    width = freqs // 4
    core, here_map = facts[0], facts[3]
    outs = [
        (curves[2 * g], curves[2 * g + 1], p) for g, size in enumerate(GROUPS) for p in range(size)
    ]
    pulse = lax.broadcasted_iota(jnp.int32, (pulses, width), 0)
    fine = lax.broadcasted_iota(jnp.int32, (pulses, width), 1).astype(jnp.float32) / freqs
    pulse_on_lanes = lax.broadcasted_iota(jnp.int32, (STOPS, pulses), 1)
    stop_on_rows = lax.broadcasted_iota(jnp.int32, (STOPS, pulses), 0)

    def bend(stop, index):
        along = ((stop * map_count + here_map) * pulses + index).astype(jnp.float32) / span - 0.5
        return curvature[0] * (along * along)

    quarter = bend(stop_on_rows, pulse_on_lanes) * 0.25
    step = jnp.concatenate([jnp.cos(quarter), jnp.sin(quarter)] * (pulses // STOPS // 2), axis=0)
    turned = step.T
    stops = stop_order(core)
    for place in range(STOPS):
        cosines, sines, row = outs[place]
        options = sorted({stop_order(0)[place], stop_order(1)[place]})
        step_c, step_s = (
            turned[:, options[-1] + part : options[-1] + part + 1] for part in (0, STOPS)
        )
        if len(options) == 2:
            is_last = stops[place] == options[-1]
            step_c = jnp.where(is_last, step_c, turned[:, options[0] : options[0] + 1])
            step_s = jnp.where(
                is_last, step_s, turned[:, options[0] + STOPS : options[0] + STOPS + 1]
            )
        step_c = jnp.broadcast_to(step_c, (pulses, width))
        step_s = jnp.broadcast_to(step_s, (pulses, width))
        angle = bend(stops[place], pulse) * fine
        low_c, low_s = jnp.cos(angle), jnp.sin(angle)
        now_c = step_c * low_c - step_s * low_s
        now_s = step_s * low_c + step_c * low_s
        for h in range(4):
            now_c, now_s = step_c * now_c - step_s * now_s, step_s * now_c + step_c * now_s
            cosines[row, :, h * width : (h + 1) * width] = now_c
            sines[row, :, h * width : (h + 1) * width] = now_s


def transform(blocks, cosines, sines, ranges, phased, right_side):
    freqs = cosines.shape[2]
    pulses = cosines.shape[1]
    for place, block in enumerate(blocks):
        values = block().astype(jnp.float32)
        real_part, imag_part = values[:, :freqs], values[:, freqs:]
        cosine, sine = cosines[place], sines[place]
        rows = slice(place * pulses, (place + 1) * pulses)
        phased[rows, :freqs] = (real_part * cosine - imag_part * sine).astype(jnp.bfloat16)
        phased[rows, freqs:] = (real_part * sine + imag_part * cosine).astype(jnp.bfloat16)
    for half in range(2):
        columns = slice(half * freqs, (half + 1) * freqs)
        spectrum = jnp.dot(
            phased[...], ranges[:, columns], preferred_element_type=jnp.float32
        ).astype(jnp.bfloat16)
        for place in range(len(blocks)):
            piece = spectrum[place * pulses : (place + 1) * pulses]
            top = 2 * place * pulses
            right_side[top : top + pulses, columns] = piece
            other = slice((1 - half) * freqs, (2 - half) * freqs)
            right_side[top + pulses : top + 2 * pulses, other] = piece if half == 0 else -piece


def fetch(facts, tables, cross, arrival):
    copy = pltpu.make_async_copy(tables.at[facts[4]], cross, arrival)
    copy.start()
    return copy


def first_kernel(
    facts, own, twin, cosines, sines, ranges, tables, total, phased, right_side, cross, arrival
):
    copy = fetch(facts, tables, cross, arrival)
    transform([lambda: own[...], lambda: twin[...]], cosines, sines, ranges, phased, right_side)
    copy.wait()
    total[...] = jnp.dot(cross[...], right_side[...], preferred_element_type=jnp.float32)


def second_kernel(
    facts, near_a, near_b, cosines, sines, ranges, tables, before, total,
    phased, right_side, cross, arrival,
):
    copy = fetch(facts, tables, cross, arrival)
    chip_odd = facts[1] == 1
    blocks = [
        lambda: jnp.where(chip_odd, near_a[...], near_b[...]),
        lambda: jnp.where(chip_odd, near_b[...], near_a[...]),
    ]
    transform(blocks, cosines, sines, ranges, phased, right_side)
    copy.wait()
    total[...] = before[...] + jnp.dot(
        cross[...], right_side[...], preferred_element_type=jnp.float32
    )


def part_rows(ref, part):
    rows = ref.shape[0] // 2
    return ref[pl.ds(pl.multiple_of(part * rows, rows), rows), :]


def last_kernel(
    facts, twin_near_a, twin_near_b, far_a, far_b, twin_far_a, twin_far_b,
    cosines, sines, ranges, tables, before, sent, right_side, phased, cross, arrival,
):
    copy = fetch(facts, tables, cross, arrival)
    chip_odd, group_odd = facts[1] == 1, facts[2] == 1
    from_a = facts[0] != facts[2]
    blocks = [
        lambda: jnp.where(chip_odd, twin_near_a[...], twin_near_b[...]),
        lambda: jnp.where(chip_odd, twin_near_b[...], twin_near_a[...]),
        lambda: jnp.where(from_a, twin_far_a[...], twin_far_b[...]),
        lambda: jnp.where(group_odd, far_b[...], far_a[...]),
    ]
    transform(blocks, cosines, sines, ranges, phased, right_side)
    copy.wait()
    other = 1 - facts[3]
    sent[...] = (
        part_rows(before, other)
        + jnp.dot(
            part_rows(cross, other), right_side[...], preferred_element_type=jnp.float32
        )
    ).astype(sent.dtype)


def kept_kernel(facts, right_side, tables, before, kept, cross, arrival):
    copy = fetch(facts, tables, cross, arrival)
    copy.wait()
    kept[...] = part_rows(before, facts[3]) + jnp.dot(
        part_rows(cross, facts[3]), right_side[...], preferred_element_type=jnp.float32
    )


def slot_kernel(facts, tiles, offsets, owner, slot_hot, marks):
    count, rows = owner.shape[1], tiles.shape[1]
    _, pairs, _ = slot_hot.shape
    capacity = 2 * pairs // count
    tile_hot = (lax.broadcasted_iota(jnp.int32, (count, rows), 0) == tiles[...]).astype(
        jnp.bfloat16
    )
    owners = jnp.broadcast_to(owner[...].astype(jnp.float32), (8, count)).astype(jnp.bfloat16)
    holder = jnp.dot(owners, tile_hot, preferred_element_type=jnp.float32)[0:1]
    same = lax.dot_general(
        tile_hot, tile_hot, (((0,), (0,)), ((), ())), preferred_element_type=jnp.float32
    )
    earlier = lax.broadcasted_iota(jnp.int32, (rows, rows), 0) < lax.broadcasted_iota(
        jnp.int32, (rows, rows), 1
    )
    rank = jnp.sum(jnp.where(earlier, same, 0.0), axis=0, keepdims=True)
    slot = (holder * capacity + rank).astype(jnp.int32)
    numbers = 2 * lax.broadcasted_iota(jnp.int32, (pairs, rows), 0)
    half = marks.shape[1] // 2
    for part in range(2):
        hot = numbers + part == slot
        slot_hot[part] = hot.astype(jnp.float32).astype(jnp.bfloat16)
        mark = jnp.sum(
            jnp.where(hot, offsets[...].astype(jnp.float32), 0.0), axis=1, keepdims=True
        )
        spread = jnp.broadcast_to(mark, (pairs, half))
        sides = [spread, jnp.zeros_like(spread)]
        both = jnp.concatenate(sides if part == 0 else sides[::-1], axis=1)
        total = both if part == 0 else total + both
    marks[...] = total.astype(jnp.bfloat16)


def pack_kernel(facts, kept, arrived, slot_hot, marks, packed):
    width = kept.shape[1]
    image = (kept[...] + arrived[...].astype(jnp.float32)).astype(jnp.bfloat16)
    for part in range(2):
        packed[:, part * width : (part + 1) * width] = jnp.dot(
            slot_hot[part], image, preferred_element_type=jnp.float32
        ).astype(packed.dtype)
    packed[:, 2 * width :] = marks[...]


def map_kernel(facts, got, weights, out):
    columns = weights.shape[0]
    marks = got[:, 4 * columns :].astype(jnp.float32)
    total = 0.0
    for part in range(2):
        first = 2 * part * columns
        real_out = jnp.dot(
            got[:, first : first + columns], weights[...], preferred_element_type=jnp.float32
        )
        imag_out = jnp.dot(
            got[:, first + columns : first + 2 * columns],
            weights[...],
            preferred_element_type=jnp.float32,
        )
        power = real_out * real_out + imag_out * imag_out
        mark = marks[:, part * (SIDE // 2) : part * (SIDE // 2) + 1].astype(jnp.int32)
        spots = lax.broadcasted_iota(jnp.int32, (power.shape[0], MAPH), 1)
        hot = (mark == spots).astype(jnp.bfloat16)
        high = power.astype(jnp.bfloat16)
        low = (power - high.astype(jnp.float32)).astype(jnp.bfloat16)
        for piece in (low, high):
            total += lax.dot_general(
                hot, piece, (((0,), (0,)), ((), ())), preferred_element_type=jnp.float32
            )
    out[...] = total


def swap(block, count):
    return lax.ppermute(block, "blk", [(i, i ^ 1) for i in range(count)])


def body(ranges, crosses, phase_history, tile_curvature, interp_weights, strip_tiles, row_offsets, tile_owner):
    blk_count = lax.axis_size("blk")
    map_count = lax.axis_size("map")
    here_blk = lax.axis_index("blk")
    here_map = lax.axis_index("map")
    own_block = phase_history[0, 0]
    pulse_count = own_block.shape[0]
    freq_count = own_block.shape[1] // 2
    columns = interp_weights.shape[2]
    rows_here = strip_tiles.shape[2]

    core, chip_odd, group_odd = here_blk % 2, (here_blk // 2) % 2, (here_blk // 4) % 2
    facts = jnp.stack([core, chip_odd, group_odd, here_map, here_map * 2 + core]).astype(jnp.int32)

    near = [lax.ppermute(own_block, "blk", matching(blk_count, 2, p)) for p in (0, 1)]
    far = [lax.ppermute(own_block, "blk", matching(blk_count, 4, p)) for p in (0, 1)]
    twin = swap(own_block, blk_count)

    f32 = lambda *shape: jax.ShapeDtypeStruct(shape, jnp.float32)
    b16 = lambda *shape: jax.ShapeDtypeStruct(shape, jnp.bfloat16)
    curves = pl.pallas_call(
        functools.partial(phase_kernel, map_count, STOPS * map_count * pulse_count),
        out_shape=[f32(n, pulse_count, freq_count) for n in GROUPS for _ in range(2)],
        in_specs=[pl.BlockSpec(memory_space=pltpu.SMEM)] * 2,
        out_specs=[pl.BlockSpec(memory_space=pltpu.VMEM)] * (2 * len(GROUPS)),
        compiler_params=pltpu.CompilerParams(vmem_limit_bytes=16 * 2**20),
        cost_estimate=pl.CostEstimate(flops=2**22, bytes_accessed=2**22, transcendentals=2**18),
    )(facts, tile_curvature)
    deep = 2 * pulse_count
    image_shape = (map_count * rows_here, 2 * columns)
    half_shape = (rows_here, 2 * columns)
    right = lambda n: pltpu.VMEM((n * deep, 2 * columns), jnp.bfloat16)
    spread = lambda n: pltpu.VMEM((n * pulse_count, 2 * freq_count), jnp.bfloat16)
    table = lambda n: [
        pltpu.VMEM((map_count * rows_here, n * deep), jnp.bfloat16),
        pltpu.SemaphoreType.DMA,
    ]
    flops = lambda n: 2 * n * pulse_count * 4 * columns * (freq_count + map_count * rows_here)
    n = GROUPS[0]
    [total] = call(
        first_kernel,
        [f32(*image_shape)],
        [facts, own_block, twin, *curves[:2], ranges, crosses[0]],
        [spread(n), right(n), *table(n)],
        flops(n),
        far=(6,),
    )
    near, far, total = lax.optimization_barrier((near, far, total))
    twin_near = [swap(block, blk_count) for block in near]
    twin_far = [swap(block, blk_count) for block in far]
    n = GROUPS[1]
    [total] = call(
        second_kernel,
        [f32(*image_shape)],
        [facts, *near, *curves[2:4], ranges, crosses[1], total],
        [spread(n), right(n), *table(n)],
        flops(n),
        far=(6,),
    )
    twin_near, twin_far, total = lax.optimization_barrier((twin_near, twin_far, total))
    n = GROUPS[2]
    sent, right_side = call(
        last_kernel,
        [b16(*half_shape), b16(n * deep, 2 * columns)],
        [facts, *twin_near, *far, *twin_far, *curves[4:], ranges, crosses[2], total],
        [spread(n), *table(n)],
        flops(n),
        far=(10,),
    )
    sent, right_side, strip_tiles, row_offsets = lax.optimization_barrier(
        (sent, right_side, strip_tiles, row_offsets)
    )
    arrived = lax.ppermute(sent, "map", [(0, 1), (1, 0)])
    pairs = max(2, 2 * rows_here // blk_count) * blk_count // 2
    slot_hot, marks = call(
        slot_kernel,
        [b16(2, pairs, rows_here), b16(pairs, SIDE)],
        [
            facts,
            strip_tiles.reshape(1, rows_here),
            row_offsets.reshape(1, rows_here),
            tile_owner.reshape(1, blk_count),
        ],
    )
    [kept] = call(
        kept_kernel,
        [f32(*half_shape)],
        [facts, right_side, crosses[2], total],
        table(n),
        far=(2,),
    )

    wide = 4 * columns + SIDE
    [packed] = call(
        pack_kernel,
        [b16(pairs, wide)],
        [facts, kept, arrived, slot_hot, marks],
        (),
        2 * pairs * rows_here * wide,
    )
    packed = packed.reshape(blk_count, pairs // blk_count, wide)
    got = lax.all_to_all(packed, "blk", split_axis=0, concat_axis=0, tiled=True)
    [tile_map] = call(
        map_kernel,
        [f32(MAPH, columns)],
        [facts, got.reshape(pairs, wide), interp_weights[0]],
        (),
        2 * pairs * 4 * columns * (columns + MAPH),
    )
    return tile_map.reshape(1, 1, MAPH, columns)


def solution(mesh):
    in_specs = (
        P("blk", "map", None, None),
        P("blk"),
        P("blk", None, None),
        P("blk", "map", None, None),
        P("blk", "map", None),
        P(),
    )
    out_specs = P("blk", "map", None, None)

    def run(*args):
        map_count, pulse_count, width = args[0].shape[1:]
        ranges = jnp.asarray(range_table(width // 2))
        crosses = [
            jnp.asarray(table)
            for table in cross_tables(map_count, map_count * args[3].shape[2], pulse_count)
        ]
        held = lambda *here: body(ranges, crosses, *here)
        return jax.shard_map(
            held, mesh=mesh, in_specs=in_specs, out_specs=out_specs, check_vma=False
        )(*args)

    return run
```

```python
import functools
import math

import jax
import jax.numpy as jnp
import ml_dtypes
import numpy as np
from jax import lax
from jax.experimental import pallas as pl
from jax.experimental.pallas import tpu as pltpu
from jax.sharding import PartitionSpec as P

STOPS = 8
MAPH = 256
SIDE = 128
GROUPS = (2, 2, 4)


def matching(count, distance, parity):
    seen, pairs = set(), []
    for start in range(count):
        cycle, at = [], start
        while at not in seen:
            seen.add(at)
            cycle.append(at)
            at = (at + distance) % count
        for place in range(parity, len(cycle) + parity, 2) if cycle else ():
            a, b = cycle[place % len(cycle)], cycle[(place + 1) % len(cycle)]
            pairs += [(a, b), (b, a)]
    return pairs


def range_table(freq_count):
    index = np.arange(freq_count, dtype=np.int64)
    angle = (index[:, None] * index[None, :] % freq_count).astype(np.float32) * np.float32(
        2.0 * math.pi / freq_count
    )
    factor = np.float32(1.0 / math.sqrt(freq_count))
    real_part, imag_part = np.cos(angle) * factor, -np.sin(angle) * factor
    table = np.block([[real_part, imag_part], [-imag_part, real_part]])
    return table.astype(ml_dtypes.bfloat16)


def stop_order(core):
    return [3, 4 - 2 * core, 1, 5, 2 - 2 * core, 6 - 2 * core, 6 * core, 7]


def cross_tables(map_count, row_count, pulse_count):
    span = STOPS * map_count * pulse_count
    rows = np.arange(row_count, dtype=np.int64)[:, None]
    factor = np.float32(1.0 / math.sqrt(span))
    tables, first = [], 0
    for size in GROUPS:
        table = []
        for m in range(map_count):
            for core in range(2):
                parts = []
                for k in stop_order(core)[first : first + size]:
                    along = (k * map_count + m) * pulse_count + np.arange(pulse_count)
                    angle = (rows * along[None, :] % span).astype(np.float32) * np.float32(
                        2.0 * math.pi / span
                    )
                    parts += [np.cos(angle) * factor, -np.sin(angle) * factor]
                table.append(np.concatenate(parts, axis=1))
        tables.append(np.stack(table).astype(ml_dtypes.bfloat16))
        first += size
    return tables


def call(kernel, outs, operands, scratch=(), flops=0, limit=24, far=()):
    specs = [pl.BlockSpec(memory_space=pltpu.SMEM)] + [
        pl.BlockSpec(memory_space=pltpu.HBM if n in far else pltpu.VMEM)
        for n in range(1, len(operands))
    ]
    size = sum(math.prod(a.shape) * a.dtype.itemsize for a in [*operands, *outs]) if flops else 0
    return pl.pallas_call(
        kernel,
        out_shape=outs,
        in_specs=specs,
        out_specs=[pl.BlockSpec(memory_space=pltpu.VMEM) for _ in outs],
        scratch_shapes=list(scratch),
        compiler_params=pltpu.CompilerParams(vmem_limit_bytes=limit * 2**20),
        cost_estimate=pl.CostEstimate(flops=flops, bytes_accessed=size, transcendentals=0),
    )(*operands)


def phase_factors(map_count, span, facts, curvature, curves):
    _, pulses, freqs = curves[0].shape
    width = freqs // 4
    core, here_map = facts[0], facts[3]
    outs = [
        (curves[2 * g], curves[2 * g + 1], p) for g, size in enumerate(GROUPS) for p in range(size)
    ]
    pulse = lax.broadcasted_iota(jnp.int32, (pulses, width), 0)
    fine = lax.broadcasted_iota(jnp.int32, (pulses, width), 1).astype(jnp.float32) / freqs
    pulse_on_lanes = lax.broadcasted_iota(jnp.int32, (STOPS, pulses), 1)
    stop_on_rows = lax.broadcasted_iota(jnp.int32, (STOPS, pulses), 0)

    def bend(stop, index):
        along = ((stop * map_count + here_map) * pulses + index).astype(jnp.float32) / span - 0.5
        return curvature[0] * (along * along)

    quarter = bend(stop_on_rows, pulse_on_lanes) * 0.25
    step = jnp.concatenate([jnp.cos(quarter), jnp.sin(quarter)] * (pulses // STOPS // 2), axis=0)
    turned = step.T
    stops = stop_order(core)
    for place in range(STOPS):
        cosines, sines, row = outs[place]
        options = sorted({stop_order(0)[place], stop_order(1)[place]})
        step_c, step_s = (
            turned[:, options[-1] + part : options[-1] + part + 1] for part in (0, STOPS)
        )
        if len(options) == 2:
            is_last = stops[place] == options[-1]
            step_c = jnp.where(is_last, step_c, turned[:, options[0] : options[0] + 1])
            step_s = jnp.where(
                is_last, step_s, turned[:, options[0] + STOPS : options[0] + STOPS + 1]
            )
        step_c = jnp.broadcast_to(step_c, (pulses, width))
        step_s = jnp.broadcast_to(step_s, (pulses, width))
        angle = bend(stops[place], pulse) * fine
        low_c, low_s = jnp.cos(angle), jnp.sin(angle)
        now_c = step_c * low_c - step_s * low_s
        now_s = step_s * low_c + step_c * low_s
        for h in range(4):
            now_c, now_s = step_c * now_c - step_s * now_s, step_s * now_c + step_c * now_s
            cosines[row, :, h * width : (h + 1) * width] = now_c
            sines[row, :, h * width : (h + 1) * width] = now_s


def transform(blocks, cosines, sines, ranges, phased, right_side):
    freqs = cosines.shape[2]
    pulses = cosines.shape[1]
    for place, block in enumerate(blocks):
        values = block().astype(jnp.float32)
        real_part, imag_part = values[:, :freqs], values[:, freqs:]
        cosine, sine = cosines[place], sines[place]
        rows = slice(place * pulses, (place + 1) * pulses)
        phased[rows, :freqs] = (real_part * cosine - imag_part * sine).astype(jnp.bfloat16)
        phased[rows, freqs:] = (real_part * sine + imag_part * cosine).astype(jnp.bfloat16)
    for half in range(2):
        columns = slice(half * freqs, (half + 1) * freqs)
        spectrum = jnp.dot(
            phased[...], ranges[:, columns], preferred_element_type=jnp.float32
        ).astype(jnp.bfloat16)
        for place in range(len(blocks)):
            piece = spectrum[place * pulses : (place + 1) * pulses]
            top = 2 * place * pulses
            right_side[top : top + pulses, columns] = piece
            other = slice((1 - half) * freqs, (2 - half) * freqs)
            right_side[top + pulses : top + 2 * pulses, other] = piece if half == 0 else -piece


def fetch(facts, tables, cross, arrival):
    copy = pltpu.make_async_copy(tables.at[facts[4]], cross, arrival)
    copy.start()
    return copy


def first_kernel(
    map_count, span, facts, curvature, own_far, twin, tables, total, *rest
):
    later = 2 * len(GROUPS) - 2
    cosines, sines, phased, right_side, cross, own, ranges, arrival, own_here, ranges_here = rest[
        later:
    ]
    copies = [
        pltpu.make_async_copy(own_far, own, own_here),
        pltpu.make_async_copy(tables.at[facts[4], : ranges.shape[0]], ranges, ranges_here),
        pltpu.make_async_copy(
            tables.at[facts[4], ranges.shape[0] :, : cross.shape[1]], cross, arrival
        ),
    ]
    for copy in copies:
        copy.start()
    phase_factors(map_count, span, facts, curvature, (cosines, sines, *rest[:later]))
    for copy in copies:
        copy.wait()
    transform([lambda: own[...], lambda: twin[...]], cosines, sines, ranges, phased, right_side)
    total[...] = jnp.dot(cross[...], right_side[...], preferred_element_type=jnp.float32)


def second_kernel(
    facts, near_a, near_b, cosines, sines, ranges, tables, before, total,
    phased, right_side, cross, arrival,
):
    copy = fetch(facts, tables, cross, arrival)
    chip_odd = facts[1] == 1
    blocks = [
        lambda: jnp.where(chip_odd, near_a[...], near_b[...]),
        lambda: jnp.where(chip_odd, near_b[...], near_a[...]),
    ]
    transform(blocks, cosines, sines, ranges, phased, right_side)
    copy.wait()
    total[...] = before[...] + jnp.dot(
        cross[...], right_side[...], preferred_element_type=jnp.float32
    )


def part_rows(ref, part):
    rows = ref.shape[0] // 2
    return ref[pl.ds(pl.multiple_of(part * rows, rows), rows), :]


def last_kernel(
    facts, twin_near_a, twin_near_b, far_a, far_b, twin_far_a, twin_far_b,
    cosines, sines, ranges, tables, before, sent, right_side, phased, cross, arrival,
):
    copy = fetch(facts, tables, cross, arrival)
    chip_odd, group_odd = facts[1] == 1, facts[2] == 1
    from_a = facts[0] != facts[2]
    blocks = [
        lambda: jnp.where(chip_odd, twin_near_a[...], twin_near_b[...]),
        lambda: jnp.where(chip_odd, twin_near_b[...], twin_near_a[...]),
        lambda: jnp.where(from_a, twin_far_a[...], twin_far_b[...]),
        lambda: jnp.where(group_odd, far_b[...], far_a[...]),
    ]
    transform(blocks, cosines, sines, ranges, phased, right_side)
    copy.wait()
    other = 1 - facts[3]
    sent[...] = (
        part_rows(before, other)
        + jnp.dot(
            part_rows(cross, other), right_side[...], preferred_element_type=jnp.float32
        )
    ).astype(sent.dtype)


def kept_kernel(facts, right_side, tables, before, kept, cross, arrival):
    copy = fetch(facts, tables, cross, arrival)
    copy.wait()
    kept[...] = part_rows(before, facts[3]) + jnp.dot(
        part_rows(cross, facts[3]), right_side[...], preferred_element_type=jnp.float32
    )


def slot_kernel(facts, tiles, offsets, owner, slot_hot, marks):
    count, rows = owner.shape[1], tiles.shape[1]
    _, pairs, _ = slot_hot.shape
    capacity = 2 * pairs // count
    tile_hot = (lax.broadcasted_iota(jnp.int32, (count, rows), 0) == tiles[...]).astype(
        jnp.bfloat16
    )
    owners = jnp.broadcast_to(owner[...].astype(jnp.float32), (8, count)).astype(jnp.bfloat16)
    holder = jnp.dot(owners, tile_hot, preferred_element_type=jnp.float32)[0:1]
    same = lax.dot_general(
        tile_hot, tile_hot, (((0,), (0,)), ((), ())), preferred_element_type=jnp.float32
    )
    earlier = lax.broadcasted_iota(jnp.int32, (rows, rows), 0) < lax.broadcasted_iota(
        jnp.int32, (rows, rows), 1
    )
    rank = jnp.sum(jnp.where(earlier, same, 0.0), axis=0, keepdims=True)
    slot = (holder * capacity + rank).astype(jnp.int32)
    numbers = 2 * lax.broadcasted_iota(jnp.int32, (pairs, rows), 0)
    half = marks.shape[1] // 2
    for part in range(2):
        hot = numbers + part == slot
        slot_hot[part] = hot.astype(jnp.float32).astype(jnp.bfloat16)
        mark = jnp.sum(
            jnp.where(hot, offsets[...].astype(jnp.float32), 0.0), axis=1, keepdims=True
        )
        spread = jnp.broadcast_to(mark, (pairs, half))
        sides = [spread, jnp.zeros_like(spread)]
        both = jnp.concatenate(sides if part == 0 else sides[::-1], axis=1)
        total = both if part == 0 else total + both
    marks[...] = total.astype(jnp.bfloat16)


def pack_kernel(facts, kept, arrived, slot_hot, marks, packed):
    width = kept.shape[1]
    image = (kept[...] + arrived[...].astype(jnp.float32)).astype(jnp.bfloat16)
    for part in range(2):
        packed[:, part * width : (part + 1) * width] = jnp.dot(
            slot_hot[part], image, preferred_element_type=jnp.float32
        ).astype(packed.dtype)
    packed[:, 2 * width :] = marks[...]


def map_kernel(facts, got, weights, out):
    columns = weights.shape[0]
    pairs = got.shape[0]
    parts = [got[:, n * columns : (n + 1) * columns] for n in range(4)]
    mapped = jnp.dot(
        jnp.concatenate(parts, axis=0), weights[...], preferred_element_type=jnp.float32
    )
    squared = mapped * mapped
    marks = got[:, 4 * columns :].astype(jnp.float32).T
    spots = lax.broadcasted_iota(jnp.int32, (MAPH, pairs), 0)
    hots, pieces = [], []
    for part in range(2):
        real_out = squared[2 * part * pairs : (2 * part + 1) * pairs]
        power = real_out + squared[(2 * part + 1) * pairs : (2 * part + 2) * pairs]
        mark = marks[part * (SIDE // 2) : part * (SIDE // 2) + 1].astype(jnp.int32)
        hot = (mark == spots).astype(jnp.float32).astype(jnp.bfloat16)
        high = power.astype(jnp.bfloat16)
        low = (power - high.astype(jnp.float32)).astype(jnp.bfloat16)
        hots += [hot, hot]
        pieces += [low, high]
    out[...] = jnp.dot(
        jnp.concatenate(hots, axis=1),
        jnp.concatenate(pieces, axis=0),
        preferred_element_type=jnp.float32,
    )


def swap(block, count):
    return lax.ppermute(block, "blk", [(i, i ^ 1) for i in range(count)])


def body(ranges, crosses, phase_history, tile_curvature, interp_weights, strip_tiles, row_offsets, tile_owner):
    blk_count = lax.axis_size("blk")
    map_count = lax.axis_size("map")
    here_blk = lax.axis_index("blk")
    here_map = lax.axis_index("map")
    own_block = phase_history[0, 0]
    pulse_count = own_block.shape[0]
    freq_count = own_block.shape[1] // 2
    columns = interp_weights.shape[2]
    rows_here = strip_tiles.shape[2]

    core, chip_odd, group_odd = here_blk % 2, (here_blk // 2) % 2, (here_blk // 4) % 2
    facts = jnp.stack([core, chip_odd, group_odd, here_map, here_map * 2 + core]).astype(jnp.int32)

    near = [lax.ppermute(own_block, "blk", matching(blk_count, 2, p)) for p in (0, 1)]
    far = [lax.ppermute(own_block, "blk", matching(blk_count, 4, p)) for p in (0, 1)]
    twin = swap(own_block, blk_count)

    f32 = lambda *shape: jax.ShapeDtypeStruct(shape, jnp.float32)
    b16 = lambda *shape: jax.ShapeDtypeStruct(shape, jnp.bfloat16)
    deep = 2 * pulse_count
    image_shape = (map_count * rows_here, 2 * columns)
    half_shape = (rows_here, 2 * columns)
    right = lambda n: pltpu.VMEM((n * deep, 2 * columns), jnp.bfloat16)
    spread = lambda n: pltpu.VMEM((n * pulse_count, 2 * freq_count), jnp.bfloat16)
    table = lambda n: [
        pltpu.VMEM((map_count * rows_here, n * deep), jnp.bfloat16),
        pltpu.SemaphoreType.DMA,
    ]
    flops = lambda n: 2 * n * pulse_count * 4 * columns * (freq_count + map_count * rows_here)
    n = GROUPS[0]
    smem, vmem, hbm = (
        pl.BlockSpec(memory_space=kind) for kind in (pltpu.SMEM, pltpu.VMEM, pltpu.HBM)
    )
    total, *curves = pl.pallas_call(
        functools.partial(first_kernel, map_count, STOPS * map_count * pulse_count),
        out_shape=[f32(*image_shape)]
        + [f32(size, pulse_count, freq_count) for size in GROUPS[1:] for _ in range(2)],
        in_specs=[smem, smem, hbm, vmem, hbm],
        out_specs=[vmem] * (2 * len(GROUPS) - 1),
        scratch_shapes=[pltpu.VMEM((n, pulse_count, freq_count), jnp.float32)] * 2
        + [
            spread(n),
            right(n),
            table(n)[0],
            pltpu.VMEM(own_block.shape, jnp.bfloat16),
            pltpu.VMEM(ranges.shape, jnp.bfloat16),
        ]
        + [pltpu.SemaphoreType.DMA] * 3,
        compiler_params=pltpu.CompilerParams(vmem_limit_bytes=44 * 2**20),
        cost_estimate=pl.CostEstimate(flops=flops(n), bytes_accessed=0, transcendentals=2**18),
    )(facts, tile_curvature, own_block, twin, crosses[0])
    far, near, total = lax.optimization_barrier((far, near, total))
    twin_near = [swap(block, blk_count) for block in near]
    twin_far = [swap(block, blk_count) for block in far]
    n = GROUPS[1]
    [total] = call(
        second_kernel,
        [f32(*image_shape)],
        [facts, *near, *curves[:2], ranges, crosses[1], total],
        [spread(n), right(n), *table(n)],
        flops(n),
        far=(6,),
    )
    twin_near, twin_far, total = lax.optimization_barrier((twin_near, twin_far, total))
    n = GROUPS[2]
    sent, right_side = call(
        last_kernel,
        [b16(*half_shape), b16(n * deep, 2 * columns)],
        [facts, *twin_near, *far, *twin_far, *curves[2:], ranges, crosses[2], total],
        [spread(n), *table(n)],
        flops(n),
        far=(10,),
    )
    sent, right_side, strip_tiles, row_offsets = lax.optimization_barrier(
        (sent, right_side, strip_tiles, row_offsets)
    )
    arrived = lax.ppermute(sent, "map", [(0, 1), (1, 0)])
    pairs = max(2, 2 * rows_here // blk_count) * blk_count // 2
    slot_hot, marks = call(
        slot_kernel,
        [b16(2, pairs, rows_here), b16(pairs, SIDE)],
        [
            facts,
            strip_tiles.reshape(1, rows_here),
            row_offsets.reshape(1, rows_here),
            tile_owner.reshape(1, blk_count),
        ],
    )
    [kept] = call(
        kept_kernel,
        [f32(*half_shape)],
        [facts, right_side, crosses[2], total],
        table(n),
        far=(2,),
    )

    wide = 4 * columns + SIDE
    [packed] = call(
        pack_kernel,
        [b16(pairs, wide)],
        [facts, kept, arrived, slot_hot, marks],
        (),
        2 * pairs * rows_here * wide,
    )
    packed = packed.reshape(blk_count, pairs // blk_count, wide)
    got = lax.all_to_all(packed, "blk", split_axis=0, concat_axis=0, tiled=True)
    [tile_map] = call(
        map_kernel,
        [f32(MAPH, columns)],
        [facts, got.reshape(pairs, wide), interp_weights[0]],
        (),
        2 * pairs * 4 * columns * (columns + MAPH),
    )
    return tile_map.reshape(1, 1, MAPH, columns)


def solution(mesh):
    in_specs = (
        P("blk", "map", None, None),
        P("blk"),
        P("blk", None, None),
        P("blk", "map", None, None),
        P("blk", "map", None),
        P(),
    )
    out_specs = P("blk", "map", None, None)

    def run(*args):
        map_count, pulse_count, width = args[0].shape[1:]
        ranges = jnp.asarray(range_table(width // 2))
        crosses = cross_tables(map_count, map_count * args[3].shape[2], pulse_count)
        first = np.zeros((len(crosses[0]), width + crosses[0].shape[1], width), crosses[0].dtype)
        first[:, : width] = range_table(width // 2)
        first[:, width : , : crosses[0].shape[2]] = crosses[0]
        crosses = [jnp.asarray(table) for table in (first, *crosses[1:])]
        held = lambda *here: body(ranges, crosses, *here)
        return jax.shard_map(
            held, mesh=mesh, in_specs=in_specs, out_specs=out_specs, check_vma=False
        )(*args)

    return run
```

```python
import functools
import math

import jax
import jax.numpy as jnp
import ml_dtypes
import numpy as np
from jax import lax
from jax.experimental import pallas as pl
from jax.experimental.pallas import tpu as pltpu
from jax.sharding import PartitionSpec as P

STOPS = 8
MAPH = 256
SIDE = 128
GROUPS = (2, 2, 4)


def matching(count, distance, parity):
    seen, pairs = set(), []
    for start in range(count):
        cycle, at = [], start
        while at not in seen:
            seen.add(at)
            cycle.append(at)
            at = (at + distance) % count
        for place in range(parity, len(cycle) + parity, 2) if cycle else ():
            a, b = cycle[place % len(cycle)], cycle[(place + 1) % len(cycle)]
            pairs += [(a, b), (b, a)]
    return pairs


def range_tables(freq_count):
    index = np.arange(freq_count, dtype=np.int64)
    angle = (index[: freq_count // 2, None] * index[None, :] % freq_count).astype(
        np.float32
    ) * np.float32(2.0 * math.pi / freq_count)
    factor = np.float32(1.0 / math.sqrt(freq_count))
    real_part, imag_part = np.cos(angle) * factor, -np.sin(angle) * factor
    tables = [
        np.block([[real_part[:, p::2], imag_part[:, p::2]], [-imag_part[:, p::2], real_part[:, p::2]]])
        for p in (0, 1)
    ]
    return np.concatenate(tables).astype(ml_dtypes.bfloat16)


def stop_order(core):
    return [3, 4 - 2 * core, 1, 5, 2 - 2 * core, 6 - 2 * core, 6 * core, 7]


def cross_tables(map_count, row_count, pulse_count):
    span = STOPS * map_count * pulse_count
    rows = np.arange(row_count, dtype=np.int64)[:, None]
    factor = np.float32(1.0 / math.sqrt(span))
    tables, first = [], 0
    for size in GROUPS:
        table = []
        for m in range(map_count):
            for core in range(2):
                parts = []
                for k in stop_order(core)[first : first + size]:
                    along = (k * map_count + m) * pulse_count + np.arange(pulse_count)
                    angle = (rows * along[None, :] % span).astype(np.float32) * np.float32(
                        2.0 * math.pi / span
                    )
                    parts += [np.cos(angle) * factor, -np.sin(angle) * factor]
                table.append(np.concatenate(parts, axis=1))
        tables.append(np.stack(table).astype(ml_dtypes.bfloat16))
        first += size
    return tables


def call(kernel, outs, operands, scratch=(), flops=0, limit=24, far=()):
    specs = [
        pl.BlockSpec(memory_space=pltpu.HBM if n in far else pltpu.VMEM)
        for n in range(len(operands))
    ]
    size = sum(math.prod(a.shape) * a.dtype.itemsize for a in [*operands, *outs]) if flops else 0
    return pl.pallas_call(
        kernel,
        out_shape=outs,
        in_specs=specs,
        out_specs=[pl.BlockSpec(memory_space=pltpu.VMEM) for _ in outs],
        scratch_shapes=list(scratch),
        compiler_params=pltpu.CompilerParams(vmem_limit_bytes=limit * 2**20),
        cost_estimate=pl.CostEstimate(flops=flops, bytes_accessed=size, transcendentals=0),
    )(*operands)


def whereabouts():
    here, here_map = lax.axis_index("blk"), lax.axis_index("map")
    core = here % 2
    return core, here // 2 % 2, here // 4 % 2, here_map, here_map * 2 + core


def phase_factors(map_count, span, curvature, curves):
    _, pulses, freqs = curves[0].shape
    width = freqs // 4
    core, _, _, here_map, _ = whereabouts()
    outs = [
        (curves[2 * g], curves[2 * g + 1], p) for g, size in enumerate(GROUPS) for p in range(size)
    ]
    pulse = lax.broadcasted_iota(jnp.int32, (pulses, width), 0)
    fine = lax.broadcasted_iota(jnp.int32, (pulses, width), 1).astype(jnp.float32) / freqs
    pulse_on_lanes = lax.broadcasted_iota(jnp.int32, (STOPS, pulses), 1)
    stop_on_rows = lax.broadcasted_iota(jnp.int32, (STOPS, pulses), 0)

    def bend(stop, index):
        along = ((stop * map_count + here_map) * pulses + index).astype(jnp.float32) / span - 0.5
        return curvature[0] * (along * along)

    quarter = bend(stop_on_rows, pulse_on_lanes) * 0.25
    step = jnp.concatenate([jnp.cos(quarter), jnp.sin(quarter)] * (pulses // STOPS // 2), axis=0)
    turned = step.T
    stops = stop_order(core)
    for place in range(STOPS):
        cosines, sines, row = outs[place]
        options = sorted({stop_order(0)[place], stop_order(1)[place]})
        step_c, step_s = (
            turned[:, options[-1] + part : options[-1] + part + 1] for part in (0, STOPS)
        )
        if len(options) == 2:
            is_last = stops[place] == options[-1]
            step_c = jnp.where(is_last, step_c, turned[:, options[0] : options[0] + 1])
            step_s = jnp.where(
                is_last, step_s, turned[:, options[0] + STOPS : options[0] + STOPS + 1]
            )
        step_c = jnp.broadcast_to(step_c, (pulses, width))
        step_s = jnp.broadcast_to(step_s, (pulses, width))
        angle = bend(stops[place], pulse) * fine
        low_c, low_s = jnp.cos(angle), jnp.sin(angle)
        now_c = step_c * low_c - step_s * low_s
        now_s = step_s * low_c + step_c * low_s
        for h in range(4):
            now_c, now_s = step_c * now_c - step_s * now_s, step_s * now_c + step_c * now_s
            cosines[row, :, h * width : (h + 1) * width] = now_c
            sines[row, :, h * width : (h + 1) * width] = now_s


def transform(blocks, cosines, sines, ranges, phased, right_side):
    freqs = cosines.shape[2]
    pulses = cosines.shape[1]
    half = freqs // 2
    for place, block in enumerate(blocks):
        values = block().astype(jnp.float32)
        real_part, imag_part = values[:, :freqs], values[:, freqs:]
        cosine, sine = cosines[place], sines[place]
        rows = slice(place * pulses, (place + 1) * pulses)
        turned = (real_part * cosine - imag_part * sine, real_part * sine + imag_part * cosine)
        for n, part in enumerate(turned):
            columns = slice(n * half, (n + 1) * half)
            low, high = part[:, :half], part[:, half:]
            phased[0, rows, columns] = (low + high).astype(jnp.bfloat16)
            phased[1, rows, columns] = (low - high).astype(jnp.bfloat16)
    for parity in range(2):
        spectrum = jnp.dot(
            phased[parity],
            ranges[parity * freqs : (parity + 1) * freqs],
            preferred_element_type=jnp.float32,
        ).astype(jnp.bfloat16)
        first = slice(parity * half, (parity + 1) * half)
        second = slice(freqs + parity * half, freqs + (parity + 1) * half)
        for place in range(len(blocks)):
            piece = spectrum[place * pulses : (place + 1) * pulses]
            real_part, imag_part = piece[:, :half], piece[:, half:]
            top = slice(2 * place * pulses, (2 * place + 1) * pulses)
            below = slice((2 * place + 1) * pulses, (2 * place + 2) * pulses)
            right_side[top, first] = real_part
            right_side[top, second] = imag_part
            right_side[below, first] = -imag_part
            right_side[below, second] = real_part


def fetch(tables, cross, arrival):
    copy = pltpu.make_async_copy(tables.at[whereabouts()[4]], cross, arrival)
    copy.start()
    return copy


def first_kernel(
    map_count, span, curvature, own_far, twin, tables, total, *rest
):
    later = 2 * len(GROUPS) - 2
    cosines, sines, phased, right_side, cross, own, ranges, arrival, own_here, ranges_here = rest[
        later:
    ]
    index = whereabouts()[4]
    copies = [
        pltpu.make_async_copy(own_far, own, own_here),
        pltpu.make_async_copy(
            tables.at[index, : ranges.shape[0], : ranges.shape[1]], ranges, ranges_here
        ),
        pltpu.make_async_copy(
            tables.at[index, ranges.shape[0] :, : cross.shape[1]], cross, arrival
        ),
    ]
    for copy in copies:
        copy.start()
    phase_factors(map_count, span, curvature, (cosines, sines, *rest[:later]))
    for copy in copies:
        copy.wait()
    transform([lambda: own[...], lambda: twin[...]], cosines, sines, ranges, phased, right_side)
    total[...] = jnp.dot(cross[...], right_side[...], preferred_element_type=jnp.float32)


def second_kernel(
    near_a, near_b, cosines, sines, ranges, tables, before, total,
    phased, right_side, cross, arrival,
):
    copy = fetch(tables, cross, arrival)
    chip_odd = whereabouts()[1] == 1
    blocks = [
        lambda: jnp.where(chip_odd, near_a[...], near_b[...]),
        lambda: jnp.where(chip_odd, near_b[...], near_a[...]),
    ]
    transform(blocks, cosines, sines, ranges, phased, right_side)
    copy.wait()
    total[...] = before[...] + jnp.dot(
        cross[...], right_side[...], preferred_element_type=jnp.float32
    )


def part_rows(ref, part):
    rows = ref.shape[0] // 2
    return ref[pl.ds(pl.multiple_of(part * rows, rows), rows), :]


def last_kernel(
    twin_near_a, twin_near_b, far_a, far_b, twin_far_a, twin_far_b,
    cosines, sines, ranges, tables, before, sent, right_side, phased, cross, arrival,
):
    copy = fetch(tables, cross, arrival)
    core, chip, group, here_map, _ = whereabouts()
    chip_odd, group_odd, from_a = chip == 1, group == 1, core != group
    blocks = [
        lambda: jnp.where(chip_odd, twin_near_a[...], twin_near_b[...]),
        lambda: jnp.where(chip_odd, twin_near_b[...], twin_near_a[...]),
        lambda: jnp.where(from_a, twin_far_a[...], twin_far_b[...]),
        lambda: jnp.where(group_odd, far_b[...], far_a[...]),
    ]
    transform(blocks, cosines, sines, ranges, phased, right_side)
    copy.wait()
    other = 1 - here_map
    sent[...] = (
        part_rows(before, other)
        + jnp.dot(
            part_rows(cross, other), right_side[...], preferred_element_type=jnp.float32
        )
    ).astype(sent.dtype)


def kept_kernel(right_side, tables, before, kept, cross, arrival):
    copy = fetch(tables, cross, arrival)
    copy.wait()
    here_map = whereabouts()[3]
    kept[...] = part_rows(before, here_map) + jnp.dot(
        part_rows(cross, here_map), right_side[...], preferred_element_type=jnp.float32
    )


def slot_kernel(tiles, offsets, owner, weights, slot_hot, marks, ordered):
    columns = weights.shape[0]
    place = lax.broadcasted_iota(jnp.int32, weights.shape, 0)
    source = jnp.where(place < columns // 2, 2 * place, 2 * place - columns + 1)
    order = source == lax.broadcasted_iota(jnp.int32, weights.shape, 1)
    ordered[...] = jnp.dot(
        order.astype(jnp.float32).astype(jnp.bfloat16),
        weights[...],
        preferred_element_type=jnp.float32,
    ).astype(jnp.bfloat16)
    count, rows = owner.shape[1], tiles.shape[1]
    _, pairs, _ = slot_hot.shape
    capacity = 2 * pairs // count
    tile_hot = (lax.broadcasted_iota(jnp.int32, (count, rows), 0) == tiles[...]).astype(
        jnp.bfloat16
    )
    owners = jnp.broadcast_to(owner[...].astype(jnp.float32), (8, count)).astype(jnp.bfloat16)
    holder = jnp.dot(owners, tile_hot, preferred_element_type=jnp.float32)[0:1]
    same = lax.dot_general(
        tile_hot, tile_hot, (((0,), (0,)), ((), ())), preferred_element_type=jnp.float32
    )
    earlier = lax.broadcasted_iota(jnp.int32, (rows, rows), 0) < lax.broadcasted_iota(
        jnp.int32, (rows, rows), 1
    )
    rank = jnp.sum(jnp.where(earlier, same, 0.0), axis=0, keepdims=True)
    slot = (holder * capacity + rank).astype(jnp.int32)
    numbers = 2 * lax.broadcasted_iota(jnp.int32, (pairs, rows), 0)
    half = marks.shape[1] // 2
    for part in range(2):
        hot = numbers + part == slot
        slot_hot[part] = hot.astype(jnp.float32).astype(jnp.bfloat16)
        mark = jnp.sum(
            jnp.where(hot, offsets[...].astype(jnp.float32), 0.0), axis=1, keepdims=True
        )
        spread = jnp.broadcast_to(mark, (pairs, half))
        sides = [spread, jnp.zeros_like(spread)]
        both = jnp.concatenate(sides if part == 0 else sides[::-1], axis=1)
        total = both if part == 0 else total + both
    marks[...] = total.astype(jnp.bfloat16)


def pack_kernel(kept, arrived, slot_hot, marks, packed):
    width = kept.shape[1]
    image = (kept[...] + arrived[...].astype(jnp.float32)).astype(jnp.bfloat16)
    for part in range(2):
        packed[:, part * width : (part + 1) * width] = jnp.dot(
            slot_hot[part], image, preferred_element_type=jnp.float32
        ).astype(packed.dtype)
    packed[:, 2 * width :] = marks[...]


def map_kernel(got, weights, out):
    columns = weights.shape[0]
    pairs = got.shape[0]
    parts = [got[:, n * columns : (n + 1) * columns] for n in range(4)]
    mapped = jnp.dot(
        jnp.concatenate(parts, axis=0), weights[...], preferred_element_type=jnp.float32
    )
    squared = mapped * mapped
    marks = got[:, 4 * columns :].astype(jnp.float32).T
    spots = lax.broadcasted_iota(jnp.int32, (MAPH, pairs), 0)
    hots, pieces = [], []
    for part in range(2):
        real_out = squared[2 * part * pairs : (2 * part + 1) * pairs]
        power = real_out + squared[(2 * part + 1) * pairs : (2 * part + 2) * pairs]
        mark = marks[part * (SIDE // 2) : part * (SIDE // 2) + 1].astype(jnp.int32)
        hot = (mark == spots).astype(jnp.float32).astype(jnp.bfloat16)
        high = power.astype(jnp.bfloat16)
        low = (power - high.astype(jnp.float32)).astype(jnp.bfloat16)
        hots += [hot, hot]
        pieces += [low, high]
    out[...] = jnp.dot(
        jnp.concatenate(hots, axis=1),
        jnp.concatenate(pieces, axis=0),
        preferred_element_type=jnp.float32,
    )


def swap(block, count):
    return lax.ppermute(block, "blk", [(i, i ^ 1) for i in range(count)])


def body(ranges, crosses, phase_history, tile_curvature, interp_weights, strip_tiles, row_offsets, tile_owner):
    blk_count = lax.axis_size("blk")
    map_count = lax.axis_size("map")
    own_block = phase_history[0, 0]
    pulse_count = own_block.shape[0]
    freq_count = own_block.shape[1] // 2
    columns = interp_weights.shape[2]
    rows_here = strip_tiles.shape[2]

    near = [lax.ppermute(own_block, "blk", matching(blk_count, 2, p)) for p in (0, 1)]
    far = [lax.ppermute(own_block, "blk", matching(blk_count, 4, p)) for p in (0, 1)]
    twin = swap(own_block, blk_count)

    f32 = lambda *shape: jax.ShapeDtypeStruct(shape, jnp.float32)
    b16 = lambda *shape: jax.ShapeDtypeStruct(shape, jnp.bfloat16)
    deep = 2 * pulse_count
    image_shape = (map_count * rows_here, 2 * columns)
    half_shape = (rows_here, 2 * columns)
    right = lambda n: pltpu.VMEM((n * deep, 2 * columns), jnp.bfloat16)
    spread = lambda n: pltpu.VMEM((2, n * pulse_count, freq_count), jnp.bfloat16)
    table = lambda n: [
        pltpu.VMEM((map_count * rows_here, n * deep), jnp.bfloat16),
        pltpu.SemaphoreType.DMA,
    ]
    flops = lambda n: 2 * n * pulse_count * 4 * columns * (freq_count + map_count * rows_here)
    n = GROUPS[0]
    smem, vmem, hbm = (
        pl.BlockSpec(memory_space=kind) for kind in (pltpu.SMEM, pltpu.VMEM, pltpu.HBM)
    )
    total, *curves = pl.pallas_call(
        functools.partial(first_kernel, map_count, STOPS * map_count * pulse_count),
        out_shape=[f32(*image_shape)]
        + [f32(size, pulse_count, freq_count) for size in GROUPS[1:] for _ in range(2)],
        in_specs=[smem, hbm, vmem, hbm],
        out_specs=[vmem] * (2 * len(GROUPS) - 1),
        scratch_shapes=[pltpu.VMEM((n, pulse_count, freq_count), jnp.float32)] * 2
        + [
            spread(n),
            right(n),
            table(n)[0],
            pltpu.VMEM(own_block.shape, jnp.bfloat16),
            pltpu.VMEM(ranges.shape, jnp.bfloat16),
        ]
        + [pltpu.SemaphoreType.DMA] * 3,
        compiler_params=pltpu.CompilerParams(vmem_limit_bytes=44 * 2**20),
        cost_estimate=pl.CostEstimate(flops=flops(n), bytes_accessed=0, transcendentals=2**18),
    )(tile_curvature, own_block, twin, crosses[0])
    far, near, total = lax.optimization_barrier((far, near, total))
    twin_near = [swap(block, blk_count) for block in near]
    twin_far = [swap(block, blk_count) for block in far]
    n = GROUPS[1]
    [total] = call(
        second_kernel,
        [f32(*image_shape)],
        [*near, *curves[:2], ranges, crosses[1], total],
        [spread(n), right(n), *table(n)],
        flops(n),
        far=(5,),
    )
    twin_near, twin_far, total = lax.optimization_barrier((twin_near, twin_far, total))
    n = GROUPS[2]
    sent, right_side = call(
        last_kernel,
        [b16(*half_shape), b16(n * deep, 2 * columns)],
        [*twin_near, *far, *twin_far, *curves[2:], ranges, crosses[2], total],
        [spread(n), *table(n)],
        flops(n),
        far=(9,),
    )
    sent, right_side, strip_tiles, row_offsets, interp_weights = lax.optimization_barrier(
        (sent, right_side, strip_tiles, row_offsets, interp_weights)
    )
    arrived = lax.ppermute(sent, "map", [(0, 1), (1, 0)])
    pairs = max(2, 2 * rows_here // blk_count) * blk_count // 2
    slot_hot, marks, ordered = call(
        slot_kernel,
        [b16(2, pairs, rows_here), b16(pairs, SIDE), b16(columns, columns)],
        [
            strip_tiles.reshape(1, rows_here),
            row_offsets.reshape(1, rows_here),
            tile_owner.reshape(1, blk_count),
            interp_weights[0],
        ],
    )
    [kept] = call(
        kept_kernel,
        [f32(*half_shape)],
        [right_side, crosses[2], total],
        table(n),
        far=(1,),
    )

    wide = 4 * columns + SIDE
    [packed] = call(
        pack_kernel,
        [b16(pairs, wide)],
        [kept, arrived, slot_hot, marks],
        (),
        2 * pairs * rows_here * wide,
    )
    packed = packed.reshape(blk_count, pairs // blk_count, wide)
    got = lax.all_to_all(packed, "blk", split_axis=0, concat_axis=0, tiled=True)
    [tile_map] = call(
        map_kernel,
        [f32(MAPH, columns)],
        [got.reshape(pairs, wide), ordered],
        (),
        2 * pairs * 4 * columns * (columns + MAPH),
    )
    return tile_map.reshape(1, 1, MAPH, columns)


def solution(mesh):
    in_specs = (
        P("blk", "map", None, None),
        P("blk"),
        P("blk", None, None),
        P("blk", "map", None, None),
        P("blk", "map", None),
        P(),
    )
    out_specs = P("blk", "map", None, None)

    def run(*args):
        map_count, pulse_count, width = args[0].shape[1:]
        ranges = jnp.asarray(range_tables(width // 2))
        crosses = cross_tables(map_count, map_count * args[3].shape[2], pulse_count)
        first = np.zeros((len(crosses[0]), width + crosses[0].shape[1], width), crosses[0].dtype)
        first[:, :width, : width // 2] = range_tables(width // 2)
        first[:, width : , : crosses[0].shape[2]] = crosses[0]
        crosses = [jnp.asarray(table) for table in (first, *crosses[1:])]
        held = lambda *here: body(ranges, crosses, *here)
        return jax.shard_map(
            held, mesh=mesh, in_specs=in_specs, out_specs=out_specs, check_vma=False
        )(*args)

    return run
```

```python
import functools
import math

import jax
import jax.numpy as jnp
import ml_dtypes
import numpy as np
from jax import lax
from jax.experimental import pallas as pl
from jax.experimental.pallas import tpu as pltpu
from jax.sharding import PartitionSpec as P

STOPS = 8
MAPH = 256
SIDE = 128
GROUPS = (2, 2, 4)


def matching(count, distance, parity):
    seen, pairs = set(), []
    for start in range(count):
        cycle, at = [], start
        while at not in seen:
            seen.add(at)
            cycle.append(at)
            at = (at + distance) % count
        for place in range(parity, len(cycle) + parity, 2) if cycle else ():
            a, b = cycle[place % len(cycle)], cycle[(place + 1) % len(cycle)]
            pairs += [(a, b), (b, a)]
    return pairs


def range_tables(freq_count):
    index = np.arange(freq_count, dtype=np.int64)
    angle = (index[: freq_count // 2, None] * index[None, :] % freq_count).astype(
        np.float32
    ) * np.float32(2.0 * math.pi / freq_count)
    factor = np.float32(1.0 / math.sqrt(freq_count))
    real_part, imag_part = np.cos(angle) * factor, -np.sin(angle) * factor
    tables = [
        np.block([[real_part[:, p::2], imag_part[:, p::2]], [-imag_part[:, p::2], real_part[:, p::2]]])
        for p in (0, 1)
    ]
    return np.concatenate(tables).astype(ml_dtypes.bfloat16)


def stop_order(core):
    return [3, 4 - 2 * core, 1, 5, 2 - 2 * core, 6 - 2 * core, 6 * core, 7]


def cross_tables(map_count, row_count, pulse_count):
    span = STOPS * map_count * pulse_count
    rows = np.arange(row_count, dtype=np.int64)[:, None]
    factor = np.float32(1.0 / math.sqrt(span))
    tables, first = [], 0
    for size in GROUPS:
        table = []
        for m in range(map_count):
            for core in range(2):
                parts = []
                for k in stop_order(core)[first : first + size]:
                    along = (k * map_count + m) * pulse_count + np.arange(pulse_count)
                    angle = (rows * along[None, :] % span).astype(np.float32) * np.float32(
                        2.0 * math.pi / span
                    )
                    parts += [np.cos(angle) * factor, -np.sin(angle) * factor]
                table.append(np.concatenate(parts, axis=1))
        tables.append(np.stack(table).astype(ml_dtypes.bfloat16))
        first += size
    return tables


def call(kernel, outs, operands, scratch=(), flops=0, limit=24, far=()):
    specs = [
        pl.BlockSpec(memory_space=pltpu.HBM if n in far else pltpu.VMEM)
        for n in range(len(operands))
    ]
    size = sum(math.prod(a.shape) * a.dtype.itemsize for a in [*operands, *outs]) if flops else 0
    return pl.pallas_call(
        kernel,
        out_shape=outs,
        in_specs=specs,
        out_specs=[pl.BlockSpec(memory_space=pltpu.VMEM) for _ in outs],
        scratch_shapes=list(scratch),
        compiler_params=pltpu.CompilerParams(vmem_limit_bytes=limit * 2**20),
        cost_estimate=pl.CostEstimate(flops=flops, bytes_accessed=size, transcendentals=0),
    )(*operands)


def whereabouts():
    here, here_map = lax.axis_index("blk"), lax.axis_index("map")
    core = here % 2
    return core, here // 2 % 2, here // 4 % 2, here_map, here_map * 2 + core


def phase_factors(map_count, span, curvature, curves):
    _, pulses, freqs = curves[0].shape
    width = freqs // 4
    core, _, _, here_map, _ = whereabouts()
    outs = [
        (curves[2 * g], curves[2 * g + 1], p) for g, size in enumerate(GROUPS) for p in range(size)
    ]
    pulse = lax.broadcasted_iota(jnp.int32, (pulses, width), 0)
    fine = lax.broadcasted_iota(jnp.int32, (pulses, width), 1).astype(jnp.float32) / freqs
    pulse_on_lanes = lax.broadcasted_iota(jnp.int32, (STOPS, pulses), 1)
    stop_on_rows = lax.broadcasted_iota(jnp.int32, (STOPS, pulses), 0)

    def bend(stop, index):
        along = ((stop * map_count + here_map) * pulses + index).astype(jnp.float32) / span - 0.5
        return curvature[0] * (along * along)

    quarter = bend(stop_on_rows, pulse_on_lanes) * 0.25
    step = jnp.concatenate([jnp.cos(quarter), jnp.sin(quarter)] * (pulses // STOPS // 2), axis=0)
    turned = step.T
    stops = stop_order(core)
    for place in range(STOPS):
        cosines, sines, row = outs[place]
        options = sorted({stop_order(0)[place], stop_order(1)[place]})
        step_c, step_s = (
            turned[:, options[-1] + part : options[-1] + part + 1] for part in (0, STOPS)
        )
        if len(options) == 2:
            is_last = stops[place] == options[-1]
            step_c = jnp.where(is_last, step_c, turned[:, options[0] : options[0] + 1])
            step_s = jnp.where(
                is_last, step_s, turned[:, options[0] + STOPS : options[0] + STOPS + 1]
            )
        step_c = jnp.broadcast_to(step_c, (pulses, width))
        step_s = jnp.broadcast_to(step_s, (pulses, width))
        angle = bend(stops[place], pulse) * fine
        low_c, low_s = jnp.cos(angle), jnp.sin(angle)
        now_c = step_c * low_c - step_s * low_s
        now_s = step_s * low_c + step_c * low_s
        for h in range(4):
            now_c, now_s = step_c * now_c - step_s * now_s, step_s * now_c + step_c * now_s
            cosines[row, :, h * width : (h + 1) * width] = now_c
            sines[row, :, h * width : (h + 1) * width] = now_s


def transform(blocks, cosines, sines, ranges, phased, right_side):
    freqs = cosines.shape[2]
    pulses = cosines.shape[1]
    half = freqs // 2
    for place, block in enumerate(blocks):
        values = block().astype(jnp.float32)
        real_part, imag_part = values[:, :freqs], values[:, freqs:]
        cosine, sine = cosines[place], sines[place]
        rows = slice(place * pulses, (place + 1) * pulses)
        turned = (real_part * cosine - imag_part * sine, real_part * sine + imag_part * cosine)
        for n, part in enumerate(turned):
            columns = slice(n * half, (n + 1) * half)
            low, high = part[:, :half], part[:, half:]
            phased[0, rows, columns] = (low + high).astype(jnp.bfloat16)
            phased[1, rows, columns] = (low - high).astype(jnp.bfloat16)
    for parity in range(2):
        spectrum = jnp.dot(
            phased[parity],
            ranges[parity * freqs : (parity + 1) * freqs],
            preferred_element_type=jnp.float32,
        ).astype(jnp.bfloat16)
        first = slice(parity * half, (parity + 1) * half)
        second = slice(freqs + parity * half, freqs + (parity + 1) * half)
        for place in range(len(blocks)):
            piece = spectrum[place * pulses : (place + 1) * pulses]
            real_part, imag_part = piece[:, :half], piece[:, half:]
            top = slice(2 * place * pulses, (2 * place + 1) * pulses)
            below = slice((2 * place + 1) * pulses, (2 * place + 2) * pulses)
            right_side[top, first] = real_part
            right_side[top, second] = imag_part
            right_side[below, first] = -imag_part
            right_side[below, second] = real_part


def fetch(tables, cross, arrival):
    copy = pltpu.make_async_copy(tables.at[whereabouts()[4]], cross, arrival)
    copy.start()
    return copy


def first_kernel(
    map_count, span, curvature, own_far, twin, tables, total, *rest
):
    later = 2 * len(GROUPS) - 2
    cosines, sines, phased, right_side, cross, own, ranges, arrival, own_here, ranges_here = rest[
        later:
    ]
    index = whereabouts()[4]
    copies = [
        pltpu.make_async_copy(own_far, own, own_here),
        pltpu.make_async_copy(
            tables.at[index, : ranges.shape[0], : ranges.shape[1]], ranges, ranges_here
        ),
        pltpu.make_async_copy(
            tables.at[index, ranges.shape[0] :, : cross.shape[1]], cross, arrival
        ),
    ]
    for copy in copies:
        copy.start()
    phase_factors(map_count, span, curvature, (cosines, sines, *rest[:later]))
    for copy in copies:
        copy.wait()
    transform([lambda: own[...], lambda: twin[...]], cosines, sines, ranges, phased, right_side)
    total[...] = jnp.dot(cross[...], right_side[...], preferred_element_type=jnp.float32)


def second_kernel(
    near_a, near_b, cosines, sines, ranges, tables, before, total,
    phased, right_side, cross, arrival,
):
    copy = fetch(tables, cross, arrival)
    chip_odd = whereabouts()[1] == 1
    blocks = [
        lambda: jnp.where(chip_odd, near_a[...], near_b[...]),
        lambda: jnp.where(chip_odd, near_b[...], near_a[...]),
    ]
    transform(blocks, cosines, sines, ranges, phased, right_side)
    copy.wait()
    total[...] = before[...] + jnp.dot(
        cross[...], right_side[...], preferred_element_type=jnp.float32
    )


def part_rows(ref, part):
    rows = ref.shape[0] // 2
    return ref[pl.ds(pl.multiple_of(part * rows, rows), rows), :]


def last_kernel(
    twin_near_a, twin_near_b, far_a, far_b, twin_far_a, twin_far_b,
    cosines, sines, ranges, tables, before, sent, right_side, phased, cross, arrival,
):
    copy = fetch(tables, cross, arrival)
    core, chip, group, here_map, _ = whereabouts()
    chip_odd, group_odd, from_a = chip == 1, group == 1, core != group
    blocks = [
        lambda: jnp.where(chip_odd, twin_near_a[...], twin_near_b[...]),
        lambda: jnp.where(chip_odd, twin_near_b[...], twin_near_a[...]),
        lambda: jnp.where(from_a, twin_far_a[...], twin_far_b[...]),
        lambda: jnp.where(group_odd, far_b[...], far_a[...]),
    ]
    transform(blocks, cosines, sines, ranges, phased, right_side)
    copy.wait()
    other = 1 - here_map
    sent[...] = (
        part_rows(before, other)
        + jnp.dot(
            part_rows(cross, other), right_side[...], preferred_element_type=jnp.float32
        )
    ).astype(sent.dtype)


def kept_kernel(right_side, tables, before, kept, cross, arrival):
    copy = fetch(tables, cross, arrival)
    copy.wait()
    here_map = whereabouts()[3]
    kept[...] = part_rows(before, here_map) + jnp.dot(
        part_rows(cross, here_map), right_side[...], preferred_element_type=jnp.float32
    )


def slot_kernel(tiles, offsets, owner, weights, slot_hot, marks, ordered):
    columns = weights.shape[0]
    place = lax.broadcasted_iota(jnp.int32, weights.shape, 0)
    source = jnp.where(place < columns // 2, 2 * place, 2 * place - columns + 1)
    order = source == lax.broadcasted_iota(jnp.int32, weights.shape, 1)
    ordered[...] = jnp.dot(
        order.astype(jnp.float32).astype(jnp.bfloat16),
        weights[...],
        preferred_element_type=jnp.float32,
    ).astype(jnp.bfloat16)
    count, rows = owner.shape[1], tiles.shape[1]
    _, pairs, _ = slot_hot.shape
    capacity = 2 * pairs // count
    tile_hot = (lax.broadcasted_iota(jnp.int32, (count, rows), 0) == tiles[...]).astype(
        jnp.bfloat16
    )
    owners = jnp.broadcast_to(owner[...].astype(jnp.float32), (8, count)).astype(jnp.bfloat16)
    holder = jnp.dot(owners, tile_hot, preferred_element_type=jnp.float32)[0:1]
    same = lax.dot_general(
        tile_hot, tile_hot, (((0,), (0,)), ((), ())), preferred_element_type=jnp.float32
    )
    earlier = lax.broadcasted_iota(jnp.int32, (rows, rows), 0) < lax.broadcasted_iota(
        jnp.int32, (rows, rows), 1
    )
    rank = jnp.sum(jnp.where(earlier, same, 0.0), axis=0, keepdims=True)
    slot = (holder * capacity + rank).astype(jnp.int32)
    numbers = 2 * lax.broadcasted_iota(jnp.int32, (pairs, rows), 0)
    half = marks.shape[1] // 2
    for part in range(2):
        hot = numbers + part == slot
        slot_hot[part] = hot.astype(jnp.float32).astype(jnp.bfloat16)
        mark = jnp.sum(
            jnp.where(hot, offsets[...].astype(jnp.float32), 0.0), axis=1, keepdims=True
        )
        spread = jnp.broadcast_to(mark, (pairs, half))
        sides = [spread, jnp.zeros_like(spread)]
        both = jnp.concatenate(sides if part == 0 else sides[::-1], axis=1)
        total = both if part == 0 else total + both
    marks[...] = total.astype(jnp.bfloat16)


def pack_kernel(kept, arrived, slot_hot, marks, packed):
    width = kept.shape[1]
    count, group, _ = packed.shape
    image = (kept[...] + arrived[...].astype(jnp.float32)).astype(jnp.bfloat16)
    for part in range(2):
        packed[:, :, part * width : (part + 1) * width] = (
            jnp.dot(slot_hot[part], image, preferred_element_type=jnp.float32)
            .astype(packed.dtype)
            .reshape(count, group, width)
        )
    packed[:, :, 2 * width :] = marks[...].reshape(count, group, marks.shape[1])


def map_kernel(got, weights, out):
    columns = weights.shape[0]
    pairs = got.shape[0] * got.shape[1]
    flat = got[...].reshape(pairs, got.shape[2])
    parts = [flat[:, n * columns : (n + 1) * columns] for n in range(4)]
    mapped = jnp.dot(
        jnp.concatenate(parts, axis=0), weights[...], preferred_element_type=jnp.float32
    )
    squared = mapped * mapped
    marks = flat[:, 4 * columns :].astype(jnp.float32).T
    spots = lax.broadcasted_iota(jnp.int32, (MAPH, pairs), 0)
    hots, pieces = [], []
    for part in range(2):
        real_out = squared[2 * part * pairs : (2 * part + 1) * pairs]
        power = real_out + squared[(2 * part + 1) * pairs : (2 * part + 2) * pairs]
        mark = marks[part * (SIDE // 2) : part * (SIDE // 2) + 1].astype(jnp.int32)
        hot = (mark == spots).astype(jnp.float32).astype(jnp.bfloat16)
        high = power.astype(jnp.bfloat16)
        low = (power - high.astype(jnp.float32)).astype(jnp.bfloat16)
        hots += [hot, hot]
        pieces += [low, high]
    out[...] = jnp.dot(
        jnp.concatenate(hots, axis=1),
        jnp.concatenate(pieces, axis=0),
        preferred_element_type=jnp.float32,
    )


def swap(block, count):
    return lax.ppermute(block, "blk", [(i, i ^ 1) for i in range(count)])


def body(ranges, crosses, phase_history, tile_curvature, interp_weights, strip_tiles, row_offsets, tile_owner):
    blk_count = lax.axis_size("blk")
    map_count = lax.axis_size("map")
    own_block = phase_history[0, 0]
    pulse_count = own_block.shape[0]
    freq_count = own_block.shape[1] // 2
    columns = interp_weights.shape[2]
    rows_here = strip_tiles.shape[2]

    near = [lax.ppermute(own_block, "blk", matching(blk_count, 2, p)) for p in (0, 1)]
    far = [lax.ppermute(own_block, "blk", matching(blk_count, 4, p)) for p in (0, 1)]
    twin = swap(own_block, blk_count)

    f32 = lambda *shape: jax.ShapeDtypeStruct(shape, jnp.float32)
    b16 = lambda *shape: jax.ShapeDtypeStruct(shape, jnp.bfloat16)
    deep = 2 * pulse_count
    image_shape = (map_count * rows_here, 2 * columns)
    half_shape = (rows_here, 2 * columns)
    right = lambda n: pltpu.VMEM((n * deep, 2 * columns), jnp.bfloat16)
    spread = lambda n: pltpu.VMEM((2, n * pulse_count, freq_count), jnp.bfloat16)
    table = lambda n: [
        pltpu.VMEM((map_count * rows_here, n * deep), jnp.bfloat16),
        pltpu.SemaphoreType.DMA,
    ]
    flops = lambda n: 2 * n * pulse_count * 4 * columns * (freq_count + map_count * rows_here)
    n = GROUPS[0]
    smem, vmem, hbm = (
        pl.BlockSpec(memory_space=kind) for kind in (pltpu.SMEM, pltpu.VMEM, pltpu.HBM)
    )
    total, *curves = pl.pallas_call(
        functools.partial(first_kernel, map_count, STOPS * map_count * pulse_count),
        out_shape=[f32(*image_shape)]
        + [f32(size, pulse_count, freq_count) for size in GROUPS[1:] for _ in range(2)],
        in_specs=[smem, hbm, vmem, hbm],
        out_specs=[vmem] * (2 * len(GROUPS) - 1),
        scratch_shapes=[pltpu.VMEM((n, pulse_count, freq_count), jnp.float32)] * 2
        + [
            spread(n),
            right(n),
            table(n)[0],
            pltpu.VMEM(own_block.shape, jnp.bfloat16),
            pltpu.VMEM(ranges.shape, jnp.bfloat16),
        ]
        + [pltpu.SemaphoreType.DMA] * 3,
        compiler_params=pltpu.CompilerParams(vmem_limit_bytes=44 * 2**20),
        cost_estimate=pl.CostEstimate(flops=flops(n), bytes_accessed=0, transcendentals=2**18),
    )(tile_curvature, own_block, twin, crosses[0])
    far, near, total = lax.optimization_barrier((far, near, total))
    twin_near = [swap(block, blk_count) for block in near]
    twin_far = [swap(block, blk_count) for block in far]
    n = GROUPS[1]
    [total] = call(
        second_kernel,
        [f32(*image_shape)],
        [*near, *curves[:2], ranges, crosses[1], total],
        [spread(n), right(n), *table(n)],
        flops(n),
        far=(5,),
    )
    twin_near, twin_far, total = lax.optimization_barrier((twin_near, twin_far, total))
    n = GROUPS[2]
    sent, right_side = call(
        last_kernel,
        [b16(*half_shape), b16(n * deep, 2 * columns)],
        [*twin_near, *far, *twin_far, *curves[2:], ranges, crosses[2], total],
        [spread(n), *table(n)],
        flops(n),
        far=(9,),
    )
    sent, right_side, strip_tiles, row_offsets, interp_weights = lax.optimization_barrier(
        (sent, right_side, strip_tiles, row_offsets, interp_weights)
    )
    arrived = lax.ppermute(sent, "map", [(0, 1), (1, 0)])
    pairs = max(2, 2 * rows_here // blk_count) * blk_count // 2
    slot_hot, marks, ordered = call(
        slot_kernel,
        [b16(2, pairs, rows_here), b16(pairs, SIDE), b16(columns, columns)],
        [
            strip_tiles.reshape(1, rows_here),
            row_offsets.reshape(1, rows_here),
            tile_owner.reshape(1, blk_count),
            interp_weights[0],
        ],
    )
    [kept] = call(
        kept_kernel,
        [f32(*half_shape)],
        [right_side, crosses[2], total],
        table(n),
        far=(1,),
    )

    wide = 4 * columns + SIDE
    [packed] = call(
        pack_kernel,
        [b16(blk_count, pairs // blk_count, wide)],
        [kept, arrived, slot_hot, marks],
        (),
        2 * pairs * rows_here * wide,
    )
    got = lax.all_to_all(packed, "blk", split_axis=0, concat_axis=0, tiled=True)
    [tile_map] = call(
        map_kernel,
        [f32(MAPH, columns)],
        [got, ordered],
        (),
        2 * pairs * 4 * columns * (columns + MAPH),
    )
    return tile_map.reshape(1, 1, MAPH, columns)


def solution(mesh):
    in_specs = (
        P("blk", "map", None, None),
        P("blk"),
        P("blk", None, None),
        P("blk", "map", None, None),
        P("blk", "map", None),
        P(),
    )
    out_specs = P("blk", "map", None, None)

    def run(*args):
        map_count, pulse_count, width = args[0].shape[1:]
        ranges = jnp.asarray(range_tables(width // 2))
        crosses = cross_tables(map_count, map_count * args[3].shape[2], pulse_count)
        first = np.zeros((len(crosses[0]), width + crosses[0].shape[1], width), crosses[0].dtype)
        first[:, :width, : width // 2] = range_tables(width // 2)
        first[:, width : , : crosses[0].shape[2]] = crosses[0]
        crosses = [jnp.asarray(table) for table in (first, *crosses[1:])]
        held = lambda *here: body(ranges, crosses, *here)
        return jax.shard_map(
            held, mesh=mesh, in_specs=in_specs, out_specs=out_specs, check_vma=False
        )(*args)

    return run
```

```python
import functools
import math

import jax
import jax.numpy as jnp
import ml_dtypes
import numpy as np
from jax import lax
from jax.experimental import pallas as pl
from jax.experimental.pallas import tpu as pltpu
from jax.sharding import PartitionSpec as P

STOPS = 8
MAPH = 256
SIDE = 128
GROUPS = (2, 2, 4)


def matching(count, distance, parity):
    seen, pairs = set(), []
    for start in range(count):
        cycle, at = [], start
        while at not in seen:
            seen.add(at)
            cycle.append(at)
            at = (at + distance) % count
        for place in range(parity, len(cycle) + parity, 2) if cycle else ():
            a, b = cycle[place % len(cycle)], cycle[(place + 1) % len(cycle)]
            pairs += [(a, b), (b, a)]
    return pairs


def range_tables(freq_count):
    index = np.arange(freq_count, dtype=np.int64)
    angle = (index[: freq_count // 2, None] * index[None, :] % freq_count).astype(
        np.float32
    ) * np.float32(2.0 * math.pi / freq_count)
    factor = np.float32(1.0 / math.sqrt(freq_count))
    real_part, imag_part = np.cos(angle) * factor, -np.sin(angle) * factor
    tables = [
        np.block([[real_part[:, p::2], imag_part[:, p::2]], [-imag_part[:, p::2], real_part[:, p::2]]])
        for p in (0, 1)
    ]
    return np.concatenate(tables).astype(ml_dtypes.bfloat16)


def stop_order(core):
    return [3, 4 - 2 * core, 1, 5, 2 - 2 * core, 6 - 2 * core, 6 * core, 7]


def cross_tables(map_count, row_count, pulse_count):
    span = STOPS * map_count * pulse_count
    rows = np.arange(row_count, dtype=np.int64)[:, None]
    factor = np.float32(1.0 / math.sqrt(span))
    tables, first = [], 0
    for size in GROUPS:
        table = []
        for m in range(map_count):
            for core in range(2):
                parts = []
                for k in stop_order(core)[first : first + size]:
                    along = (k * map_count + m) * pulse_count + np.arange(pulse_count)
                    angle = (rows * along[None, :] % span).astype(np.float32) * np.float32(
                        2.0 * math.pi / span
                    )
                    parts += [np.cos(angle) * factor, -np.sin(angle) * factor]
                table.append(np.concatenate(parts, axis=1))
        tables.append(np.stack(table).astype(ml_dtypes.bfloat16))
        first += size
    return tables


def call(kernel, outs, operands, scratch=(), flops=0, limit=24, far=()):
    specs = [
        pl.BlockSpec(memory_space=pltpu.HBM if n in far else pltpu.VMEM)
        for n in range(len(operands))
    ]
    size = sum(math.prod(a.shape) * a.dtype.itemsize for a in [*operands, *outs]) if flops else 0
    return pl.pallas_call(
        kernel,
        out_shape=outs,
        in_specs=specs,
        out_specs=[pl.BlockSpec(memory_space=pltpu.VMEM) for _ in outs],
        scratch_shapes=list(scratch),
        compiler_params=pltpu.CompilerParams(vmem_limit_bytes=limit * 2**20),
        cost_estimate=pl.CostEstimate(flops=flops, bytes_accessed=size, transcendentals=0),
    )(*operands)


def whereabouts():
    here, here_map = lax.axis_index("blk"), lax.axis_index("map")
    core = here % 2
    return core, here // 2 % 2, here // 4 % 2, here_map, here_map * 2 + core


def phase_factors(map_count, span, curvature, curves):
    _, pulses, freqs = curves[0].shape
    width = freqs // 4
    core, _, _, here_map, _ = whereabouts()
    outs = [
        (curves[2 * g], curves[2 * g + 1], p) for g, size in enumerate(GROUPS) for p in range(size)
    ]
    pulse = lax.broadcasted_iota(jnp.int32, (pulses, width), 0)
    fine = lax.broadcasted_iota(jnp.int32, (pulses, width), 1).astype(jnp.float32) / freqs
    pulse_on_lanes = lax.broadcasted_iota(jnp.int32, (STOPS, pulses), 1)
    stop_on_rows = lax.broadcasted_iota(jnp.int32, (STOPS, pulses), 0)

    def bend(stop, index):
        along = ((stop * map_count + here_map) * pulses + index).astype(jnp.float32) / span - 0.5
        return curvature[0] * (along * along)

    quarter = bend(stop_on_rows, pulse_on_lanes) * 0.25
    step = jnp.concatenate([jnp.cos(quarter), jnp.sin(quarter)] * (pulses // STOPS // 2), axis=0)
    turned = step.T
    stops = stop_order(core)
    for place in range(STOPS):
        cosines, sines, row = outs[place]
        options = sorted({stop_order(0)[place], stop_order(1)[place]})
        step_c, step_s = (
            turned[:, options[-1] + part : options[-1] + part + 1] for part in (0, STOPS)
        )
        if len(options) == 2:
            is_last = stops[place] == options[-1]
            step_c = jnp.where(is_last, step_c, turned[:, options[0] : options[0] + 1])
            step_s = jnp.where(
                is_last, step_s, turned[:, options[0] + STOPS : options[0] + STOPS + 1]
            )
        step_c = jnp.broadcast_to(step_c, (pulses, width))
        step_s = jnp.broadcast_to(step_s, (pulses, width))
        angle = bend(stops[place], pulse) * fine
        low_c, low_s = jnp.cos(angle), jnp.sin(angle)
        now_c = step_c * low_c - step_s * low_s
        now_s = step_s * low_c + step_c * low_s
        for h in range(4):
            now_c, now_s = step_c * now_c - step_s * now_s, step_s * now_c + step_c * now_s
            cosines[row, :, h * width : (h + 1) * width] = now_c
            sines[row, :, h * width : (h + 1) * width] = now_s


def transform(blocks, cosines, sines, ranges, phased, right_side):
    freqs = cosines.shape[2]
    pulses = cosines.shape[1]
    half = freqs // 2
    for place, block in enumerate(blocks):
        values = block().astype(jnp.float32)
        real_part, imag_part = values[:, :freqs], values[:, freqs:]
        cosine, sine = cosines[place], sines[place]
        rows = slice(place * pulses, (place + 1) * pulses)
        turned = (real_part * cosine - imag_part * sine, real_part * sine + imag_part * cosine)
        for n, part in enumerate(turned):
            columns = slice(n * half, (n + 1) * half)
            low, high = part[:, :half], part[:, half:]
            phased[0, rows, columns] = (low + high).astype(jnp.bfloat16)
            phased[1, rows, columns] = (low - high).astype(jnp.bfloat16)
    for parity in range(2):
        spectrum = jnp.dot(
            phased[parity],
            ranges[parity * freqs : (parity + 1) * freqs],
            preferred_element_type=jnp.float32,
        ).astype(jnp.bfloat16)
        first = slice(parity * half, (parity + 1) * half)
        second = slice(freqs + parity * half, freqs + (parity + 1) * half)
        for place in range(len(blocks)):
            piece = spectrum[place * pulses : (place + 1) * pulses]
            real_part, imag_part = piece[:, :half], piece[:, half:]
            top = slice(2 * place * pulses, (2 * place + 1) * pulses)
            below = slice((2 * place + 1) * pulses, (2 * place + 2) * pulses)
            right_side[top, first] = real_part
            right_side[top, second] = imag_part
            right_side[below, first] = -imag_part
            right_side[below, second] = real_part


def first_kernel(map_count, span, curvature, own_far, twin, tables, total, *rest):
    later = 2 * len(GROUPS) - 2
    ranges, second, last, cosines, sines, phased, right_side, cross, own, arrivals = rest[later:]
    index = whereabouts()[4]
    depth, side = ranges.shape
    rows = cross.shape[0]
    left, right = slice(0, side), slice(side, 2 * side)
    moves = [
        (own_far, own),
        (tables.at[index, :depth, left], ranges),
        (tables.at[index, depth : depth + rows, left], cross),
        (tables.at[index, depth : depth + rows, right], second),
        (tables.at[index, :rows, right], last.at[:, left]),
        (tables.at[index, rows : 2 * rows, right], last.at[:, right]),
    ]
    copies = [
        pltpu.make_async_copy(source, target, arrivals.at[n])
        for n, (source, target) in enumerate(moves)
    ]
    for copy in copies:
        copy.start()
    phase_factors(map_count, span, curvature, (cosines, sines, *rest[:later]))
    for copy in copies:
        copy.wait()
    transform([lambda: own[...], lambda: twin[...]], cosines, sines, ranges, phased, right_side)
    total[...] = jnp.dot(cross[...], right_side[...], preferred_element_type=jnp.float32)


def second_kernel(
    near_a, near_b, cosines, sines, ranges, cross, before, total, phased, right_side
):
    chip_odd = whereabouts()[1] == 1
    blocks = [
        lambda: jnp.where(chip_odd, near_a[...], near_b[...]),
        lambda: jnp.where(chip_odd, near_b[...], near_a[...]),
    ]
    transform(blocks, cosines, sines, ranges, phased, right_side)
    total[...] = before[...] + jnp.dot(
        cross[...], right_side[...], preferred_element_type=jnp.float32
    )


def part_rows(ref, part):
    rows = ref.shape[0] // 2
    return ref[pl.ds(pl.multiple_of(part * rows, rows), rows), :]


def last_kernel(
    twin_near_a, twin_near_b, far_a, far_b, twin_far_a, twin_far_b,
    cosines, sines, ranges, cross, before, sent, right_side, phased,
):
    core, chip, group, here_map, _ = whereabouts()
    chip_odd, group_odd, from_a = chip == 1, group == 1, core != group
    blocks = [
        lambda: jnp.where(chip_odd, twin_near_a[...], twin_near_b[...]),
        lambda: jnp.where(chip_odd, twin_near_b[...], twin_near_a[...]),
        lambda: jnp.where(from_a, twin_far_a[...], twin_far_b[...]),
        lambda: jnp.where(group_odd, far_b[...], far_a[...]),
    ]
    transform(blocks, cosines, sines, ranges, phased, right_side)
    other = 1 - here_map
    sent[...] = (
        part_rows(before, other)
        + jnp.dot(
            part_rows(cross, other), right_side[...], preferred_element_type=jnp.float32
        )
    ).astype(sent.dtype)


def kept_kernel(right_side, cross, before, kept):
    here_map = whereabouts()[3]
    kept[...] = part_rows(before, here_map) + jnp.dot(
        part_rows(cross, here_map), right_side[...], preferred_element_type=jnp.float32
    )


def slot_kernel(tiles, offsets, owner, weights, slot_hot, marks, ordered):
    columns = weights.shape[0]
    place = lax.broadcasted_iota(jnp.int32, weights.shape, 0)
    source = jnp.where(place < columns // 2, 2 * place, 2 * place - columns + 1)
    order = source == lax.broadcasted_iota(jnp.int32, weights.shape, 1)
    ordered[...] = jnp.dot(
        order.astype(jnp.float32).astype(jnp.bfloat16),
        weights[...],
        preferred_element_type=jnp.float32,
    ).astype(jnp.bfloat16)
    count, rows = owner.shape[1], tiles.shape[1]
    _, pairs, _ = slot_hot.shape
    capacity = 2 * pairs // count
    tile_hot = (lax.broadcasted_iota(jnp.int32, (count, rows), 0) == tiles[...]).astype(
        jnp.bfloat16
    )
    owners = jnp.broadcast_to(owner[...].astype(jnp.float32), (8, count)).astype(jnp.bfloat16)
    holder = jnp.dot(owners, tile_hot, preferred_element_type=jnp.float32)[0:1]
    same = lax.dot_general(
        tile_hot, tile_hot, (((0,), (0,)), ((), ())), preferred_element_type=jnp.float32
    )
    earlier = lax.broadcasted_iota(jnp.int32, (rows, rows), 0) < lax.broadcasted_iota(
        jnp.int32, (rows, rows), 1
    )
    rank = jnp.sum(jnp.where(earlier, same, 0.0), axis=0, keepdims=True)
    slot = (holder * capacity + rank).astype(jnp.int32)
    numbers = 2 * lax.broadcasted_iota(jnp.int32, (pairs, rows), 0)
    half = marks.shape[1] // 2
    for part in range(2):
        hot = numbers + part == slot
        slot_hot[part] = hot.astype(jnp.float32).astype(jnp.bfloat16)
        mark = jnp.sum(
            jnp.where(hot, offsets[...].astype(jnp.float32), 0.0), axis=1, keepdims=True
        )
        spread = jnp.broadcast_to(mark, (pairs, half))
        sides = [spread, jnp.zeros_like(spread)]
        both = jnp.concatenate(sides if part == 0 else sides[::-1], axis=1)
        total = both if part == 0 else total + both
    marks[...] = total.astype(jnp.bfloat16)


def pack_kernel(kept, arrived, slot_hot, marks, packed):
    width = kept.shape[1]
    count, group, _ = packed.shape
    image = (kept[...] + arrived[...].astype(jnp.float32)).astype(jnp.bfloat16)
    for part in range(2):
        packed[:, :, part * width : (part + 1) * width] = (
            jnp.dot(slot_hot[part], image, preferred_element_type=jnp.float32)
            .astype(packed.dtype)
            .reshape(count, group, width)
        )
    packed[:, :, 2 * width :] = marks[...].reshape(count, group, marks.shape[1])


def map_kernel(got, weights, out):
    columns = weights.shape[0]
    pairs = got.shape[0] * got.shape[1]
    flat = got[...].reshape(pairs, got.shape[2])
    parts = [flat[:, n * columns : (n + 1) * columns] for n in range(4)]
    mapped = jnp.dot(
        jnp.concatenate(parts, axis=0), weights[...], preferred_element_type=jnp.float32
    )
    squared = mapped * mapped
    marks = flat[:, 4 * columns :].astype(jnp.float32).T
    spots = lax.broadcasted_iota(jnp.int32, (MAPH, pairs), 0)
    hots, pieces = [], []
    for part in range(2):
        real_out = squared[2 * part * pairs : (2 * part + 1) * pairs]
        power = real_out + squared[(2 * part + 1) * pairs : (2 * part + 2) * pairs]
        mark = marks[part * (SIDE // 2) : part * (SIDE // 2) + 1].astype(jnp.int32)
        hot = (mark == spots).astype(jnp.float32).astype(jnp.bfloat16)
        high = power.astype(jnp.bfloat16)
        low = (power - high.astype(jnp.float32)).astype(jnp.bfloat16)
        hots += [hot, hot]
        pieces += [low, high]
    out[...] = jnp.dot(
        jnp.concatenate(hots, axis=1),
        jnp.concatenate(pieces, axis=0),
        preferred_element_type=jnp.float32,
    )


def swap(block, count):
    return lax.ppermute(block, "blk", [(i, i ^ 1) for i in range(count)])


def body(tables, phase_history, tile_curvature, interp_weights, strip_tiles, row_offsets, tile_owner):
    blk_count = lax.axis_size("blk")
    map_count = lax.axis_size("map")
    own_block = phase_history[0, 0]
    pulse_count = own_block.shape[0]
    freq_count = own_block.shape[1] // 2
    columns = interp_weights.shape[2]
    rows_here = strip_tiles.shape[2]

    near = [lax.ppermute(own_block, "blk", matching(blk_count, 2, p)) for p in (0, 1)]
    far = [lax.ppermute(own_block, "blk", matching(blk_count, 4, p)) for p in (0, 1)]
    twin = swap(own_block, blk_count)

    f32 = lambda *shape: jax.ShapeDtypeStruct(shape, jnp.float32)
    b16 = lambda *shape: jax.ShapeDtypeStruct(shape, jnp.bfloat16)
    deep = 2 * pulse_count
    image_shape = (map_count * rows_here, 2 * columns)
    half_shape = (rows_here, 2 * columns)
    right = lambda n: pltpu.VMEM((n * deep, 2 * columns), jnp.bfloat16)
    spread = lambda n: pltpu.VMEM((2, n * pulse_count, freq_count), jnp.bfloat16)
    cross = lambda n: (map_count * rows_here, n * deep)
    flops = lambda n: 2 * n * pulse_count * 4 * columns * (freq_count + map_count * rows_here)
    n = GROUPS[0]
    smem, vmem, hbm = (
        pl.BlockSpec(memory_space=kind) for kind in (pltpu.SMEM, pltpu.VMEM, pltpu.HBM)
    )
    outs = [
        f32(*image_shape),
        *(f32(size, pulse_count, freq_count) for size in GROUPS[1:] for _ in range(2)),
        b16(2 * freq_count, freq_count),
        b16(*cross(GROUPS[1])),
        b16(*cross(GROUPS[2])),
    ]
    total, *curves, ranges, second_cross, last_cross = pl.pallas_call(
        functools.partial(first_kernel, map_count, STOPS * map_count * pulse_count),
        out_shape=outs,
        in_specs=[smem, hbm, vmem, hbm],
        out_specs=[vmem] * len(outs),
        scratch_shapes=[pltpu.VMEM((n, pulse_count, freq_count), jnp.float32)] * 2
        + [
            spread(n),
            right(n),
            pltpu.VMEM(cross(n), jnp.bfloat16),
            pltpu.VMEM(own_block.shape, jnp.bfloat16),
            pltpu.SemaphoreType.DMA((6,)),
        ],
        compiler_params=pltpu.CompilerParams(vmem_limit_bytes=44 * 2**20),
        cost_estimate=pl.CostEstimate(flops=flops(n), bytes_accessed=0, transcendentals=2**18),
    )(tile_curvature, own_block, twin, tables)
    *others, total = lax.optimization_barrier((far[1], far[0], near[1], near[0], total))
    far, near = others[1::-1], others[:1:-1]
    twin_near = [swap(block, blk_count) for block in near]
    twin_far = [swap(block, blk_count) for block in far]
    n = GROUPS[1]
    [total] = call(
        second_kernel,
        [f32(*image_shape)],
        [*near, *curves[:2], ranges, second_cross, total],
        [spread(n), right(n)],
        flops(n),
    )
    twin_near, twin_far, total = lax.optimization_barrier((twin_near, twin_far, total))
    n = GROUPS[2]
    sent, right_side = call(
        last_kernel,
        [b16(*half_shape), b16(n * deep, 2 * columns)],
        [*twin_near, *far, *twin_far, *curves[2:], ranges, last_cross, total],
        [spread(n)],
        flops(n),
    )
    sent, right_side, strip_tiles, row_offsets, interp_weights = lax.optimization_barrier(
        (sent, right_side, strip_tiles, row_offsets, interp_weights)
    )
    arrived = lax.ppermute(sent, "map", [(0, 1), (1, 0)])
    pairs = max(2, 2 * rows_here // blk_count) * blk_count // 2
    slot_hot, marks, ordered = call(
        slot_kernel,
        [b16(2, pairs, rows_here), b16(pairs, SIDE), b16(columns, columns)],
        [
            strip_tiles.reshape(1, rows_here),
            row_offsets.reshape(1, rows_here),
            tile_owner.reshape(1, blk_count),
            interp_weights[0],
        ],
    )
    [kept] = call(kept_kernel, [f32(*half_shape)], [right_side, last_cross, total])

    wide = 4 * columns + SIDE
    [packed] = call(
        pack_kernel,
        [b16(blk_count, pairs // blk_count, wide)],
        [kept, arrived, slot_hot, marks],
        (),
        2 * pairs * rows_here * wide,
    )
    got = lax.all_to_all(packed, "blk", split_axis=0, concat_axis=0, tiled=True)
    [tile_map] = call(
        map_kernel,
        [f32(MAPH, columns)],
        [got, ordered],
        (),
        2 * pairs * 4 * columns * (columns + MAPH),
    )
    return tile_map.reshape(1, 1, MAPH, columns)


def solution(mesh):
    in_specs = (
        P("blk", "map", None, None),
        P("blk"),
        P("blk", None, None),
        P("blk", "map", None, None),
        P("blk", "map", None),
        P(),
    )
    out_specs = P("blk", "map", None, None)

    def run(*args):
        map_count, pulse_count, width = args[0].shape[1:]
        side = width // 2
        first, second, last = cross_tables(map_count, map_count * args[3].shape[2], pulse_count)
        rows = first.shape[1]
        tables = np.zeros((len(first), width + rows, width), first.dtype)
        tables[:, :width, :side] = range_tables(side)
        tables[:, width:, :side] = first
        tables[:, width:, side:] = second
        tables[:, :rows, side:] = last[:, :, :side]
        tables[:, rows : 2 * rows, side:] = last[:, :, side:]
        tables = jnp.asarray(tables)
        held = lambda *here: body(tables, *here)
        return jax.shard_map(
            held, mesh=mesh, in_specs=in_specs, out_specs=out_specs, check_vma=False
        )(*args)

    return run
```

```python
import functools
import math

import jax
import jax.numpy as jnp
import ml_dtypes
import numpy as np
from jax import lax
from jax.experimental import pallas as pl
from jax.experimental.pallas import tpu as pltpu
from jax.sharding import PartitionSpec as P

STOPS = 8
MAPH = 256
SIDE = 128
GROUPS = (2, 2, 4)


def matching(count, distance, parity):
    seen, pairs = set(), []
    for start in range(count):
        cycle, at = [], start
        while at not in seen:
            seen.add(at)
            cycle.append(at)
            at = (at + distance) % count
        for place in range(parity, len(cycle) + parity, 2) if cycle else ():
            a, b = cycle[place % len(cycle)], cycle[(place + 1) % len(cycle)]
            pairs += [(a, b), (b, a)]
    return pairs


def range_tables(freq_count):
    index = np.arange(freq_count, dtype=np.int64)
    angle = (index[: freq_count // 2, None] * index[None, :] % freq_count).astype(
        np.float32
    ) * np.float32(2.0 * math.pi / freq_count)
    factor = np.float32(1.0 / math.sqrt(freq_count))
    real_part, imag_part = np.cos(angle) * factor, -np.sin(angle) * factor
    tables = [
        np.block([[real_part[:, p::2], imag_part[:, p::2]], [-imag_part[:, p::2], real_part[:, p::2]]])
        for p in (0, 1)
    ]
    return np.concatenate(tables).astype(ml_dtypes.bfloat16)


def stop_order(core):
    return [3, 4 - 2 * core, 1, 5, 2 - 2 * core, 6 - 2 * core, 6 * core, 7]


def cross_tables(map_count, row_count, pulse_count):
    span = STOPS * map_count * pulse_count
    rows = np.arange(row_count, dtype=np.int64)[:, None]
    factor = np.float32(1.0 / math.sqrt(span))
    tables, first = [], 0
    for size in GROUPS:
        table = []
        for m in range(map_count):
            for core in range(2):
                parts = []
                for k in stop_order(core)[first : first + size]:
                    along = (k * map_count + m) * pulse_count + np.arange(pulse_count)
                    angle = (rows * along[None, :] % span).astype(np.float32) * np.float32(
                        2.0 * math.pi / span
                    )
                    parts += [np.cos(angle) * factor, -np.sin(angle) * factor]
                table.append(np.concatenate(parts, axis=1))
        tables.append(np.stack(table).astype(ml_dtypes.bfloat16))
        first += size
    return tables


def call(kernel, outs, operands, scratch=(), flops=0, limit=24, far=()):
    specs = [
        pl.BlockSpec(memory_space=pltpu.HBM if n in far else pltpu.VMEM)
        for n in range(len(operands))
    ]
    size = sum(math.prod(a.shape) * a.dtype.itemsize for a in [*operands, *outs]) if flops else 0
    return pl.pallas_call(
        kernel,
        out_shape=outs,
        in_specs=specs,
        out_specs=[pl.BlockSpec(memory_space=pltpu.VMEM) for _ in outs],
        scratch_shapes=list(scratch),
        compiler_params=pltpu.CompilerParams(vmem_limit_bytes=limit * 2**20),
        cost_estimate=pl.CostEstimate(flops=flops, bytes_accessed=size, transcendentals=0),
    )(*operands)


def whereabouts():
    here, here_map = lax.axis_index("blk"), lax.axis_index("map")
    core = here % 2
    return core, here // 2 % 2, here // 4 % 2, here_map, here_map * 2 + core


def phase_factors(map_count, span, curvature, curves):
    _, pulses, freqs = curves[0].shape
    width = freqs // 4
    core, _, _, here_map, _ = whereabouts()
    outs = [
        (curves[2 * g], curves[2 * g + 1], p) for g, size in enumerate(GROUPS) for p in range(size)
    ]
    pulse = lax.broadcasted_iota(jnp.int32, (pulses, width), 0)
    fine = lax.broadcasted_iota(jnp.int32, (pulses, width), 1).astype(jnp.float32) / freqs
    pulse_on_lanes = lax.broadcasted_iota(jnp.int32, (STOPS, pulses), 1)
    stop_on_rows = lax.broadcasted_iota(jnp.int32, (STOPS, pulses), 0)

    def bend(stop, index):
        along = ((stop * map_count + here_map) * pulses + index).astype(jnp.float32) / span - 0.5
        return curvature[0] * (along * along)

    quarter = bend(stop_on_rows, pulse_on_lanes) * 0.25
    step = jnp.concatenate([jnp.cos(quarter), jnp.sin(quarter)] * (pulses // STOPS // 2), axis=0)
    turned = step.T
    stops = stop_order(core)
    for place in range(STOPS):
        cosines, sines, row = outs[place]
        options = sorted({stop_order(0)[place], stop_order(1)[place]})
        step_c, step_s = (
            turned[:, options[-1] + part : options[-1] + part + 1] for part in (0, STOPS)
        )
        if len(options) == 2:
            is_last = stops[place] == options[-1]
            step_c = jnp.where(is_last, step_c, turned[:, options[0] : options[0] + 1])
            step_s = jnp.where(
                is_last, step_s, turned[:, options[0] + STOPS : options[0] + STOPS + 1]
            )
        step_c = jnp.broadcast_to(step_c, (pulses, width))
        step_s = jnp.broadcast_to(step_s, (pulses, width))
        angle = bend(stops[place], pulse) * fine
        low_c, low_s = jnp.cos(angle), jnp.sin(angle)
        now_c = step_c * low_c - step_s * low_s
        now_s = step_s * low_c + step_c * low_s
        for h in range(4):
            now_c, now_s = step_c * now_c - step_s * now_s, step_s * now_c + step_c * now_s
            cosines[row, :, h * width : (h + 1) * width] = now_c
            sines[row, :, h * width : (h + 1) * width] = now_s


def transform(blocks, cosines, sines, ranges, phased, right_side):
    freqs = cosines.shape[2]
    pulses = cosines.shape[1]
    half = freqs // 2
    for place, block in enumerate(blocks):
        values = block().astype(jnp.float32)
        real_part, imag_part = values[:, :freqs], values[:, freqs:]
        cosine, sine = cosines[place], sines[place]
        rows = slice(place * pulses, (place + 1) * pulses)
        turned = (real_part * cosine - imag_part * sine, real_part * sine + imag_part * cosine)
        for n, part in enumerate(turned):
            columns = slice(n * half, (n + 1) * half)
            low, high = part[:, :half], part[:, half:]
            phased[0, rows, columns] = (low + high).astype(jnp.bfloat16)
            phased[1, rows, columns] = (low - high).astype(jnp.bfloat16)
    for parity in range(2):
        spectrum = jnp.dot(
            phased[parity],
            ranges[parity * freqs : (parity + 1) * freqs],
            preferred_element_type=jnp.float32,
        ).astype(jnp.bfloat16)
        first = slice(parity * half, (parity + 1) * half)
        second = slice(freqs + parity * half, freqs + (parity + 1) * half)
        for place in range(len(blocks)):
            piece = spectrum[place * pulses : (place + 1) * pulses]
            real_part, imag_part = piece[:, :half], piece[:, half:]
            top = slice(2 * place * pulses, (2 * place + 1) * pulses)
            below = slice((2 * place + 1) * pulses, (2 * place + 2) * pulses)
            right_side[top, first] = real_part
            right_side[top, second] = imag_part
            right_side[below, first] = -imag_part
            right_side[below, second] = real_part


def first_kernel(map_count, span, curvature, own_far, twin, tables, total, *rest):
    later = 2 * len(GROUPS) - 2
    ranges, second, last, cosines, sines, phased, right_side, cross, own, arrivals = rest[later:]
    index = whereabouts()[4]
    depth, side = ranges.shape
    rows = cross.shape[0]
    left, right = slice(0, side), slice(side, 2 * side)
    moves = [
        (own_far, own),
        (tables.at[index, :depth, left], ranges),
        (tables.at[index, depth : depth + rows, left], cross),
        (tables.at[index, depth : depth + rows, right], second),
        (tables.at[index, :rows, right], last.at[:, left]),
        (tables.at[index, rows : 2 * rows, right], last.at[:, right]),
    ]
    copies = [
        pltpu.make_async_copy(source, target, arrivals.at[n])
        for n, (source, target) in enumerate(moves)
    ]
    for copy in copies:
        copy.start()
    phase_factors(map_count, span, curvature, (cosines, sines, *rest[:later]))
    for copy in copies[:3]:
        copy.wait()
    transform([lambda: own[...], lambda: twin[...]], cosines, sines, ranges, phased, right_side)
    total[...] = jnp.dot(cross[...], right_side[...], preferred_element_type=jnp.float32)
    for copy in copies[3:]:
        copy.wait()


def second_kernel(
    near_a, near_b, cosines, sines, ranges, cross, before, total, phased, right_side
):
    chip_odd = whereabouts()[1] == 1
    blocks = [
        lambda: jnp.where(chip_odd, near_a[...], near_b[...]),
        lambda: jnp.where(chip_odd, near_b[...], near_a[...]),
    ]
    transform(blocks, cosines, sines, ranges, phased, right_side)
    total[...] = before[...] + jnp.dot(
        cross[...], right_side[...], preferred_element_type=jnp.float32
    )


def part_rows(ref, part):
    rows = ref.shape[0] // 2
    return ref[pl.ds(pl.multiple_of(part * rows, rows), rows), :]


def last_kernel(
    twin_near_a, twin_near_b, far_a, far_b, twin_far_a, twin_far_b,
    cosines, sines, ranges, cross, before, sent, right_side, phased,
):
    core, chip, group, here_map, _ = whereabouts()
    chip_odd, group_odd, from_a = chip == 1, group == 1, core != group
    blocks = [
        lambda: jnp.where(chip_odd, twin_near_a[...], twin_near_b[...]),
        lambda: jnp.where(chip_odd, twin_near_b[...], twin_near_a[...]),
        lambda: jnp.where(from_a, twin_far_a[...], twin_far_b[...]),
        lambda: jnp.where(group_odd, far_b[...], far_a[...]),
    ]
    transform(blocks, cosines, sines, ranges, phased, right_side)
    other = 1 - here_map
    sent[...] = (
        part_rows(before, other)
        + jnp.dot(
            part_rows(cross, other), right_side[...], preferred_element_type=jnp.float32
        )
    ).astype(sent.dtype)


def kept_kernel(right_side, cross, before, kept):
    here_map = whereabouts()[3]
    kept[...] = part_rows(before, here_map) + jnp.dot(
        part_rows(cross, here_map), right_side[...], preferred_element_type=jnp.float32
    )


def slot_kernel(tiles, offsets, owner, weights, slot_hot, marks, ordered):
    columns = weights.shape[0]
    place = lax.broadcasted_iota(jnp.int32, weights.shape, 0)
    source = jnp.where(place < columns // 2, 2 * place, 2 * place - columns + 1)
    order = source == lax.broadcasted_iota(jnp.int32, weights.shape, 1)
    ordered[...] = jnp.dot(
        order.astype(jnp.float32).astype(jnp.bfloat16),
        weights[...],
        preferred_element_type=jnp.float32,
    ).astype(jnp.bfloat16)
    count, rows = owner.shape[1], tiles.shape[1]
    _, pairs, _ = slot_hot.shape
    capacity = 2 * pairs // count
    tile_hot = (lax.broadcasted_iota(jnp.int32, (count, rows), 0) == tiles[...]).astype(
        jnp.bfloat16
    )
    owners = jnp.broadcast_to(owner[...].astype(jnp.float32), (8, count)).astype(jnp.bfloat16)
    holder = jnp.dot(owners, tile_hot, preferred_element_type=jnp.float32)[0:1]
    same = lax.dot_general(
        tile_hot, tile_hot, (((0,), (0,)), ((), ())), preferred_element_type=jnp.float32
    )
    earlier = lax.broadcasted_iota(jnp.int32, (rows, rows), 0) < lax.broadcasted_iota(
        jnp.int32, (rows, rows), 1
    )
    rank = jnp.sum(jnp.where(earlier, same, 0.0), axis=0, keepdims=True)
    slot = (holder * capacity + rank).astype(jnp.int32)
    numbers = 2 * lax.broadcasted_iota(jnp.int32, (pairs, rows), 0)
    half = marks.shape[1] // 2
    for part in range(2):
        hot = numbers + part == slot
        slot_hot[part] = hot.astype(jnp.float32).astype(jnp.bfloat16)
        mark = jnp.sum(
            jnp.where(hot, offsets[...].astype(jnp.float32), 0.0), axis=1, keepdims=True
        )
        spread = jnp.broadcast_to(mark, (pairs, half))
        sides = [spread, jnp.zeros_like(spread)]
        both = jnp.concatenate(sides if part == 0 else sides[::-1], axis=1)
        total = both if part == 0 else total + both
    marks[...] = total.astype(jnp.bfloat16)


def pack_kernel(kept, arrived, slot_hot, marks, packed):
    width = kept.shape[1]
    count, group, _ = packed.shape
    image = (kept[...] + arrived[...].astype(jnp.float32)).astype(jnp.bfloat16)
    for part in range(2):
        packed[:, :, part * width : (part + 1) * width] = (
            jnp.dot(slot_hot[part], image, preferred_element_type=jnp.float32)
            .astype(packed.dtype)
            .reshape(count, group, width)
        )
    packed[:, :, 2 * width :] = marks[...].reshape(count, group, marks.shape[1])


def map_kernel(got, weights, out):
    columns = weights.shape[0]
    pairs = got.shape[0] * got.shape[1]
    flat = got[...].reshape(pairs, got.shape[2])
    parts = [flat[:, n * columns : (n + 1) * columns] for n in range(4)]
    mapped = jnp.dot(
        jnp.concatenate(parts, axis=0), weights[...], preferred_element_type=jnp.float32
    )
    squared = mapped * mapped
    marks = flat[:, 4 * columns :].astype(jnp.float32).T
    spots = lax.broadcasted_iota(jnp.int32, (MAPH, pairs), 0)
    hots, pieces = [], []
    for part in range(2):
        real_out = squared[2 * part * pairs : (2 * part + 1) * pairs]
        power = real_out + squared[(2 * part + 1) * pairs : (2 * part + 2) * pairs]
        mark = marks[part * (SIDE // 2) : part * (SIDE // 2) + 1].astype(jnp.int32)
        hot = (mark == spots).astype(jnp.float32).astype(jnp.bfloat16)
        high = power.astype(jnp.bfloat16)
        low = (power - high.astype(jnp.float32)).astype(jnp.bfloat16)
        hots += [hot, hot]
        pieces += [low, high]
    out[...] = jnp.dot(
        jnp.concatenate(hots, axis=1),
        jnp.concatenate(pieces, axis=0),
        preferred_element_type=jnp.float32,
    )


def swap(block, count):
    return lax.ppermute(block, "blk", [(i, i ^ 1) for i in range(count)])


def body(tables, phase_history, tile_curvature, interp_weights, strip_tiles, row_offsets, tile_owner):
    blk_count = lax.axis_size("blk")
    map_count = lax.axis_size("map")
    own_block = phase_history[0, 0]
    pulse_count = own_block.shape[0]
    freq_count = own_block.shape[1] // 2
    columns = interp_weights.shape[2]
    rows_here = strip_tiles.shape[2]

    near = [lax.ppermute(own_block, "blk", matching(blk_count, 2, p)) for p in (0, 1)]
    far = [lax.ppermute(own_block, "blk", matching(blk_count, 4, p)) for p in (0, 1)]
    twin = swap(own_block, blk_count)

    f32 = lambda *shape: jax.ShapeDtypeStruct(shape, jnp.float32)
    b16 = lambda *shape: jax.ShapeDtypeStruct(shape, jnp.bfloat16)
    deep = 2 * pulse_count
    image_shape = (map_count * rows_here, 2 * columns)
    half_shape = (rows_here, 2 * columns)
    right = lambda n: pltpu.VMEM((n * deep, 2 * columns), jnp.bfloat16)
    spread = lambda n: pltpu.VMEM((2, n * pulse_count, freq_count), jnp.bfloat16)
    cross = lambda n: (map_count * rows_here, n * deep)
    flops = lambda n: 2 * n * pulse_count * 4 * columns * (freq_count + map_count * rows_here)
    n = GROUPS[0]
    smem, vmem, hbm = (
        pl.BlockSpec(memory_space=kind) for kind in (pltpu.SMEM, pltpu.VMEM, pltpu.HBM)
    )
    outs = [
        f32(*image_shape),
        *(f32(size, pulse_count, freq_count) for size in GROUPS[1:] for _ in range(2)),
        b16(2 * freq_count, freq_count),
        b16(*cross(GROUPS[1])),
        b16(*cross(GROUPS[2])),
    ]
    total, *curves, ranges, second_cross, last_cross = pl.pallas_call(
        functools.partial(first_kernel, map_count, STOPS * map_count * pulse_count),
        out_shape=outs,
        in_specs=[smem, hbm, vmem, hbm],
        out_specs=[vmem] * len(outs),
        scratch_shapes=[pltpu.VMEM((n, pulse_count, freq_count), jnp.float32)] * 2
        + [
            spread(n),
            right(n),
            pltpu.VMEM(cross(n), jnp.bfloat16),
            pltpu.VMEM(own_block.shape, jnp.bfloat16),
            pltpu.SemaphoreType.DMA((6,)),
        ],
        compiler_params=pltpu.CompilerParams(vmem_limit_bytes=44 * 2**20),
        cost_estimate=pl.CostEstimate(flops=flops(n), bytes_accessed=0, transcendentals=2**18),
    )(tile_curvature, own_block, twin, tables)
    *others, total = lax.optimization_barrier((far[0], far[1], near[0], near[1], total))
    far, near = [others[0], others[1]], [others[2], others[3]]
    twin_near = [swap(block, blk_count) for block in near]
    twin_far = [swap(block, blk_count) for block in far]
    n = GROUPS[1]
    [total] = call(
        second_kernel,
        [f32(*image_shape)],
        [*near, *curves[:2], ranges, second_cross, total],
        [spread(n), right(n)],
        flops(n),
    )
    twin_near, twin_far, total = lax.optimization_barrier((twin_near, twin_far, total))
    n = GROUPS[2]
    sent, right_side = call(
        last_kernel,
        [b16(*half_shape), b16(n * deep, 2 * columns)],
        [*twin_near, *far, *twin_far, *curves[2:], ranges, last_cross, total],
        [spread(n)],
        flops(n),
    )
    sent, right_side, strip_tiles, row_offsets, interp_weights = lax.optimization_barrier(
        (sent, right_side, strip_tiles, row_offsets, interp_weights)
    )
    arrived = lax.ppermute(sent, "map", [(0, 1), (1, 0)])
    pairs = max(2, 2 * rows_here // blk_count) * blk_count // 2
    slot_hot, marks, ordered = call(
        slot_kernel,
        [b16(2, pairs, rows_here), b16(pairs, SIDE), b16(columns, columns)],
        [
            strip_tiles.reshape(1, rows_here),
            row_offsets.reshape(1, rows_here),
            tile_owner.reshape(1, blk_count),
            interp_weights[0],
        ],
    )
    [kept] = call(kept_kernel, [f32(*half_shape)], [right_side, last_cross, total])

    wide = 4 * columns + SIDE
    [packed] = call(
        pack_kernel,
        [b16(blk_count, pairs // blk_count, wide)],
        [kept, arrived, slot_hot, marks],
        (),
        2 * pairs * rows_here * wide,
    )
    got = lax.all_to_all(packed, "blk", split_axis=0, concat_axis=0, tiled=True)
    [tile_map] = call(
        map_kernel,
        [f32(MAPH, columns)],
        [got, ordered],
        (),
        2 * pairs * 4 * columns * (columns + MAPH),
    )
    return tile_map.reshape(1, 1, MAPH, columns)


def solution(mesh):
    in_specs = (
        P("blk", "map", None, None),
        P("blk"),
        P("blk", None, None),
        P("blk", "map", None, None),
        P("blk", "map", None),
        P(),
    )
    out_specs = P("blk", "map", None, None)

    def run(*args):
        map_count, pulse_count, width = args[0].shape[1:]
        side = width // 2
        first, second, last = cross_tables(map_count, map_count * args[3].shape[2], pulse_count)
        rows = first.shape[1]
        tables = np.zeros((len(first), width + rows, width), first.dtype)
        tables[:, :width, :side] = range_tables(side)
        tables[:, width:, :side] = first
        tables[:, width:, side:] = second
        tables[:, :rows, side:] = last[:, :, :side]
        tables[:, rows : 2 * rows, side:] = last[:, :, side:]
        tables = jnp.asarray(tables)
        held = lambda *here: body(tables, *here)
        return jax.shard_map(
            held, mesh=mesh, in_specs=in_specs, out_specs=out_specs, check_vma=False
        )(*args)

    return run
```

```python
import functools
import math

import jax
import jax.numpy as jnp
import ml_dtypes
import numpy as np
from jax import lax
from jax.experimental import pallas as pl
from jax.experimental.pallas import tpu as pltpu
from jax.sharding import PartitionSpec as P

STOPS = 8
MAPH = 256
SIDE = 128
GROUPS = (2, 2, 4)


def matching(count, distance, parity):
    seen, pairs = set(), []
    for start in range(count):
        cycle, at = [], start
        while at not in seen:
            seen.add(at)
            cycle.append(at)
            at = (at + distance) % count
        for place in range(parity, len(cycle) + parity, 2) if cycle else ():
            a, b = cycle[place % len(cycle)], cycle[(place + 1) % len(cycle)]
            pairs += [(a, b), (b, a)]
    return pairs


def range_tables(freq_count):
    index = np.arange(freq_count, dtype=np.int64)
    angle = (index[: freq_count // 2, None] * index[None, :] % freq_count).astype(
        np.float32
    ) * np.float32(2.0 * math.pi / freq_count)
    factor = np.float32(1.0 / math.sqrt(freq_count))
    real_part, imag_part = np.cos(angle) * factor, -np.sin(angle) * factor
    tables = [
        np.block([[real_part[:, p::2], imag_part[:, p::2]], [-imag_part[:, p::2], real_part[:, p::2]]])
        for p in (0, 1)
    ]
    return np.concatenate(tables).astype(ml_dtypes.bfloat16)


def stop_order(core):
    return [3, 4 - 2 * core, 1, 5, 2 - 2 * core, 6 - 2 * core, 6 * core, 7]


def cross_tables(map_count, row_count, pulse_count):
    span = STOPS * map_count * pulse_count
    rows = np.arange(row_count, dtype=np.int64)[:, None]
    factor = np.float32(1.0 / math.sqrt(span))
    tables, first = [], 0
    for size in GROUPS:
        table = []
        for m in range(map_count):
            for core in range(2):
                parts = []
                for k in stop_order(core)[first : first + size]:
                    along = (k * map_count + m) * pulse_count + np.arange(pulse_count)
                    angle = (rows * along[None, :] % span).astype(np.float32) * np.float32(
                        2.0 * math.pi / span
                    )
                    parts += [np.cos(angle) * factor, -np.sin(angle) * factor]
                table.append(np.concatenate(parts, axis=1))
        tables.append(np.stack(table).astype(ml_dtypes.bfloat16))
        first += size
    return tables


def call(kernel, outs, operands, scratch=(), flops=0, limit=24, far=()):
    specs = [
        pl.BlockSpec(memory_space=pltpu.HBM if n in far else pltpu.VMEM)
        for n in range(len(operands))
    ]
    size = sum(math.prod(a.shape) * a.dtype.itemsize for a in [*operands, *outs]) if flops else 0
    return pl.pallas_call(
        kernel,
        out_shape=outs,
        in_specs=specs,
        out_specs=[pl.BlockSpec(memory_space=pltpu.VMEM) for _ in outs],
        scratch_shapes=list(scratch),
        compiler_params=pltpu.CompilerParams(vmem_limit_bytes=limit * 2**20),
        cost_estimate=pl.CostEstimate(flops=flops, bytes_accessed=size, transcendentals=0),
    )(*operands)


def whereabouts():
    here, here_map = lax.axis_index("blk"), lax.axis_index("map")
    core = here % 2
    return core, here // 2 % 2, here // 4 % 2, here_map, here_map * 2 + core


def phase_factors(map_count, span, curvature, curves):
    _, pulses, freqs = curves[0].shape
    width = freqs // 4
    core, _, _, here_map, _ = whereabouts()
    outs = [
        (curves[2 * g], curves[2 * g + 1], p) for g, size in enumerate(GROUPS) for p in range(size)
    ]
    pulse = lax.broadcasted_iota(jnp.int32, (pulses, width), 0)
    fine = lax.broadcasted_iota(jnp.int32, (pulses, width), 1).astype(jnp.float32) / freqs
    pulse_on_lanes = lax.broadcasted_iota(jnp.int32, (STOPS, pulses), 1)
    stop_on_rows = lax.broadcasted_iota(jnp.int32, (STOPS, pulses), 0)

    def bend(stop, index):
        along = ((stop * map_count + here_map) * pulses + index).astype(jnp.float32) / span - 0.5
        return curvature[0] * (along * along)

    quarter = bend(stop_on_rows, pulse_on_lanes) * 0.25
    step = jnp.concatenate([jnp.cos(quarter), jnp.sin(quarter)] * (pulses // STOPS // 2), axis=0)
    turned = step.T
    stops = stop_order(core)
    for place in range(STOPS):
        cosines, sines, row = outs[place]
        options = sorted({stop_order(0)[place], stop_order(1)[place]})
        step_c, step_s = (
            turned[:, options[-1] + part : options[-1] + part + 1] for part in (0, STOPS)
        )
        if len(options) == 2:
            is_last = stops[place] == options[-1]
            step_c = jnp.where(is_last, step_c, turned[:, options[0] : options[0] + 1])
            step_s = jnp.where(
                is_last, step_s, turned[:, options[0] + STOPS : options[0] + STOPS + 1]
            )
        step_c = jnp.broadcast_to(step_c, (pulses, width))
        step_s = jnp.broadcast_to(step_s, (pulses, width))
        angle = bend(stops[place], pulse) * fine
        low_c, low_s = jnp.cos(angle), jnp.sin(angle)
        now_c = step_c * low_c - step_s * low_s
        now_s = step_s * low_c + step_c * low_s
        for h in range(4):
            now_c, now_s = step_c * now_c - step_s * now_s, step_s * now_c + step_c * now_s
            cosines[row, :, h * width : (h + 1) * width] = now_c
            sines[row, :, h * width : (h + 1) * width] = now_s


def transform(blocks, cosines, sines, ranges, phased, right_side):
    freqs = cosines.shape[2]
    pulses = cosines.shape[1]
    half = freqs // 2
    for place, block in enumerate(blocks):
        values = block().astype(jnp.float32)
        real_part, imag_part = values[:, :freqs], values[:, freqs:]
        cosine, sine = cosines[place], sines[place]
        rows = slice(place * pulses, (place + 1) * pulses)
        turned = (real_part * cosine - imag_part * sine, real_part * sine + imag_part * cosine)
        for n, part in enumerate(turned):
            columns = slice(n * half, (n + 1) * half)
            low, high = part[:, :half], part[:, half:]
            phased[0, rows, columns] = (low + high).astype(jnp.bfloat16)
            phased[1, rows, columns] = (low - high).astype(jnp.bfloat16)
    for parity in range(2):
        spectrum = jnp.dot(
            phased[parity],
            ranges[parity * freqs : (parity + 1) * freqs],
            preferred_element_type=jnp.float32,
        ).astype(jnp.bfloat16)
        first = slice(parity * half, (parity + 1) * half)
        second = slice(freqs + parity * half, freqs + (parity + 1) * half)
        for place in range(len(blocks)):
            piece = spectrum[place * pulses : (place + 1) * pulses]
            real_part, imag_part = piece[:, :half], piece[:, half:]
            top = slice(2 * place * pulses, (2 * place + 1) * pulses)
            below = slice((2 * place + 1) * pulses, (2 * place + 2) * pulses)
            right_side[top, first] = real_part
            right_side[top, second] = imag_part
            right_side[below, first] = -imag_part
            right_side[below, second] = real_part


def first_kernel(map_count, span, curvature, own_far, twin, tables, total, *rest):
    later = 2 * len(GROUPS) - 2
    ranges, second, last, cosines, sines, phased, right_side, cross, own, arrivals = rest[later:]
    index = whereabouts()[4]
    depth, side = ranges.shape
    rows = cross.shape[0]
    left, right = slice(0, side), slice(side, 2 * side)
    moves = [
        (own_far, own),
        (tables.at[index, :depth, left], ranges),
        (tables.at[index, depth : depth + rows, left], cross),
        (tables.at[index, depth : depth + rows, right], second),
        (tables.at[index, :rows, right], last.at[:, left]),
        (tables.at[index, rows : 2 * rows, right], last.at[:, right]),
    ]
    copies = [
        pltpu.make_async_copy(source, target, arrivals.at[n])
        for n, (source, target) in enumerate(moves)
    ]
    for copy in copies:
        copy.start()
    phase_factors(map_count, span, curvature, (cosines, sines, *rest[:later]))
    for copy in copies[:3]:
        copy.wait()
    transform([lambda: own[...], lambda: twin[...]], cosines, sines, ranges, phased, right_side)
    total[...] = jnp.dot(cross[...], right_side[...], preferred_element_type=jnp.float32)
    for copy in copies[3:]:
        copy.wait()


def second_kernel(
    near_a, near_b, cosines, sines, ranges, cross, before, total, phased, right_side
):
    chip_odd = whereabouts()[1] == 1
    blocks = [
        lambda: jnp.where(chip_odd, near_a[...], near_b[...]),
        lambda: jnp.where(chip_odd, near_b[...], near_a[...]),
    ]
    transform(blocks, cosines, sines, ranges, phased, right_side)
    total[...] = before[...] + jnp.dot(
        cross[...], right_side[...], preferred_element_type=jnp.float32
    )


def part_rows(ref, part):
    rows = ref.shape[0] // 2
    return ref[pl.ds(pl.multiple_of(part * rows, rows), rows), :]


def last_kernel(
    twin_near_a, twin_near_b, far_a, far_b, twin_far_a, twin_far_b,
    cosines, sines, ranges, cross, before, sent, right_side, phased,
):
    core, chip, group, here_map, _ = whereabouts()
    chip_odd, group_odd, from_a = chip == 1, group == 1, core != group
    blocks = [
        lambda: jnp.where(chip_odd, twin_near_a[...], twin_near_b[...]),
        lambda: jnp.where(chip_odd, twin_near_b[...], twin_near_a[...]),
        lambda: jnp.where(from_a, twin_far_a[...], twin_far_b[...]),
        lambda: jnp.where(group_odd, far_b[...], far_a[...]),
    ]
    transform(blocks, cosines, sines, ranges, phased, right_side)
    other = 1 - here_map
    sent[...] = (
        part_rows(before, other)
        + jnp.dot(
            part_rows(cross, other), right_side[...], preferred_element_type=jnp.float32
        )
    ).astype(sent.dtype)


def kept_kernel(right_side, cross, before, kept):
    here_map = whereabouts()[3]
    kept[...] = part_rows(before, here_map) + jnp.dot(
        part_rows(cross, here_map), right_side[...], preferred_element_type=jnp.float32
    )


def slot_kernel(tiles, offsets, owner, weights, slot_hot, marks, ordered):
    columns = weights.shape[0]
    place = lax.broadcasted_iota(jnp.int32, weights.shape, 0)
    source = jnp.where(place < columns // 2, 2 * place, 2 * place - columns + 1)
    order = source == lax.broadcasted_iota(jnp.int32, weights.shape, 1)
    ordered[...] = jnp.dot(
        order.astype(jnp.float32).astype(jnp.bfloat16),
        weights[...],
        preferred_element_type=jnp.float32,
    ).astype(jnp.bfloat16)
    count, rows = owner.shape[1], tiles.shape[1]
    _, pairs, _ = slot_hot.shape
    capacity = 2 * pairs // count
    tile_hot = (lax.broadcasted_iota(jnp.int32, (count, rows), 0) == tiles[...]).astype(
        jnp.bfloat16
    )
    owners = jnp.broadcast_to(owner[...].astype(jnp.float32), (8, count)).astype(jnp.bfloat16)
    holder = jnp.dot(owners, tile_hot, preferred_element_type=jnp.float32)[0:1]
    same = lax.dot_general(
        tile_hot, tile_hot, (((0,), (0,)), ((), ())), preferred_element_type=jnp.float32
    )
    earlier = lax.broadcasted_iota(jnp.int32, (rows, rows), 0) < lax.broadcasted_iota(
        jnp.int32, (rows, rows), 1
    )
    rank = jnp.sum(jnp.where(earlier, same, 0.0), axis=0, keepdims=True)
    slot = (holder * capacity + rank).astype(jnp.int32)
    numbers = 2 * lax.broadcasted_iota(jnp.int32, (pairs, rows), 0)
    half = marks.shape[1] // 2
    for part in range(2):
        hot = numbers + part == slot
        slot_hot[part] = hot.astype(jnp.float32).astype(jnp.bfloat16)
        mark = jnp.sum(
            jnp.where(hot, offsets[...].astype(jnp.float32), 0.0), axis=1, keepdims=True
        )
        spread = jnp.broadcast_to(mark, (pairs, half))
        sides = [spread, jnp.zeros_like(spread)]
        both = jnp.concatenate(sides if part == 0 else sides[::-1], axis=1)
        total = both if part == 0 else total + both
    marks[...] = total.astype(jnp.bfloat16)


def pack_kernel(kept, arrived, slot_hot, marks, packed):
    width = kept.shape[1]
    count, group, _ = packed.shape
    image = (kept[...] + arrived[...].astype(jnp.float32)).astype(jnp.bfloat16)
    for part in range(2):
        packed[:, :, part * width : (part + 1) * width] = (
            jnp.dot(slot_hot[part], image, preferred_element_type=jnp.float32)
            .astype(packed.dtype)
            .reshape(count, group, width)
        )
    packed[:, :, 2 * width :] = marks[...].reshape(count, group, marks.shape[1])


def map_kernel(got, weights, out):
    columns = weights.shape[0]
    pairs = got.shape[0] * got.shape[1]
    flat = got[...].reshape(pairs, got.shape[2])
    parts = [flat[:, n * columns : (n + 1) * columns] for n in range(4)]
    mapped = jnp.dot(
        jnp.concatenate(parts, axis=0), weights[...], preferred_element_type=jnp.float32
    )
    squared = mapped * mapped
    marks = flat[:, 4 * columns :].astype(jnp.float32).T
    spots = lax.broadcasted_iota(jnp.int32, (MAPH, pairs), 0)
    hots, pieces = [], []
    for part in range(2):
        real_out = squared[2 * part * pairs : (2 * part + 1) * pairs]
        power = real_out + squared[(2 * part + 1) * pairs : (2 * part + 2) * pairs]
        mark = marks[part * (SIDE // 2) : part * (SIDE // 2) + 1].astype(jnp.int32)
        hot = (mark == spots).astype(jnp.float32).astype(jnp.bfloat16)
        high = power.astype(jnp.bfloat16)
        low = (power - high.astype(jnp.float32)).astype(jnp.bfloat16)
        hots += [hot, hot]
        pieces += [low, high]
    out[...] = jnp.dot(
        jnp.concatenate(hots, axis=1),
        jnp.concatenate(pieces, axis=0),
        preferred_element_type=jnp.float32,
    )


def swap(block, count):
    return lax.ppermute(block, "blk", [(i, i ^ 1) for i in range(count)])


def body(tables, phase_history, tile_curvature, interp_weights, strip_tiles, row_offsets, tile_owner):
    blk_count = lax.axis_size("blk")
    map_count = lax.axis_size("map")
    own_block = phase_history[0, 0]
    pulse_count = own_block.shape[0]
    freq_count = own_block.shape[1] // 2
    columns = interp_weights.shape[2]
    rows_here = strip_tiles.shape[2]

    near = [lax.ppermute(own_block, "blk", matching(blk_count, 2, p)) for p in (0, 1)]
    far = [lax.ppermute(own_block, "blk", matching(blk_count, 4, p)) for p in (0, 1)]
    twin = swap(own_block, blk_count)

    f32 = lambda *shape: jax.ShapeDtypeStruct(shape, jnp.float32)
    b16 = lambda *shape: jax.ShapeDtypeStruct(shape, jnp.bfloat16)
    deep = 2 * pulse_count
    image_shape = (map_count * rows_here, 2 * columns)
    half_shape = (rows_here, 2 * columns)
    right = lambda n: pltpu.VMEM((n * deep, 2 * columns), jnp.bfloat16)
    spread = lambda n: pltpu.VMEM((2, n * pulse_count, freq_count), jnp.bfloat16)
    cross = lambda n: (map_count * rows_here, n * deep)
    flops = lambda n: 2 * n * pulse_count * 4 * columns * (freq_count + map_count * rows_here)
    n = GROUPS[0]
    smem, vmem, hbm = (
        pl.BlockSpec(memory_space=kind) for kind in (pltpu.SMEM, pltpu.VMEM, pltpu.HBM)
    )
    outs = [
        f32(*image_shape),
        *(f32(size, pulse_count, freq_count) for size in GROUPS[1:] for _ in range(2)),
        b16(2 * freq_count, freq_count),
        b16(*cross(GROUPS[1])),
        b16(*cross(GROUPS[2])),
    ]
    total, *curves, ranges, second_cross, last_cross = pl.pallas_call(
        functools.partial(first_kernel, map_count, STOPS * map_count * pulse_count),
        out_shape=outs,
        in_specs=[smem, hbm, vmem, hbm],
        out_specs=[vmem] * len(outs),
        scratch_shapes=[pltpu.VMEM((n, pulse_count, freq_count), jnp.float32)] * 2
        + [
            spread(n),
            right(n),
            pltpu.VMEM(cross(n), jnp.bfloat16),
            pltpu.VMEM(own_block.shape, jnp.bfloat16),
            pltpu.SemaphoreType.DMA((6,)),
        ],
        compiler_params=pltpu.CompilerParams(vmem_limit_bytes=44 * 2**20),
        cost_estimate=pl.CostEstimate(flops=flops(n), bytes_accessed=0, transcendentals=2**18),
    )(tile_curvature, own_block, twin, tables)
    near[0], near[1], total = lax.optimization_barrier((near[0], near[1], total))
    twin_near = [swap(block, blk_count) for block in near]
    twin_far = [swap(block, blk_count) for block in far]
    n = GROUPS[1]
    [total] = call(
        second_kernel,
        [f32(*image_shape)],
        [*near, *curves[:2], ranges, second_cross, total],
        [spread(n), right(n)],
        flops(n),
    )
    twin_near, twin_far, total = lax.optimization_barrier((twin_near, twin_far, total))
    n = GROUPS[2]
    sent, right_side = call(
        last_kernel,
        [b16(*half_shape), b16(n * deep, 2 * columns)],
        [*twin_near, *far, *twin_far, *curves[2:], ranges, last_cross, total],
        [spread(n)],
        flops(n),
    )
    sent, right_side, strip_tiles, row_offsets, interp_weights = lax.optimization_barrier(
        (sent, right_side, strip_tiles, row_offsets, interp_weights)
    )
    arrived = lax.ppermute(sent, "map", [(0, 1), (1, 0)])
    pairs = max(2, 2 * rows_here // blk_count) * blk_count // 2
    slot_hot, marks, ordered = call(
        slot_kernel,
        [b16(2, pairs, rows_here), b16(pairs, SIDE), b16(columns, columns)],
        [
            strip_tiles.reshape(1, rows_here),
            row_offsets.reshape(1, rows_here),
            tile_owner.reshape(1, blk_count),
            interp_weights[0],
        ],
    )
    [kept] = call(kept_kernel, [f32(*half_shape)], [right_side, last_cross, total])

    wide = 4 * columns + SIDE
    [packed] = call(
        pack_kernel,
        [b16(blk_count, pairs // blk_count, wide)],
        [kept, arrived, slot_hot, marks],
        (),
        2 * pairs * rows_here * wide,
    )
    got = lax.all_to_all(packed, "blk", split_axis=0, concat_axis=0, tiled=True)
    [tile_map] = call(
        map_kernel,
        [f32(MAPH, columns)],
        [got, ordered],
        (),
        2 * pairs * 4 * columns * (columns + MAPH),
    )
    return tile_map.reshape(1, 1, MAPH, columns)


def solution(mesh):
    in_specs = (
        P("blk", "map", None, None),
        P("blk"),
        P("blk", None, None),
        P("blk", "map", None, None),
        P("blk", "map", None),
        P(),
    )
    out_specs = P("blk", "map", None, None)

    def run(*args):
        map_count, pulse_count, width = args[0].shape[1:]
        side = width // 2
        first, second, last = cross_tables(map_count, map_count * args[3].shape[2], pulse_count)
        rows = first.shape[1]
        tables = np.zeros((len(first), width + rows, width), first.dtype)
        tables[:, :width, :side] = range_tables(side)
        tables[:, width:, :side] = first
        tables[:, width:, side:] = second
        tables[:, :rows, side:] = last[:, :, :side]
        tables[:, rows : 2 * rows, side:] = last[:, :, side:]
        tables = jnp.asarray(tables)
        held = lambda *here: body(tables, *here)
        return jax.shard_map(
            held, mesh=mesh, in_specs=in_specs, out_specs=out_specs, check_vma=False
        )(*args)

    return run
```

```python
import functools
import math

import jax
import jax.numpy as jnp
import ml_dtypes
import numpy as np
from jax import lax
from jax.experimental import pallas as pl
from jax.experimental.pallas import tpu as pltpu
from jax.sharding import PartitionSpec as P

STOPS = 8
MAPH = 256
SIDE = 128
GROUPS = (2, 3, 3)


def matching(count, distance, parity):
    seen, pairs = set(), []
    for start in range(count):
        cycle, at = [], start
        while at not in seen:
            seen.add(at)
            cycle.append(at)
            at = (at + distance) % count
        for place in range(parity, len(cycle) + parity, 2) if cycle else ():
            a, b = cycle[place % len(cycle)], cycle[(place + 1) % len(cycle)]
            pairs += [(a, b), (b, a)]
    return pairs


def range_tables(freq_count):
    index = np.arange(freq_count, dtype=np.int64)
    angle = (index[: freq_count // 2, None] * index[None, :] % freq_count).astype(
        np.float32
    ) * np.float32(2.0 * math.pi / freq_count)
    factor = np.float32(1.0 / math.sqrt(freq_count))
    real_part, imag_part = np.cos(angle) * factor, -np.sin(angle) * factor
    tables = [
        np.block([[real_part[:, p::2], imag_part[:, p::2]], [-imag_part[:, p::2], real_part[:, p::2]]])
        for p in (0, 1)
    ]
    return np.concatenate(tables).astype(ml_dtypes.bfloat16)


def stop_order(core):
    return [3, 4 - 2 * core, 1, 5, 7, 2 - 2 * core, 6 - 2 * core, 6 * core]


def cross_tables(map_count, row_count, pulse_count):
    span = STOPS * map_count * pulse_count
    rows = np.arange(row_count, dtype=np.int64)[:, None]
    factor = np.float32(1.0 / math.sqrt(span))
    tables, first = [], 0
    for size in GROUPS:
        table = []
        for m in range(map_count):
            for core in range(2):
                parts = []
                for k in stop_order(core)[first : first + size]:
                    along = (k * map_count + m) * pulse_count + np.arange(pulse_count)
                    angle = (rows * along[None, :] % span).astype(np.float32) * np.float32(
                        2.0 * math.pi / span
                    )
                    parts += [np.cos(angle) * factor, -np.sin(angle) * factor]
                table.append(np.concatenate(parts, axis=1))
        tables.append(np.stack(table).astype(ml_dtypes.bfloat16))
        first += size
    return tables


def call(kernel, outs, operands, scratch=(), flops=0, limit=24, far=()):
    specs = [
        pl.BlockSpec(memory_space=pltpu.HBM if n in far else pltpu.VMEM)
        for n in range(len(operands))
    ]
    size = sum(math.prod(a.shape) * a.dtype.itemsize for a in [*operands, *outs]) if flops else 0
    return pl.pallas_call(
        kernel,
        out_shape=outs,
        in_specs=specs,
        out_specs=[pl.BlockSpec(memory_space=pltpu.VMEM) for _ in outs],
        scratch_shapes=list(scratch),
        compiler_params=pltpu.CompilerParams(vmem_limit_bytes=limit * 2**20),
        cost_estimate=pl.CostEstimate(flops=flops, bytes_accessed=size, transcendentals=0),
    )(*operands)


def whereabouts():
    here, here_map = lax.axis_index("blk"), lax.axis_index("map")
    core = here % 2
    return core, here // 2 % 2, here // 4 % 2, here_map, here_map * 2 + core


def phase_factors(map_count, span, curvature, curves):
    _, pulses, freqs = curves[0].shape
    width = freqs // 4
    core, _, _, here_map, _ = whereabouts()
    outs = [
        (curves[2 * g], curves[2 * g + 1], p) for g, size in enumerate(GROUPS) for p in range(size)
    ]
    pulse = lax.broadcasted_iota(jnp.int32, (pulses, width), 0)
    fine = lax.broadcasted_iota(jnp.int32, (pulses, width), 1).astype(jnp.float32) / freqs
    pulse_on_lanes = lax.broadcasted_iota(jnp.int32, (STOPS, pulses), 1)
    stop_on_rows = lax.broadcasted_iota(jnp.int32, (STOPS, pulses), 0)

    def bend(stop, index):
        along = ((stop * map_count + here_map) * pulses + index).astype(jnp.float32) / span - 0.5
        return curvature[0] * (along * along)

    quarter = bend(stop_on_rows, pulse_on_lanes) * 0.25
    step = jnp.concatenate([jnp.cos(quarter), jnp.sin(quarter)] * (pulses // STOPS // 2), axis=0)
    turned = step.T
    stops = stop_order(core)
    for place in range(STOPS):
        cosines, sines, row = outs[place]
        options = sorted({stop_order(0)[place], stop_order(1)[place]})
        step_c, step_s = (
            turned[:, options[-1] + part : options[-1] + part + 1] for part in (0, STOPS)
        )
        if len(options) == 2:
            is_last = stops[place] == options[-1]
            step_c = jnp.where(is_last, step_c, turned[:, options[0] : options[0] + 1])
            step_s = jnp.where(
                is_last, step_s, turned[:, options[0] + STOPS : options[0] + STOPS + 1]
            )
        step_c = jnp.broadcast_to(step_c, (pulses, width))
        step_s = jnp.broadcast_to(step_s, (pulses, width))
        angle = bend(stops[place], pulse) * fine
        low_c, low_s = jnp.cos(angle), jnp.sin(angle)
        now_c = step_c * low_c - step_s * low_s
        now_s = step_s * low_c + step_c * low_s
        for h in range(4):
            now_c, now_s = step_c * now_c - step_s * now_s, step_s * now_c + step_c * now_s
            cosines[row, :, h * width : (h + 1) * width] = now_c
            sines[row, :, h * width : (h + 1) * width] = now_s


def transform(blocks, cosines, sines, ranges, phased, right_side):
    freqs = cosines.shape[2]
    pulses = cosines.shape[1]
    half = freqs // 2
    for place, block in enumerate(blocks):
        values = block().astype(jnp.float32)
        real_part, imag_part = values[:, :freqs], values[:, freqs:]
        cosine, sine = cosines[place], sines[place]
        rows = slice(place * pulses, (place + 1) * pulses)
        turned = (real_part * cosine - imag_part * sine, real_part * sine + imag_part * cosine)
        for n, part in enumerate(turned):
            columns = slice(n * half, (n + 1) * half)
            low, high = part[:, :half], part[:, half:]
            phased[0, rows, columns] = (low + high).astype(jnp.bfloat16)
            phased[1, rows, columns] = (low - high).astype(jnp.bfloat16)
    for parity in range(2):
        spectrum = jnp.dot(
            phased[parity],
            ranges[parity * freqs : (parity + 1) * freqs],
            preferred_element_type=jnp.float32,
        ).astype(jnp.bfloat16)
        first = slice(parity * half, (parity + 1) * half)
        second = slice(freqs + parity * half, freqs + (parity + 1) * half)
        for place in range(len(blocks)):
            piece = spectrum[place * pulses : (place + 1) * pulses]
            real_part, imag_part = piece[:, :half], piece[:, half:]
            top = slice(2 * place * pulses, (2 * place + 1) * pulses)
            below = slice((2 * place + 1) * pulses, (2 * place + 2) * pulses)
            right_side[top, first] = real_part
            right_side[top, second] = imag_part
            right_side[below, first] = -imag_part
            right_side[below, second] = real_part


def first_kernel(map_count, span, curvature, own_far, twin, tables, total, *rest):
    later = 2 * len(GROUPS) - 2
    ranges, second, last, cosines, sines, phased, right_side, cross, own, arrivals = rest[later:]
    index = whereabouts()[4]
    depth, side = ranges.shape
    rows = cross.shape[0]
    left, right = slice(0, side), slice(side, 2 * side)
    rest_side = side // 2
    moves = [
        (own_far, own),
        (tables.at[index, :depth, left], ranges),
        (tables.at[index, depth : depth + rows, left], cross),
        (tables.at[index, depth : depth + rows, right], second.at[:, left]),
        (tables.at[index, :rows, right], last.at[:, left]),
        (tables.at[index, rows : 2 * rows, side : side + rest_side], second.at[:, side:]),
        (tables.at[index, rows : 2 * rows, side + rest_side :], last.at[:, side:]),
    ]
    copies = [
        pltpu.make_async_copy(source, target, arrivals.at[n])
        for n, (source, target) in enumerate(moves)
    ]
    for copy in copies:
        copy.start()
    phase_factors(map_count, span, curvature, (cosines, sines, *rest[:later]))
    for copy in copies[:3]:
        copy.wait()
    transform([lambda: own[...], lambda: twin[...]], cosines, sines, ranges, phased, right_side)
    total[...] = jnp.dot(cross[...], right_side[...], preferred_element_type=jnp.float32)
    for copy in copies[3:]:
        copy.wait()


def second_kernel(
    near_a, near_b, far_a, far_b, cosines, sines, ranges, cross, before, total, phased, right_side
):
    _, chip, group, _, _ = whereabouts()
    chip_odd, group_odd = chip == 1, group == 1
    blocks = [
        lambda: jnp.where(chip_odd, near_a[...], near_b[...]),
        lambda: jnp.where(chip_odd, near_b[...], near_a[...]),
        lambda: jnp.where(group_odd, far_b[...], far_a[...]),
    ]
    transform(blocks, cosines, sines, ranges, phased, right_side)
    total[...] = before[...] + jnp.dot(
        cross[...], right_side[...], preferred_element_type=jnp.float32
    )


def part_rows(ref, part):
    rows = ref.shape[0] // 2
    return ref[pl.ds(pl.multiple_of(part * rows, rows), rows), :]


def last_kernel(
    twin_near_a, twin_near_b, twin_far_a, twin_far_b,
    cosines, sines, ranges, cross, before, sent, right_side, phased,
):
    core, chip, group, here_map, _ = whereabouts()
    chip_odd, from_a = chip == 1, core != group
    blocks = [
        lambda: jnp.where(chip_odd, twin_near_a[...], twin_near_b[...]),
        lambda: jnp.where(chip_odd, twin_near_b[...], twin_near_a[...]),
        lambda: jnp.where(from_a, twin_far_a[...], twin_far_b[...]),
    ]
    transform(blocks, cosines, sines, ranges, phased, right_side)
    other = 1 - here_map
    sent[...] = (
        part_rows(before, other)
        + jnp.dot(
            part_rows(cross, other), right_side[...], preferred_element_type=jnp.float32
        )
    ).astype(sent.dtype)


def kept_kernel(right_side, cross, before, kept):
    here_map = whereabouts()[3]
    kept[...] = part_rows(before, here_map) + jnp.dot(
        part_rows(cross, here_map), right_side[...], preferred_element_type=jnp.float32
    )


def slot_kernel(tiles, offsets, owner, weights, slot_hot, marks, ordered):
    columns = weights.shape[0]
    place = lax.broadcasted_iota(jnp.int32, weights.shape, 0)
    source = jnp.where(place < columns // 2, 2 * place, 2 * place - columns + 1)
    order = source == lax.broadcasted_iota(jnp.int32, weights.shape, 1)
    ordered[...] = jnp.dot(
        order.astype(jnp.float32).astype(jnp.bfloat16),
        weights[...],
        preferred_element_type=jnp.float32,
    ).astype(jnp.bfloat16)
    count, rows = owner.shape[1], tiles.shape[1]
    _, pairs, _ = slot_hot.shape
    capacity = 2 * pairs // count
    tile_hot = (lax.broadcasted_iota(jnp.int32, (count, rows), 0) == tiles[...]).astype(
        jnp.bfloat16
    )
    owners = jnp.broadcast_to(owner[...].astype(jnp.float32), (8, count)).astype(jnp.bfloat16)
    holder = jnp.dot(owners, tile_hot, preferred_element_type=jnp.float32)[0:1]
    same = lax.dot_general(
        tile_hot, tile_hot, (((0,), (0,)), ((), ())), preferred_element_type=jnp.float32
    )
    earlier = lax.broadcasted_iota(jnp.int32, (rows, rows), 0) < lax.broadcasted_iota(
        jnp.int32, (rows, rows), 1
    )
    rank = jnp.sum(jnp.where(earlier, same, 0.0), axis=0, keepdims=True)
    slot = (holder * capacity + rank).astype(jnp.int32)
    numbers = 2 * lax.broadcasted_iota(jnp.int32, (pairs, rows), 0)
    half = marks.shape[1] // 2
    for part in range(2):
        hot = numbers + part == slot
        slot_hot[part] = hot.astype(jnp.float32).astype(jnp.bfloat16)
        mark = jnp.sum(
            jnp.where(hot, offsets[...].astype(jnp.float32), 0.0), axis=1, keepdims=True
        )
        spread = jnp.broadcast_to(mark, (pairs, half))
        sides = [spread, jnp.zeros_like(spread)]
        both = jnp.concatenate(sides if part == 0 else sides[::-1], axis=1)
        total = both if part == 0 else total + both
    marks[...] = total.astype(jnp.bfloat16)


def pack_kernel(kept, arrived, slot_hot, marks, packed):
    width = kept.shape[1]
    count, group, _ = packed.shape
    image = (kept[...] + arrived[...].astype(jnp.float32)).astype(jnp.bfloat16)
    for part in range(2):
        packed[:, :, part * width : (part + 1) * width] = (
            jnp.dot(slot_hot[part], image, preferred_element_type=jnp.float32)
            .astype(packed.dtype)
            .reshape(count, group, width)
        )
    packed[:, :, 2 * width :] = marks[...].reshape(count, group, marks.shape[1])


def map_kernel(got, weights, out):
    columns = weights.shape[0]
    pairs = got.shape[0] * got.shape[1]
    flat = got[...].reshape(pairs, got.shape[2])
    parts = [flat[:, n * columns : (n + 1) * columns] for n in range(4)]
    mapped = jnp.dot(
        jnp.concatenate(parts, axis=0), weights[...], preferred_element_type=jnp.float32
    )
    squared = mapped * mapped
    marks = flat[:, 4 * columns :].astype(jnp.float32).T
    spots = lax.broadcasted_iota(jnp.int32, (MAPH, pairs), 0)
    hots, pieces = [], []
    for part in range(2):
        real_out = squared[2 * part * pairs : (2 * part + 1) * pairs]
        power = real_out + squared[(2 * part + 1) * pairs : (2 * part + 2) * pairs]
        mark = marks[part * (SIDE // 2) : part * (SIDE // 2) + 1].astype(jnp.int32)
        hot = (mark == spots).astype(jnp.float32).astype(jnp.bfloat16)
        high = power.astype(jnp.bfloat16)
        low = (power - high.astype(jnp.float32)).astype(jnp.bfloat16)
        hots += [hot, hot]
        pieces += [low, high]
    out[...] = jnp.dot(
        jnp.concatenate(hots, axis=1),
        jnp.concatenate(pieces, axis=0),
        preferred_element_type=jnp.float32,
    )


def swap(block, count):
    return lax.ppermute(block, "blk", [(i, i ^ 1) for i in range(count)])


def body(tables, phase_history, tile_curvature, interp_weights, strip_tiles, row_offsets, tile_owner):
    blk_count = lax.axis_size("blk")
    map_count = lax.axis_size("map")
    own_block = phase_history[0, 0]
    pulse_count = own_block.shape[0]
    freq_count = own_block.shape[1] // 2
    columns = interp_weights.shape[2]
    rows_here = strip_tiles.shape[2]

    near = [lax.ppermute(own_block, "blk", matching(blk_count, 2, p)) for p in (0, 1)]
    far = [lax.ppermute(own_block, "blk", matching(blk_count, 4, p)) for p in (0, 1)]
    twin = swap(own_block, blk_count)

    f32 = lambda *shape: jax.ShapeDtypeStruct(shape, jnp.float32)
    b16 = lambda *shape: jax.ShapeDtypeStruct(shape, jnp.bfloat16)
    deep = 2 * pulse_count
    image_shape = (map_count * rows_here, 2 * columns)
    half_shape = (rows_here, 2 * columns)
    right = lambda n: pltpu.VMEM((n * deep, 2 * columns), jnp.bfloat16)
    spread = lambda n: pltpu.VMEM((2, n * pulse_count, freq_count), jnp.bfloat16)
    cross = lambda n: (map_count * rows_here, n * deep)
    flops = lambda n: 2 * n * pulse_count * 4 * columns * (freq_count + map_count * rows_here)
    n = GROUPS[0]
    smem, vmem, hbm = (
        pl.BlockSpec(memory_space=kind) for kind in (pltpu.SMEM, pltpu.VMEM, pltpu.HBM)
    )
    outs = [
        f32(*image_shape),
        *(f32(size, pulse_count, freq_count) for size in GROUPS[1:] for _ in range(2)),
        b16(2 * freq_count, freq_count),
        b16(*cross(GROUPS[1])),
        b16(*cross(GROUPS[2])),
    ]
    total, *curves, ranges, second_cross, last_cross = pl.pallas_call(
        functools.partial(first_kernel, map_count, STOPS * map_count * pulse_count),
        out_shape=outs,
        in_specs=[smem, hbm, vmem, hbm],
        out_specs=[vmem] * len(outs),
        scratch_shapes=[pltpu.VMEM((n, pulse_count, freq_count), jnp.float32)] * 2
        + [
            spread(n),
            right(n),
            pltpu.VMEM(cross(n), jnp.bfloat16),
            pltpu.VMEM(own_block.shape, jnp.bfloat16),
            pltpu.SemaphoreType.DMA((7,)),
        ],
        compiler_params=pltpu.CompilerParams(vmem_limit_bytes=44 * 2**20),
        cost_estimate=pl.CostEstimate(flops=flops(n), bytes_accessed=0, transcendentals=2**18),
    )(tile_curvature, own_block, twin, tables)
    near[0], near[1], total = lax.optimization_barrier((near[0], near[1], total))
    twin_near = [swap(block, blk_count) for block in near]
    twin_far = [swap(block, blk_count) for block in far]
    n = GROUPS[1]
    [total] = call(
        second_kernel,
        [f32(*image_shape)],
        [*near, *far, *curves[:2], ranges, second_cross, total],
        [spread(n), right(n)],
        flops(n),
    )
    twin_near, twin_far, total = lax.optimization_barrier((twin_near, twin_far, total))
    n = GROUPS[2]
    sent, right_side = call(
        last_kernel,
        [b16(*half_shape), b16(n * deep, 2 * columns)],
        [*twin_near, *twin_far, *curves[2:], ranges, last_cross, total],
        [spread(n)],
        flops(n),
    )
    sent, right_side, strip_tiles, row_offsets, interp_weights = lax.optimization_barrier(
        (sent, right_side, strip_tiles, row_offsets, interp_weights)
    )
    arrived = lax.ppermute(sent, "map", [(0, 1), (1, 0)])
    pairs = max(2, 2 * rows_here // blk_count) * blk_count // 2
    slot_hot, marks, ordered = call(
        slot_kernel,
        [b16(2, pairs, rows_here), b16(pairs, SIDE), b16(columns, columns)],
        [
            strip_tiles.reshape(1, rows_here),
            row_offsets.reshape(1, rows_here),
            tile_owner.reshape(1, blk_count),
            interp_weights[0],
        ],
    )
    [kept] = call(kept_kernel, [f32(*half_shape)], [right_side, last_cross, total])

    wide = 4 * columns + SIDE
    [packed] = call(
        pack_kernel,
        [b16(blk_count, pairs // blk_count, wide)],
        [kept, arrived, slot_hot, marks],
        (),
        2 * pairs * rows_here * wide,
    )
    got = lax.all_to_all(packed, "blk", split_axis=0, concat_axis=0, tiled=True)
    [tile_map] = call(
        map_kernel,
        [f32(MAPH, columns)],
        [got, ordered],
        (),
        2 * pairs * 4 * columns * (columns + MAPH),
    )
    return tile_map.reshape(1, 1, MAPH, columns)


def solution(mesh):
    in_specs = (
        P("blk", "map", None, None),
        P("blk"),
        P("blk", None, None),
        P("blk", "map", None, None),
        P("blk", "map", None),
        P(),
    )
    out_specs = P("blk", "map", None, None)

    def run(*args):
        map_count, pulse_count, width = args[0].shape[1:]
        side = width // 2
        first, second, last = cross_tables(map_count, map_count * args[3].shape[2], pulse_count)
        rows = first.shape[1]
        tables = np.zeros((len(first), width + rows, width), first.dtype)
        tables[:, :width, :side] = range_tables(side)
        tables[:, width:, :side] = first
        tables[:, width:, side:] = second[:, :, :side]
        tables[:, :rows, side:] = last[:, :, :side]
        tables[:, rows : 2 * rows, side:] = np.concatenate(
            [second[:, :, side:], last[:, :, side:]], axis=2
        )
        tables = jnp.asarray(tables)
        held = lambda *here: body(tables, *here)
        return jax.shard_map(
            held, mesh=mesh, in_specs=in_specs, out_specs=out_specs, check_vma=False
        )(*args)

    return run
```

```python
import functools
import math

import jax
import jax.numpy as jnp
import ml_dtypes
import numpy as np
from jax import lax
from jax.experimental import pallas as pl
from jax.experimental.pallas import tpu as pltpu
from jax.sharding import PartitionSpec as P

STOPS = 8
MAPH = 256
SIDE = 128
GROUPS = (2, 3, 3)


def matching(count, distance, parity):
    seen, pairs = set(), []
    for start in range(count):
        cycle, at = [], start
        while at not in seen:
            seen.add(at)
            cycle.append(at)
            at = (at + distance) % count
        for place in range(parity, len(cycle) + parity, 2) if cycle else ():
            a, b = cycle[place % len(cycle)], cycle[(place + 1) % len(cycle)]
            pairs += [(a, b), (b, a)]
    return pairs


def range_tables(freq_count):
    index = np.arange(freq_count, dtype=np.int64)
    angle = (index[: freq_count // 2, None] * index[None, :] % freq_count).astype(
        np.float32
    ) * np.float32(2.0 * math.pi / freq_count)
    factor = np.float32(1.0 / math.sqrt(freq_count))
    real_part, imag_part = np.cos(angle) * factor, -np.sin(angle) * factor
    tables = [
        np.block([[real_part[:, p::2], imag_part[:, p::2]], [-imag_part[:, p::2], real_part[:, p::2]]])
        for p in (0, 1)
    ]
    return np.concatenate(tables).astype(ml_dtypes.bfloat16)


def stop_order(core):
    return [3, 4 - 2 * core, 1, 5, 7, 2 - 2 * core, 6 - 2 * core, 6 * core]


def cross_tables(map_count, row_count, pulse_count):
    span = STOPS * map_count * pulse_count
    rows = np.arange(row_count, dtype=np.int64)[:, None]
    factor = np.float32(1.0 / math.sqrt(span))
    tables, first = [], 0
    for size in GROUPS:
        table = []
        for m in range(map_count):
            for core in range(2):
                parts = []
                for k in stop_order(core)[first : first + size]:
                    along = (k * map_count + m) * pulse_count + np.arange(pulse_count)
                    angle = (rows * along[None, :] % span).astype(np.float32) * np.float32(
                        2.0 * math.pi / span
                    )
                    parts += [np.cos(angle) * factor, -np.sin(angle) * factor]
                table.append(np.concatenate(parts, axis=1))
        tables.append(np.stack(table).astype(ml_dtypes.bfloat16))
        first += size
    return tables


def call(kernel, outs, operands, scratch=(), flops=0, limit=24, far=()):
    specs = [
        pl.BlockSpec(memory_space=pltpu.HBM if n in far else pltpu.VMEM)
        for n in range(len(operands))
    ]
    size = sum(math.prod(a.shape) * a.dtype.itemsize for a in [*operands, *outs]) if flops else 0
    return pl.pallas_call(
        kernel,
        out_shape=outs,
        in_specs=specs,
        out_specs=[pl.BlockSpec(memory_space=pltpu.VMEM) for _ in outs],
        scratch_shapes=list(scratch),
        compiler_params=pltpu.CompilerParams(vmem_limit_bytes=limit * 2**20),
        cost_estimate=pl.CostEstimate(flops=flops, bytes_accessed=size, transcendentals=0),
    )(*operands)


def whereabouts():
    here, here_map = lax.axis_index("blk"), lax.axis_index("map")
    core = here % 2
    return core, here // 2 % 2, here // 4 % 2, here_map, here_map * 2 + core


def phase_factors(map_count, span, curvature, curves):
    _, pulses, freqs = curves[0].shape
    width = freqs // 4
    core, _, _, here_map, _ = whereabouts()
    outs = [
        (curves[2 * g], curves[2 * g + 1], p) for g, size in enumerate(GROUPS) for p in range(size)
    ]
    pulse = lax.broadcasted_iota(jnp.int32, (pulses, width), 0)
    fine = lax.broadcasted_iota(jnp.int32, (pulses, width), 1).astype(jnp.float32) / freqs
    pulse_on_lanes = lax.broadcasted_iota(jnp.int32, (STOPS, pulses), 1)
    stop_on_rows = lax.broadcasted_iota(jnp.int32, (STOPS, pulses), 0)

    def bend(stop, index):
        along = ((stop * map_count + here_map) * pulses + index).astype(jnp.float32) / span - 0.5
        return curvature[0] * (along * along)

    quarter = bend(stop_on_rows, pulse_on_lanes) * 0.25
    step = jnp.concatenate([jnp.cos(quarter), jnp.sin(quarter)] * (pulses // STOPS // 2), axis=0)
    turned = step.T
    stops = stop_order(core)
    for place in range(STOPS):
        cosines, sines, row = outs[place]
        options = sorted({stop_order(0)[place], stop_order(1)[place]})
        step_c, step_s = (
            turned[:, options[-1] + part : options[-1] + part + 1] for part in (0, STOPS)
        )
        if len(options) == 2:
            is_last = stops[place] == options[-1]
            step_c = jnp.where(is_last, step_c, turned[:, options[0] : options[0] + 1])
            step_s = jnp.where(
                is_last, step_s, turned[:, options[0] + STOPS : options[0] + STOPS + 1]
            )
        step_c = jnp.broadcast_to(step_c, (pulses, width))
        step_s = jnp.broadcast_to(step_s, (pulses, width))
        angle = bend(stops[place], pulse) * fine
        low_c, low_s = jnp.cos(angle), jnp.sin(angle)
        now_c = step_c * low_c - step_s * low_s
        now_s = step_s * low_c + step_c * low_s
        for h in range(4):
            now_c, now_s = step_c * now_c - step_s * now_s, step_s * now_c + step_c * now_s
            cosines[row, :, h * width : (h + 1) * width] = now_c
            sines[row, :, h * width : (h + 1) * width] = now_s


def transform(blocks, cosines, sines, ranges, phased, right_side):
    freqs = cosines.shape[2]
    pulses = cosines.shape[1]
    half = freqs // 2
    for place, block in enumerate(blocks):
        values = block().astype(jnp.float32)
        real_part, imag_part = values[:, :freqs], values[:, freqs:]
        cosine, sine = cosines[place], sines[place]
        rows = slice(place * pulses, (place + 1) * pulses)
        turned = (real_part * cosine - imag_part * sine, real_part * sine + imag_part * cosine)
        for n, part in enumerate(turned):
            columns = slice(n * half, (n + 1) * half)
            low, high = part[:, :half], part[:, half:]
            phased[0, rows, columns] = (low + high).astype(jnp.bfloat16)
            phased[1, rows, columns] = (low - high).astype(jnp.bfloat16)
    for parity in range(2):
        spectrum = jnp.dot(
            phased[parity],
            ranges[parity * freqs : (parity + 1) * freqs],
            preferred_element_type=jnp.float32,
        ).astype(jnp.bfloat16)
        first = slice(parity * half, (parity + 1) * half)
        second = slice(freqs + parity * half, freqs + (parity + 1) * half)
        for place in range(len(blocks)):
            piece = spectrum[place * pulses : (place + 1) * pulses]
            real_part, imag_part = piece[:, :half], piece[:, half:]
            top = slice(2 * place * pulses, (2 * place + 1) * pulses)
            below = slice((2 * place + 1) * pulses, (2 * place + 2) * pulses)
            right_side[top, first] = real_part
            right_side[top, second] = imag_part
            right_side[below, first] = -imag_part
            right_side[below, second] = real_part


def first_kernel(map_count, span, curvature, own_far, twin, tables, total, *rest):
    later = 2 * len(GROUPS) - 2
    ranges, second, last, cosines, sines, phased, right_side, cross, own, arrivals = rest[later:]
    index = whereabouts()[4]
    depth, side = ranges.shape
    rows = cross.shape[0]
    left, right = slice(0, side), slice(side, 2 * side)
    rest_side = side // 2
    moves = [
        (own_far, own),
        (tables.at[index, :depth, left], ranges),
        (tables.at[index, depth : depth + rows, left], cross),
        (tables.at[index, depth : depth + rows, right], second.at[:, left]),
        (tables.at[index, :rows, right], last.at[:, left]),
        (tables.at[index, rows : 2 * rows, side : side + rest_side], second.at[:, side:]),
        (tables.at[index, rows : 2 * rows, side + rest_side :], last.at[:, side:]),
    ]
    copies = [
        pltpu.make_async_copy(source, target, arrivals.at[n])
        for n, (source, target) in enumerate(moves)
    ]
    for copy in copies:
        copy.start()
    phase_factors(map_count, span, curvature, (cosines, sines, *rest[:later]))
    for copy in copies[:3]:
        copy.wait()
    transform([lambda: own[...], lambda: twin[...]], cosines, sines, ranges, phased, right_side)
    total[...] = jnp.dot(cross[...], right_side[...], preferred_element_type=jnp.float32)
    for copy in copies[3:]:
        copy.wait()


def second_kernel(
    near_a, near_b, far_a, far_b, cosines, sines, ranges, cross, before, total, phased, right_side
):
    _, chip, group, _, _ = whereabouts()
    chip_odd, group_odd = chip == 1, group == 1
    blocks = [
        lambda: jnp.where(chip_odd, near_a[...], near_b[...]),
        lambda: jnp.where(chip_odd, near_b[...], near_a[...]),
        lambda: jnp.where(group_odd, far_b[...], far_a[...]),
    ]
    transform(blocks, cosines, sines, ranges, phased, right_side)
    total[...] = before[...] + jnp.dot(
        cross[...], right_side[...], preferred_element_type=jnp.float32
    )


def part_rows(ref, part):
    rows = ref.shape[0] // 2
    return ref[pl.ds(pl.multiple_of(part * rows, rows), rows), :]


def last_kernel(
    twin_near_a, twin_near_b, twin_far_a, twin_far_b,
    cosines, sines, ranges, cross, before, sent, right_side, phased,
):
    core, chip, group, here_map, _ = whereabouts()
    chip_odd, from_a = chip == 1, core != group
    blocks = [
        lambda: jnp.where(chip_odd, twin_near_a[...], twin_near_b[...]),
        lambda: jnp.where(chip_odd, twin_near_b[...], twin_near_a[...]),
        lambda: jnp.where(from_a, twin_far_a[...], twin_far_b[...]),
    ]
    transform(blocks, cosines, sines, ranges, phased, right_side)
    other = 1 - here_map
    sent[...] = (
        part_rows(before, other)
        + jnp.dot(
            part_rows(cross, other), right_side[...], preferred_element_type=jnp.float32
        )
    ).astype(sent.dtype)


def kept_kernel(right_side, cross, before, kept):
    here_map = whereabouts()[3]
    kept[...] = part_rows(before, here_map) + jnp.dot(
        part_rows(cross, here_map), right_side[...], preferred_element_type=jnp.float32
    )


def slot_kernel(tiles, offsets, owner, weights, slot_hot, marks, ordered):
    columns = weights.shape[0]
    place = lax.broadcasted_iota(jnp.int32, weights.shape, 0)
    source = jnp.where(place < columns // 2, 2 * place, 2 * place - columns + 1)
    order = source == lax.broadcasted_iota(jnp.int32, weights.shape, 1)
    ordered[...] = jnp.dot(
        order.astype(jnp.float32).astype(jnp.bfloat16),
        weights[...],
        preferred_element_type=jnp.float32,
    ).astype(jnp.bfloat16)
    count, rows = owner.shape[1], tiles.shape[1]
    _, pairs, _ = slot_hot.shape
    capacity = 2 * pairs // count
    tile_hot = (lax.broadcasted_iota(jnp.int32, (count, rows), 0) == tiles[...]).astype(
        jnp.bfloat16
    )
    owners = jnp.broadcast_to(owner[...].astype(jnp.float32), (8, count)).astype(jnp.bfloat16)
    holder = jnp.dot(owners, tile_hot, preferred_element_type=jnp.float32)[0:1]
    same = lax.dot_general(
        tile_hot, tile_hot, (((0,), (0,)), ((), ())), preferred_element_type=jnp.float32
    )
    earlier = lax.broadcasted_iota(jnp.int32, (rows, rows), 0) < lax.broadcasted_iota(
        jnp.int32, (rows, rows), 1
    )
    rank = jnp.sum(jnp.where(earlier, same, 0.0), axis=0, keepdims=True)
    slot = (holder * capacity + rank).astype(jnp.int32)
    numbers = 2 * lax.broadcasted_iota(jnp.int32, (pairs, rows), 0)
    half = marks.shape[1] // 2
    for part in range(2):
        hot = numbers + part == slot
        slot_hot[part] = hot.astype(jnp.float32).astype(jnp.bfloat16)
        mark = jnp.sum(
            jnp.where(hot, offsets[...].astype(jnp.float32), 0.0), axis=1, keepdims=True
        )
        spread = jnp.broadcast_to(mark, (pairs, half))
        sides = [spread, jnp.zeros_like(spread)]
        both = jnp.concatenate(sides if part == 0 else sides[::-1], axis=1)
        total = both if part == 0 else total + both
    marks[...] = total.astype(jnp.bfloat16)


def pack_kernel(kept, arrived, slot_hot, marks, packed):
    width = kept.shape[1]
    count, group, _ = packed.shape
    image = (kept[...] + arrived[...].astype(jnp.float32)).astype(jnp.bfloat16)
    for part in range(2):
        packed[:, :, part * width : (part + 1) * width] = (
            jnp.dot(slot_hot[part], image, preferred_element_type=jnp.float32)
            .astype(packed.dtype)
            .reshape(count, group, width)
        )
    packed[:, :, 2 * width :] = marks[...].reshape(count, group, marks.shape[1])


def map_kernel(got, weights, out):
    columns = weights.shape[0]
    pairs = got.shape[0] * got.shape[1]
    flat = got[...].reshape(pairs, got.shape[2])
    parts = [flat[:, n * columns : (n + 1) * columns] for n in range(4)]
    mapped = jnp.dot(
        jnp.concatenate(parts, axis=0), weights[...], preferred_element_type=jnp.float32
    )
    squared = mapped * mapped
    marks = flat[:, 4 * columns :].astype(jnp.float32).T
    spots = lax.broadcasted_iota(jnp.int32, (MAPH, pairs), 0)
    hots, pieces = [], []
    for part in range(2):
        real_out = squared[2 * part * pairs : (2 * part + 1) * pairs]
        power = real_out + squared[(2 * part + 1) * pairs : (2 * part + 2) * pairs]
        mark = marks[part * (SIDE // 2) : part * (SIDE // 2) + 1].astype(jnp.int32)
        hot = (mark == spots).astype(jnp.float32).astype(jnp.bfloat16)
        high = power.astype(jnp.bfloat16)
        low = (power - high.astype(jnp.float32)).astype(jnp.bfloat16)
        hots += [hot, hot]
        pieces += [low, high]
    out[...] = jnp.dot(
        jnp.concatenate(hots, axis=1),
        jnp.concatenate(pieces, axis=0),
        preferred_element_type=jnp.float32,
    )


def swap(block, count):
    return lax.ppermute(block, "blk", [(i, i ^ 1) for i in range(count)])


def body(tables, phase_history, tile_curvature, interp_weights, strip_tiles, row_offsets, tile_owner):
    blk_count = lax.axis_size("blk")
    map_count = lax.axis_size("map")
    own_block = phase_history[0, 0]
    pulse_count = own_block.shape[0]
    freq_count = own_block.shape[1] // 2
    columns = interp_weights.shape[2]
    rows_here = strip_tiles.shape[2]

    near = [lax.ppermute(own_block, "blk", matching(blk_count, 2, p)) for p in (0, 1)]
    far = [lax.ppermute(own_block, "blk", matching(blk_count, 4, p)) for p in (0, 1)]
    twin = swap(own_block, blk_count)

    f32 = lambda *shape: jax.ShapeDtypeStruct(shape, jnp.float32)
    b16 = lambda *shape: jax.ShapeDtypeStruct(shape, jnp.bfloat16)
    deep = 2 * pulse_count
    image_shape = (map_count * rows_here, 2 * columns)
    half_shape = (rows_here, 2 * columns)
    right = lambda n: pltpu.VMEM((n * deep, 2 * columns), jnp.bfloat16)
    spread = lambda n: pltpu.VMEM((2, n * pulse_count, freq_count), jnp.bfloat16)
    cross = lambda n: (map_count * rows_here, n * deep)
    flops = lambda n: 2 * n * pulse_count * 4 * columns * (freq_count + map_count * rows_here)
    n = GROUPS[0]
    smem, vmem, hbm = (
        pl.BlockSpec(memory_space=kind) for kind in (pltpu.SMEM, pltpu.VMEM, pltpu.HBM)
    )
    outs = [
        f32(*image_shape),
        *(f32(size, pulse_count, freq_count) for size in GROUPS[1:] for _ in range(2)),
        b16(2 * freq_count, freq_count),
        b16(*cross(GROUPS[1])),
        b16(*cross(GROUPS[2])),
    ]
    total, *curves, ranges, second_cross, last_cross = pl.pallas_call(
        functools.partial(first_kernel, map_count, STOPS * map_count * pulse_count),
        out_shape=outs,
        in_specs=[smem, hbm, vmem, hbm],
        out_specs=[vmem] * len(outs),
        scratch_shapes=[pltpu.VMEM((n, pulse_count, freq_count), jnp.float32)] * 2
        + [
            spread(n),
            right(n),
            pltpu.VMEM(cross(n), jnp.bfloat16),
            pltpu.VMEM(own_block.shape, jnp.bfloat16),
            pltpu.SemaphoreType.DMA((7,)),
        ],
        compiler_params=pltpu.CompilerParams(vmem_limit_bytes=44 * 2**20),
        cost_estimate=pl.CostEstimate(flops=flops(n), bytes_accessed=0, transcendentals=2**18),
    )(tile_curvature, own_block, twin, tables)
    near[1], near[0], total = lax.optimization_barrier((near[1], near[0], total))
    twin_near = [swap(block, blk_count) for block in near]
    twin_far = [swap(block, blk_count) for block in far]
    n = GROUPS[1]
    [total] = call(
        second_kernel,
        [f32(*image_shape)],
        [*near, *far, *curves[:2], ranges, second_cross, total],
        [spread(n), right(n)],
        flops(n),
    )
    twin_near, twin_far, total = lax.optimization_barrier((twin_near, twin_far, total))
    n = GROUPS[2]
    sent, right_side = call(
        last_kernel,
        [b16(*half_shape), b16(n * deep, 2 * columns)],
        [*twin_near, *twin_far, *curves[2:], ranges, last_cross, total],
        [spread(n)],
        flops(n),
    )
    sent, right_side, strip_tiles, row_offsets, interp_weights = lax.optimization_barrier(
        (sent, right_side, strip_tiles, row_offsets, interp_weights)
    )
    arrived = lax.ppermute(sent, "map", [(0, 1), (1, 0)])
    pairs = max(2, 2 * rows_here // blk_count) * blk_count // 2
    slot_hot, marks, ordered = call(
        slot_kernel,
        [b16(2, pairs, rows_here), b16(pairs, SIDE), b16(columns, columns)],
        [
            strip_tiles.reshape(1, rows_here),
            row_offsets.reshape(1, rows_here),
            tile_owner.reshape(1, blk_count),
            interp_weights[0],
        ],
    )
    [kept] = call(kept_kernel, [f32(*half_shape)], [right_side, last_cross, total])

    wide = 4 * columns + SIDE
    [packed] = call(
        pack_kernel,
        [b16(blk_count, pairs // blk_count, wide)],
        [kept, arrived, slot_hot, marks],
        (),
        2 * pairs * rows_here * wide,
    )
    got = lax.all_to_all(packed, "blk", split_axis=0, concat_axis=0, tiled=True)
    [tile_map] = call(
        map_kernel,
        [f32(MAPH, columns)],
        [got, ordered],
        (),
        2 * pairs * 4 * columns * (columns + MAPH),
    )
    return tile_map.reshape(1, 1, MAPH, columns)


def solution(mesh):
    in_specs = (
        P("blk", "map", None, None),
        P("blk"),
        P("blk", None, None),
        P("blk", "map", None, None),
        P("blk", "map", None),
        P(),
    )
    out_specs = P("blk", "map", None, None)

    def run(*args):
        map_count, pulse_count, width = args[0].shape[1:]
        side = width // 2
        first, second, last = cross_tables(map_count, map_count * args[3].shape[2], pulse_count)
        rows = first.shape[1]
        tables = np.zeros((len(first), width + rows, width), first.dtype)
        tables[:, :width, :side] = range_tables(side)
        tables[:, width:, :side] = first
        tables[:, width:, side:] = second[:, :, :side]
        tables[:, :rows, side:] = last[:, :, :side]
        tables[:, rows : 2 * rows, side:] = np.concatenate(
            [second[:, :, side:], last[:, :, side:]], axis=2
        )
        tables = jnp.asarray(tables)
        held = lambda *here: body(tables, *here)
        return jax.shard_map(
            held, mesh=mesh, in_specs=in_specs, out_specs=out_specs, check_vma=False
        )(*args)

    return run
```
